32 devices in a mesh: seq: 4 (over y, core), shard: 8 (over z, x).
Axes of the slice: x: 2, y: 2, z: 4, core: 2. Of those that a mesh axis runs over, the one named last changes fastest.
Arguments:
- inputs: bfloat16 [160, 4, 7, 7, 512], P('shard', 'seq'), may hold values from -6 to 6
- cotangent: float32 [160, 4, 7, 7, 512], P('shard', 'seq'), may hold values from -6 to 6
- image_valid: int32 [160], P('shard'), may hold values from 0 to 1, as said below
- qkv_weight: float32 [2, 512, 1536], P(None, 'shard'), may hold values from -0.25 to 0.25
- proj_weight: float32 [2, 512, 512], P(None, 'shard'), may hold values from -1 to 1
- expand_weight: float32 [2, 512, 2048], P(None, 'shard'), may hold values from -0.25 to 0.25
- contract_weight: float32 [2, 2048, 512], P(None, 'shard'), may hold values from -0.125 to 0.125
- vectors: float32 [2, 12, 512], P(None, None, 'shard'), may hold values from -1.5 to 1.5
- bias_table: float32 [32, 169], P('shard'), may hold values from -4 to 4
- qkv_first: float32 [2, 512, 1536], P(None, 'shard'), may hold values from -96 to 96
- proj_first: float32 [2, 512, 512], P(None, 'shard'), may hold values from -24 to 24
- expand_first: float32 [2, 512, 2048], P(None, 'shard'), may hold values from -48 to 48
- contract_first: float32 [2, 2048, 512], P(None, 'shard'), may hold values from -48 to 48
- vectors_first: float32 [2, 12, 512], P(None, None, 'shard'), may hold values from -96 to 96
- table_first: float32 [32, 169], P('shard'), may hold values from -56 to 56
- qkv_second: float32 [2, 512, 1536], P(None, 'shard'), may hold values from 10.4 to 83.2
- proj_second: float32 [2, 512, 512], P(None, 'shard'), may hold values from 0.64 to 5.12
- expand_second: float32 [2, 512, 2048], P(None, 'shard'), may hold values from 2.56 to 20.8
- contract_second: float32 [2, 2048, 512], P(None, 'shard'), may hold values from 2.56 to 20.8
- vectors_second: float32 [2, 12, 512], P(None, None, 'shard'), may hold values from 10.4 to 83.2
- table_second: float32 [32, 169], P('shard'), may hold values from 3.68 to 30.4
Outputs:
- output: float32 [160, 4, 7, 7, 512], P('shard', 'seq')
- input_grad: float32 [160, 4, 7, 7, 512], P('shard', 'seq')
- new_qkv_first: float32 [2, 512, 1536], P(None, 'shard')
- new_qkv_second: float32 [2, 512, 1536], P(None, 'shard')
- new_qkv_weight: float32 [2, 512, 1536], P(None, 'shard')
- new_proj_first: float32 [2, 512, 512], P(None, 'shard')
- new_proj_second: float32 [2, 512, 512], P(None, 'shard')
- new_proj_weight: float32 [2, 512, 512], P(None, 'shard')
- new_expand_first: float32 [2, 512, 2048], P(None, 'shard')
- new_expand_second: float32 [2, 512, 2048], P(None, 'shard')
- new_expand_weight: float32 [2, 512, 2048], P(None, 'shard')
- new_contract_first: float32 [2, 2048, 512], P(None, 'shard')
- new_contract_second: float32 [2, 2048, 512], P(None, 'shard')
- new_contract_weight: float32 [2, 2048, 512], P(None, 'shard')
- new_vectors_first: float32 [2, 12, 512], P(None, None, 'shard')
- new_vectors_second: float32 [2, 12, 512], P(None, None, 'shard')
- new_vectors: float32 [2, 12, 512], P(None, None, 'shard')
- new_table_first: float32 [32, 169], P('shard')
- new_table_second: float32 [32, 169], P('shard')
- new_table: float32 [32, 169], P('shard')
- bias_gradient: float32 [2, 512], P(None, 'shard')
The draws below stay inside these ranges and needn't reach their ends.
Inputs may be any that keep to these rules, and one draw needn't show every extreme that they name: `image_valid`: within the 20 slots of each index of shard the real images come first, one or more of them; the last index of shard has all its slots real.
All inputs are finite; a program needn't handle non-finite values.
Results may differ from the reference program's by a relative error of at most 0.025.
Values may be sent and summed in bfloat16 or wider, within the bound.
No kernel may reach another device: no remote copies, remote signals or barrier semaphores. Data moves between devices by JAX's collectives and lax.ppermute only.
A program may use at most 256 MiB of HBM per device.

```python
import math
import jax
import jax.numpy as jnp
from jax import lax

HEADS = 16
D = 512
FF = 2048
WIN = 7
SHIFT = 3
ADAM_STEP = 10
IMG_DEV = 20
IMAGES = 160
VEC_ROWS = 12
REL_SPAN = 169


def draw_image_valid(key, part):
    key = jax.random.fold_in(key, 11)
    device_total = IMAGES // IMG_DEV
    device_ids = jnp.arange(device_total, dtype=jnp.int32)
    floor_count = max(1, IMG_DEV // 3)
    span_last = max(device_total - 1, 1)
    rising = floor_count + (device_ids * (IMG_DEV - floor_count) + span_last // 2) // span_last
    jitters = jax.random.randint(key, (device_total,), -1, 2, dtype=jnp.int32)
    counts = jnp.clip(rising + jitters, 1, IMG_DEV)
    counts = jnp.where(device_ids == device_total - 1, IMG_DEV, counts)
    positions = jnp.arange(IMG_DEV, dtype=jnp.int32)
    return (positions[None, :] < counts[:, None]).astype(jnp.int32).reshape(-1)


def draw_vectors(key, part):
    key = jax.random.fold_in(key, 13)
    key_gain, key_shift = jax.random.split(key)
    shape_all = (2, VEC_ROWS, D)
    gain_vals = jax.random.uniform(key_gain, shape_all, jnp.float32, 0.5, 1.5)
    shifts = 0.5 * jax.random.truncated_normal(key_shift, -3.0, 3.0, shape_all, jnp.float32)
    row_ids = jnp.arange(VEC_ROWS, dtype=jnp.int32)
    is_gain = (row_ids == 0) | (row_ids == 5)
    return jnp.where(is_gain[None, :, None], gain_vals, shifts)


def levels(stream_key, dims, cuts, smallest, top_value):
    def one(position, parts):
        draws = jax.random.uniform(jax.random.fold_in(jax.random.fold_in(stream_key, 6), position), (parts,), jnp.float32, smallest / len(cuts), top_value / len(cuts))
        return jnp.repeat(jnp.exp(draws), dims[position] // parts).reshape((-1,) + (1,) * (len(dims) - position - 1))

    gain = one(*cuts[0])
    for cut in cuts[1:]:
        gain = gain * one(*cut)
    return gain


def gaussian(stream_key, shape, scale, most, cuts=(), kind=jnp.bfloat16):
    gain = levels(stream_key, shape, cuts, -0.22, 0.18) if cuts else 1.0
    drawn = jax.random.normal(stream_key, shape, jnp.float32) * scale * gain
    return jnp.minimum(jnp.maximum(drawn, -most), most).astype(kind)


def setup_inputs(seed: int = 0) -> dict:
    splits = jax.random.split(jax.random.key(seed), 22)
    inputs = gaussian(splits[0], (IMAGES, 4, WIN, WIN, D), 1.0, 6.0, ((0, 8), (1, 4)))
    cotangent = gaussian(splits[1], (IMAGES, 4, WIN, WIN, D), 1.0, 6.0, ((0, 8), (1, 4)), jnp.float32)
    image_valid = draw_image_valid(jax.random.fold_in(splits[21], 71), 0)
    qkv_weight = gaussian(splits[3], (2, D, 3 * D), D ** -0.5, 0.25, ((1, 8),), jnp.float32)
    proj_weight = gaussian(splits[4], (2, D, D), (D // 16) ** -0.5, 1.0, ((1, 8),), jnp.float32)
    expand_weight = gaussian(splits[5], (2, D, FF), D ** -0.5, 0.25, ((1, 8),), jnp.float32)
    contract_weight = gaussian(splits[6], (2, FF, D), FF ** -0.5, 0.125, ((1, 8),), jnp.float32)
    vectors = draw_vectors(jax.random.fold_in(splits[21], 71), 0)
    bias_table = gaussian(splits[8], (2 * HEADS, REL_SPAN), 1.0, 4.0, ((0, 8),), jnp.float32)
    qkv_first = gaussian(splits[9], (2, D, 3 * D), (1.25 * IMAGES ** 0.5), 96.0, ((1, 8),), jnp.float32)
    proj_first = gaussian(splits[10], (2, D, D), (0.31 * IMAGES ** 0.5), 24.0, ((1, 8),), jnp.float32)
    expand_first = gaussian(splits[11], (2, D, FF), (0.63 * IMAGES ** 0.5), 48.0, ((1, 8),), jnp.float32)
    contract_first = gaussian(splits[12], (2, FF, D), (0.63 * IMAGES ** 0.5), 48.0, ((1, 8),), jnp.float32)
    vectors_first = gaussian(splits[13], (2, VEC_ROWS, D), (1.25 * IMAGES ** 0.5), 96.0, ((2, 8),), jnp.float32)
    table_first = gaussian(splits[14], (2 * HEADS, REL_SPAN), (0.75 * IMAGES ** 0.5), 56.0, ((0, 8),), jnp.float32)
    qkv_second = jnp.clip(jnp.exp(math.log(83.2) - 2.0794415 * jax.random.uniform(splits[15], (2, D, 3 * D), jnp.float32) ** levels(splits[15], (2, D, 3 * D), ((1, 8),), -0.2, 0.2)), 10.4, 83.2)
    proj_second = jnp.clip(jnp.exp(math.log(5.12) - 2.0794415 * jax.random.uniform(splits[16], (2, D, D), jnp.float32) ** levels(splits[16], (2, D, D), ((1, 8),), -0.2, 0.2)), 0.64, 5.12)
    expand_second = jnp.clip(jnp.exp(math.log(20.8) - 2.0949457 * jax.random.uniform(splits[17], (2, D, FF), jnp.float32) ** levels(splits[17], (2, D, FF), ((1, 8),), -0.2, 0.2)), 2.56, 20.8)
    contract_second = jnp.clip(jnp.exp(math.log(20.8) - 2.0949457 * jax.random.uniform(splits[18], (2, FF, D), jnp.float32) ** levels(splits[18], (2, FF, D), ((1, 8),), -0.2, 0.2)), 2.56, 20.8)
    vectors_second = jnp.clip(jnp.exp(math.log(83.2) - 2.0794415 * jax.random.uniform(splits[19], (2, VEC_ROWS, D), jnp.float32) ** levels(splits[19], (2, VEC_ROWS, D), ((2, 8),), -0.2, 0.2)), 10.4, 83.2)
    table_second = jnp.clip(jnp.exp(math.log(30.4) - 2.1115298 * jax.random.uniform(splits[20], (2 * HEADS, REL_SPAN), jnp.float32) ** levels(splits[20], (2 * HEADS, REL_SPAN), ((0, 8),), -0.2, 0.2)), 3.68, 30.4)
    return {"inputs": inputs, "cotangent": cotangent, "image_valid": image_valid, "qkv_weight": qkv_weight, "proj_weight": proj_weight, "expand_weight": expand_weight, "contract_weight": contract_weight, "vectors": vectors, "bias_table": bias_table, "qkv_first": qkv_first, "proj_first": proj_first, "expand_first": expand_first, "contract_first": contract_first, "vectors_first": vectors_first, "table_first": table_first, "qkv_second": qkv_second, "proj_second": proj_second, "expand_second": expand_second, "contract_second": contract_second, "vectors_second": vectors_second, "table_second": table_second}


@jax.custom_vjp
def low(v):
    return lax.optimization_barrier(v.astype(jnp.bfloat16)).astype(jnp.float32)

@jax.custom_vjp
def low_back(v):
    return v

def low_keep(v):
    return (low(v), None)

def low_pass(kept, grad):
    return (grad,)

def back_keep(v):
    return (v, None)

def back_low(kept, grad):
    return (low(grad),)
low.defvjp(low_keep, low_pass)
low_back.defvjp(back_keep, back_low)
highest = lax.Precision.HIGHEST
norm_eps = 1e-05
mask_fill = -100.0
beta_one = 0.9
beta_two = 0.999
adam_eps = 1e-08
step_rates = (0.09, 0.35, 0.09, 0.045, 0.5, 2.0)
decay_rates = (0.05, 0.05, 0.05, 0.05, 0.0, 0.0)

def norm_rows(values, scale_vec, offset):
    center = values - lax.optimization_barrier(jnp.mean(values, axis=-1, keepdims=True))
    spread = lax.optimization_barrier(jnp.mean(center * center, axis=-1, keepdims=True))
    return center * lax.rsqrt(spread + norm_eps) * scale_vec + offset

def relative_index():
    places = jnp.arange(WIN * WIN, dtype=jnp.int32)
    row_of = places // WIN
    col_of = places % WIN
    return (row_of[:, None] - row_of[None, :] + WIN - 1) * (2 * WIN - 1) + col_of[:, None] - col_of[None, :] + WIN - 1

def partition_image(image):
    batch_size = image.shape[0]
    channels = image.shape[-1]
    return image.reshape(batch_size, 2, WIN, 2, WIN, channels).transpose(0, 1, 3, 2, 4, 5).reshape(batch_size, 4, WIN, WIN, channels)

def join_windows(tile_rows):
    batch_size = tile_rows.shape[0]
    channels = tile_rows.shape[-1]
    return tile_rows.reshape(batch_size, 2, 2, WIN, WIN, channels).transpose(0, 1, 3, 2, 4, 5).reshape(batch_size, 2 * WIN, 2 * WIN, channels)

def region_mask():
    image_side = 2 * WIN
    places = jnp.arange(image_side, dtype=jnp.int32)
    region = (places >= image_side - WIN).astype(jnp.int32) + (places >= image_side - SHIFT).astype(jnp.int32)
    labels = region[:, None] * 3 + region[None, :]
    tile_labels = partition_image(labels[None, :, :, None]).reshape(4, WIN * WIN)
    return jnp.where(tile_labels[:, :, None] != tile_labels[:, None, :], mask_fill, 0.0).astype(jnp.float32)

def attend(tokens, w_qkv, vector_vals, table_rows, shift_mask):
    model_width = tokens.shape[-1]
    head_dim = model_width // HEADS
    projected = jnp.einsum('bwtc,cf->bwtf', tokens, w_qkv, precision=highest)
    queries = low_back(low(projected[..., :model_width] + vector_vals[2]))
    key_rows = low_back(low(projected[..., model_width:2 * model_width]))
    value_rows = low_back(low(projected[..., 2 * model_width:] + vector_vals[3]))
    head_shape = tokens.shape[:3] + (HEADS, head_dim)
    queries = queries.reshape(head_shape)
    key_rows = key_rows.reshape(head_shape)
    value_rows = value_rows.reshape(head_shape)
    rel_bias = table_rows[:, relative_index()]
    scores = head_dim ** (-0.5) * jnp.einsum('bwqhd,bwkhd->bwhqk', queries, key_rows, precision=highest) + rel_bias[None, None] + shift_mask[None, :, None]
    scores = low_back(scores)
    attn_probs = low(jax.nn.softmax(scores, axis=-1))
    context = jnp.einsum('bwhqk,bwkhd->bwqhd', attn_probs, value_rows, precision=highest).reshape(tokens.shape)
    return low_back(low(context))

def forward(params, windows):
    tensors = tuple((low(member) for member in params))
    w_qkv, w_proj, w_expand, w_contract, vectors, bias_table = tensors
    stream = windows
    batch_size = windows.shape[0]
    model_width = windows.shape[-1]
    cell_count = WIN * WIN
    for layer_id in range(2):
        vector_vals = vectors[layer_id]
        normed = low(norm_rows(stream, vector_vals[0], vector_vals[1]))
        table_rows = bias_table[layer_id * HEADS:(layer_id + 1) * HEADS]
        if layer_id == 1:
            normed = low_back(normed)
            tile_rows = partition_image(jnp.roll(join_windows(normed), (-SHIFT, -SHIFT), axis=(1, 2)))
            shift_mask = region_mask()
        else:
            tile_rows = normed
            shift_mask = jnp.zeros((4, cell_count, cell_count), jnp.float32)
        context = attend(tile_rows.reshape(batch_size, 4, cell_count, model_width), w_qkv[layer_id], vector_vals, table_rows, shift_mask)
        context = context.reshape(tile_rows.shape)
        if layer_id == 1:
            context = partition_image(jnp.roll(join_windows(context), (SHIFT, SHIFT), axis=(1, 2)))
        branch = low_back(jnp.einsum('bwijc,cf->bwijf', context, w_proj[layer_id], precision=highest) + vector_vals[4])
        middle = stream + branch
        normed_two = low(norm_rows(middle, vector_vals[5], vector_vals[6]))
        pre_act = low_back(jnp.einsum('bwijc,cf->bwijf', normed_two, w_expand[layer_id], precision=highest) + vector_vals[8:].reshape(-1))
        hidden = low(jax.nn.gelu(pre_act, approximate=False))
        branch_two = low_back(jnp.einsum('bwijf,fc->bwijc', hidden, w_contract[layer_id], precision=highest) + vector_vals[7])
        stream = middle + branch_two
    return stream

def adam_update(weight, moment_one, moment_two, gradient, step_rate, decay_rate):
    first_new = beta_one * moment_one + (1.0 - beta_one) * gradient
    second_new = beta_two * moment_two + (1.0 - beta_two) * gradient * gradient
    correct_one = 1.0 - beta_one ** ADAM_STEP
    correct_two = 1.0 - beta_two ** ADAM_STEP
    update = first_new / correct_one / (jnp.sqrt(second_new / correct_two) + adam_eps)
    weight_new = weight * (1.0 - step_rate * decay_rate) - step_rate * update
    return (first_new, second_new, weight_new)

def reference(inputs, cotangent, image_valid, qkv_weight, proj_weight, expand_weight, contract_weight, vectors, bias_table, qkv_first, proj_first, expand_first, contract_first, vectors_first, table_first, qkv_second, proj_second, expand_second, contract_second, vectors_second, table_second):
    params = (qkv_weight, proj_weight, expand_weight, contract_weight, vectors, bias_table)
    firsts = (qkv_first, proj_first, expand_first, contract_first, vectors_first, table_first)
    seconds = (qkv_second, proj_second, expand_second, contract_second, vectors_second, table_second)
    model_width = inputs.shape[-1]
    blocks = IMAGES // 8
    windows = inputs.astype(jnp.float32).reshape(blocks, 8, 4, WIN, WIN, model_width)
    valid_rows = image_valid.astype(jnp.float32).reshape(IMAGES, 1, 1, 1, 1)
    cotangents = (cotangent * valid_rows).reshape(blocks, 8, 4, WIN, WIN, model_width)

    def block_step(totals, member):
        block_in, block_cot = member
        result, pullback = jax.vjp(forward, params, block_in)
        grad_params, grad_in = pullback(block_cot)
        return (tuple((left + right for left, right in zip(totals, grad_params))), (result, grad_in))
    zero_sums = tuple((jnp.zeros_like(member) for member in params))
    totals, (results, grads_in) = lax.scan(block_step, zero_sums, (windows, cotangents))
    full_shape = (IMAGES, 4, WIN, WIN, model_width)
    updated = [adam_update(params[pos], firsts[pos], seconds[pos], totals[pos], step_rates[pos], decay_rates[pos]) for pos in range(6)]
    bias_gradient = totals[4][:, 7]
    return (results.reshape(full_shape), grads_in.reshape(full_shape), updated[0][0], updated[0][1], updated[0][2], updated[1][0], updated[1][1], updated[1][2], updated[2][0], updated[2][1], updated[2][2], updated[3][0], updated[3][1], updated[3][2], updated[4][0], updated[4][1], updated[4][2], updated[5][0], updated[5][1], updated[5][2], bias_gradient)
```

```python
import functools
import math

import jax
import jax.numpy as jnp
from jax import lax
from jax.experimental import pallas as pl
from jax.experimental.pallas import tpu as pltpu
from jax.sharding import Mesh
from jax.sharding import PartitionSpec as P

HEADS = 16
WIN = 7
SHIFT = 3
ADAM_STEP = 10
WIDE = 512
HIDE = 2048
HEAD_DIM = 32
SPAN = 169
CELLS = 56
SEQ = 4
NWIN = 20
ROWS = NWIN * CELLS
TOK = 1152
GROUP = NWIN // SEQ
BLOCK = 288
PAIR = 2 * CELLS
NPAIR = NWIN // 2
STRIP = 384
NCH = TOK // STRIP
QUADS = 4 * WIN
FOUR = 4 * CELLS
QT = 4 * CELLS
SMALL = 32
HALF = 256
QUAD = 128

bf16 = jnp.bfloat16
f32 = jnp.float32
norm_eps = 1e-05
mask_fill = -100.0
pad_fill = -1e30
beta_one = 0.9
beta_two = 0.999
adam_eps = 1e-08
step_rates = (0.09, 0.35, 0.09, 0.045, 0.5, 2.0)
decay_rates = (0.05, 0.05, 0.05, 0.05, 0.0, 0.0)
scale = HEAD_DIM ** (-0.5)

VM = pl.BlockSpec(memory_space=pltpu.VMEM)
SM = pl.BlockSpec(memory_space=pltpu.SMEM)
HB = pl.BlockSpec(memory_space=pl.ANY)
MIB = 1024 * 1024


def call(kernel, outs, in_specs, scratch, flops, moved, out_specs=None, limit=58):
    return pl.pallas_call(
        kernel,
        out_shape=outs,
        in_specs=in_specs,
        out_specs=out_specs or tuple(VM for _ in outs),
        scratch_shapes=scratch,
        compiler_params=pltpu.CompilerParams(vmem_limit_bytes=limit * MIB),
        cost_estimate=pl.CostEstimate(flops=flops, bytes_accessed=moved, transcendentals=0),
    )


def sds(shape, dtype):
    return jax.ShapeDtypeStruct(shape, dtype)


def dot(a, b):
    return lax.dot_general(a, b, (((1,), (0,)), ((), ())), preferred_element_type=f32)


def dot_nt(a, b):
    return lax.dot_general(a, b, (((1,), (1,)), ((), ())), preferred_element_type=f32)


def dot_tn(a, b):
    return lax.dot_general(a, b, (((0,), (0,)), ((), ())), preferred_element_type=f32)


def loop(count, body):
    lax.fori_loop(0, count, lambda i, c: (body(i), c)[1], 0)


def centred(x):
    mean = jnp.mean(x, axis=-1, keepdims=True)
    cen = x - mean
    var = jnp.mean(cen * cen, axis=-1, keepdims=True)
    return cen, lax.rsqrt(var + norm_eps)


def gelu_pair(u):
    phi = 0.5 + 0.5 * lax.erf(u * math.sqrt(0.5))
    e = jnp.exp2((u * u) * (-0.5 / math.log(2.0)))
    return u * phi, phi + (u * (1.0 / math.sqrt(2.0 * math.pi))) * e


def head_masks():
    lane = lax.broadcasted_iota(jnp.int32, (1, 128), 1)
    return [(lane >> 5) == h for h in range(4)]


def stacked(t0, t1, masks):
    left = jnp.concatenate([jnp.where(m, t0, 0.0) for m in masks], axis=0)
    right = jnp.concatenate([jnp.where(m, t1, 0.0) for m in masks], axis=0)
    return jnp.concatenate([left, right], axis=1).astype(bf16)


def diagonal(t0, t1):
    z8 = jnp.zeros((64 - CELLS, 128), f32)
    z64 = jnp.zeros((64, 128), f32)
    left = jnp.concatenate([t0, z8, z64], axis=0)
    right = jnp.concatenate([z64, t1, z8], axis=0)
    return jnp.concatenate([left, right], axis=1).astype(bf16)


def from_diagonal(o):
    return jnp.concatenate([o[:CELLS, :128], o[64 : 64 + CELLS, 128:]], axis=0)


def from_stacked(o, masks):
    total = None
    for h, m in enumerate(masks):
        part = o[h * CELLS : (h + 1) * CELLS]
        part = jnp.concatenate(
            [jnp.where(m, part[:, :128], 0.0), jnp.where(m, part[:, 128:], 0.0)], axis=1
        )
        total = part if total is None else total + part
    return jnp.concatenate([total[:, :128], total[:, 128:]], axis=0)


def swap_windows(src, emit):
    col = lax.broadcasted_iota(jnp.int32, (1, 8, 1), 1)
    first = col < SHIFT

    def image(i):
        tiles = [src[pl.ds((i * 4 + w) * WIN, WIN)] for w in range(4)]
        for r in range(2):
            rows = [
                jnp.concatenate([tiles[(1 - r) * 2 + c][:SHIFT], tiles[r * 2 + c][SHIFT:]], axis=0)
                for c in range(2)
            ]
            for c in range(2):
                emit(i * 4 + r * 2 + c, jnp.where(first, rows[1 - c], rows[c]))

    loop(GROUP, image)


def swap_into(src, dst, keep):
    def emit(w, tile):
        keep[pl.ds(w * WIN, WIN)] = tile

    swap_windows(src, emit)

    def copy(p):
        v = keep[pl.ds(p * 2 * WIN, 2 * WIN)].reshape(PAIR, WIDE)
        dst[pl.ds(pl.multiple_of(p * PAIR, 16), PAIR), :] = v.astype(bf16)

    loop(NPAIR, copy)


def gather_rows(ref, off, per, first, count, c0, width):
    n = count // per
    v = ref[pl.ds(first * n, n), off : off + per, pl.ds(c0, width)]
    return v.reshape(count, width)


class Plan:
    def __init__(self, kind, shards, rows, row0=0):
        self.kind = kind
        self.shards = shards
        self.rows = rows
        self.row0 = row0

    @property
    def count(self):
        return {"near": 8, "wide": 4, "part": 8, "half": 2}[self.kind]

    def scratch(self):
        return [pltpu.VMEM((self.shards, self.rows, WIDE), bf16), pltpu.SemaphoreType.DMA]


def place(ids):
    s, m = ids[0], ids[1]
    return s & 1, s >> 1, m & 1, m >> 1


def start_load(plan, refs, dst, sem, ids, spans=None):
    c, y, x, z = place(ids)
    for lo, hi in spans or ((0, plan.rows),):
        for kc in range(2):
            if plan.kind == "half":
                lane = pl.multiple_of((c ^ kc) * HALF, HALF)
                pltpu.make_async_copy(
                    refs[kc].at[:, plan.row0 + lo : plan.row0 + hi, :],
                    dst.at[:, lo:hi, pl.ds(lane, HALF)],
                    sem,
                ).start()
                continue
            if plan.kind in ("wide", "part"):
                lane = pl.multiple_of((c ^ kc) * HALF, HALF)
                for k in range(8):
                    owner = (z ^ (k & 3)) * 2 + (x ^ (k >> 2))
                    row = 0
                    if plan.kind == "wide":
                        src = refs[kc * 2 + (k >> 2)].at[k & 3]
                    elif k & 3 == 3:
                        src = refs[kc * 4 + (k >> 2) * 2 + 1]
                        row = plan.row0
                    else:
                        src = refs[kc * 4 + (k >> 2) * 2].at[k & 3]
                    pltpu.make_async_copy(
                        src.at[row + lo : row + hi],
                        dst.at[owner, lo:hi, pl.ds(lane, HALF)],
                        sem,
                    ).start()
                continue
            for k in range(16):
                kxy, kz = k >> 2, k & 3
                owner = (z ^ kz) * 2 + (x ^ (kxy & 1))
                lane = pl.multiple_of((c ^ kc) * HALF + (y ^ (kxy >> 1)) * QUAD, QUAD)
                src = refs[kc * 4 + kxy].at[kz, lo:hi]
                pltpu.make_async_copy(src, dst.at[owner, lo:hi, pl.ds(lane, QUAD)], sem).start()


def wait_all(ref, sem):
    pltpu.make_async_copy(ref, ref, sem).wait()


def grad_shapes(plan):
    if plan.kind == "wide":
        shape = (2, 2, 2, plan.rows, HALF)
    else:
        shape = (2, plan.shards, plan.rows, QUAD)
    return (sds(shape, bf16), sds(shape, bf16))


def start_grads(plan, src, outs, sem, ids):
    c, y, x, z = place(ids)
    for kc in range(2):
        if plan.kind == "wide":
            lane = pl.multiple_of((c ^ kc) * HALF, HALF)
            for k in range(8):
                owner = (z ^ (k & 3)) * 2 + (x ^ (k >> 2))
                pltpu.make_async_copy(
                    src.at[owner, :, pl.ds(lane, HALF)],
                    outs[kc].at[k >> 2, k & 1, (k >> 1) & 1],
                    sem,
                ).start()
        else:
            for part in range(2):
                lane = pl.multiple_of((c ^ kc) * HALF + part * QUAD, QUAD)
                pltpu.make_async_copy(
                    src.at[:, :, pl.ds(lane, QUAD)], outs[kc].at[part], sem
                ).start()


def put_dense(dst, pad):
    def group(i):
        for q in range(4):
            tile = pad[i, :WIN, q * QUAD : (q + 1) * QUAD]
            dst[pl.ds(4 * WIN * i + q, WIN, stride=4), :] = tile

    loop(NWIN * WIN, group)


def prep_kernel(ids, valid_ref, x_ref, cot_ref, x_out, c0, c1, c2, c3, pad):
    s = ids[0]
    pad[...] = jnp.zeros_like(pad)
    x_out[ROWS:, :] = jnp.zeros((TOK - ROWS, WIDE), bf16)

    def xrow(i):
        pad[pl.ds(i * WIN, WIN), :WIN, :] = x_ref[pl.ds(i * WIN, WIN)].astype(f32)

    loop(NWIN, xrow)

    def xpair(i):
        v = pad[pl.ds(i * 2 * WIN, 2 * WIN)].reshape(PAIR, WIDE)
        x_out[pl.ds(pl.multiple_of(i * PAIR, 16), PAIR), :] = v.astype(bf16)

    loop(NPAIR, xpair)

    def image(i):
        v = valid_ref[i].astype(f32)

        def row(r):
            g = i * WIN + r
            for q in range(4):
                tile = cot_ref[pl.ds(4 * WIN * g + q, WIN, stride=4), :]
                pad[g, :WIN, q * QUAD : (q + 1) * QUAD] = tile * v

        loop(WIN, row)

    loop(NWIN, image)
    for k, out in enumerate((c0, c1, c2, c3)):
        d = s ^ k
        v = pad[pl.ds(d * GROUP * WIN, GROUP * WIN)].reshape(GROUP * CELLS, WIDE)
        out[: GROUP * CELLS, :] = v.astype(bf16)
        out[GROUP * CELLS :, :] = jnp.zeros((BLOCK - GROUP * CELLS, WIDE), bf16)


def prep(ids, valid, x, cot):
    block = sds((BLOCK, WIDE), bf16)
    return call(
        prep_kernel,
        (sds((TOK, WIDE), bf16), block, block, block, block),
        [SM, SM, VM, VM],
        [pltpu.VMEM((NWIN * WIN, 8, WIDE), f32)],
        10**6,
        10**7,
        limit=16,
    )(ids, valid, x, cot)


def pack_rows(per, pc, q, p, e, k):
    parts = [(q, 0, per, j * WIDE) for j in range(3)]
    parts += [(p, 0, per, 0), (k, 0, pc, 0)]
    parts += [(e, 0, per, j * WIDE) for j in range(4)]
    return parts


def pack_kernel(per, pc, widths, count, ids, q, p, e, k, vec, tab, *refs):
    outs, tmp = refs[:count], refs[count:]
    c = ids[0] & 1
    y = ids[0] >> 1
    row = 0
    for ref, r0, n, col in pack_rows(per, pc, q, p, e, k):
        at = row
        for out, (lo, hi, wide) in zip(outs, widths):
            if lo <= row < hi:
                off = c * HALF + (y * QUAD if wide == QUAD else 0)
                lane = pl.multiple_of(col + off, QUAD)
                at = row - lo
                out[at : at + n, :] = ref[0, r0 : r0 + n, pl.ds(lane, wide)].astype(bf16)
        row += n
    if tmp:
        small = tmp[0]
        small[...] = jnp.zeros_like(small)
        small[0:12, :per] = vec[0]
        small[12:24, :per] = vec[1]
        small[24 : 24 + tab.shape[0], :SPAN] = tab[...]
        n = outs[-1].shape[0]
        outs[-1][n - SMALL :, :] = small[...].astype(bf16)


def pack(layer, per, pc, pieces, small, ids, masters):
    q, p, e, k, vec, tab = masters
    outs = tuple(sds((hi - lo, wide), bf16) for lo, hi, wide in pieces)
    if small == "row":
        outs = outs[:-1] + (sds((outs[-1].shape[0] + SMALL, HALF), bf16),)
    if small == "own":
        outs = outs + (sds((SMALL, HALF), bf16),)

    def spec(a):
        return pl.BlockSpec((1,) + a.shape[1:], lambda i: (layer, 0, 0))

    def whole(shape):
        return pl.BlockSpec(shape, lambda i: (0,) * len(shape))

    return pl.pallas_call(
        functools.partial(pack_kernel, per, pc, pieces, len(outs)),
        grid=(1,),
        scratch_shapes=[pltpu.VMEM((SMALL, HALF), f32)] if small else [],
        out_shape=outs,
        in_specs=[SM, spec(q), spec(p), spec(e), spec(k), whole(vec.shape), whole(tab.shape)],
        out_specs=tuple(whole(o.shape) for o in outs),
        compiler_params=pltpu.CompilerParams(vmem_limit_bytes=24 * MIB),
        cost_estimate=pl.CostEstimate(flops=10**5, bytes_accessed=3 * 10**6, transcendentals=0),
    )(ids, q, p, e, k, vec, tab)


def onehot(rb, shifted):
    lane = lax.broadcasted_iota(jnp.int32, (1, 1024), 1)
    cb = lane >> 7
    a = lane & 63
    ra = a >> 3
    ca = a & 7

    def moved(v):
        return jnp.where(v >= SHIFT, v - SHIFT, v + WIN - SHIFT) if shifted else v

    rbm = (rb - SHIFT if rb >= SHIFT else rb + WIN - SHIFT) if shifted else rb
    idx = (moved(ra) - rbm + WIN - 1) * (2 * WIN - 1) + moved(ca) - moved(cb) + WIN - 1
    good = (ra < WIN) & (ca < WIN) & (cb < WIN)
    idx = jnp.where(good, idx, -1)
    entry = lax.broadcasted_iota(jnp.int32, (256, 1024), 0)
    return jnp.where(entry == idx, 1.0, 0.0).astype(bf16)


def smalls_kernel(per, own, natural, ids, *refs):
    vec_ref, hide_ref, b0_ref, b1_ref, nat, tmp = refs[-6:]
    shards = WIDE // per
    for k in range(shards):
        if natural:
            nat[k] = refs[0][k].astype(f32)
        else:
            i = ids[1] ^ ((k & 3) * 2 + (k >> 2))
            nat[i] = refs[k >> 2][k & 3, 3 * per :, :].astype(f32)
    for l in range(2):
        rows = jnp.concatenate(
            [nat[i, 12 * l : 12 * l + 12, :per] for i in range(shards)], axis=1
        )
        vec_ref[l] = rows[:8]
        for r in range(4):
            for half in range(2):
                hide_ref[l, 2 * r + half] = rows[8 + r : 9 + r, half * HALF : (half + 1) * HALF]
    for layer in range(2):
        first = layer * (HEADS // own)
        table = jnp.concatenate(
            [nat[first + i, 24 : 24 + own, :] for i in range(HEADS // own)], axis=0
        ).astype(bf16)
        for rb in range(WIN):
            r = dot(table, onehot(rb, layer == 1))
            for cb in range(8):
                tmp[:, rb * 8 + cb, :] = r[:, cb * 128 : (cb + 1) * 128]
        b = lax.broadcasted_iota(jnp.int32, (CELLS, 128), 0)
        lane = lax.broadcasted_iota(jnp.int32, (CELLS, 128), 1)
        a = lane & 63
        gone = (b & 7) == 7
        if layer == 0:
            add = jnp.where(gone, pad_fill, 0.0)
            for h in range(HEADS):
                b0_ref[0, h * CELLS : (h + 1) * CELLS, :] = tmp[h] + add
        else:
            rows = ((b >> 3) < SHIFT) != ((a >> 3) < SHIFT)
            cols = (((b & 7) < SHIFT) != ((a & 7) < SHIFT)) & (lane >= 64)
            for r in range(2):
                cut = cols | rows if r else cols
                add = jnp.where(gone, pad_fill, jnp.where(cut, mask_fill, 0.0))
                for h in range(HEADS):
                    b1_ref[r, h * CELLS : (h + 1) * CELLS, :] = tmp[h] + add


def expand_smalls(per, own, natural, ids, small):
    shards = WIDE // per
    return call(
        functools.partial(smalls_kernel, per, own, natural),
        (
            sds((2, 8, WIDE), f32),
            sds((2, 8, 1, HALF), f32),
            sds((1, HEADS * CELLS, 128), f32),
            sds((2, HEADS * CELLS, 128), f32),
        ),
        [SM] + [VM] * len(small),
        [pltpu.VMEM((shards, SMALL, HALF), f32), pltpu.VMEM((HEADS, CELLS, 128), f32)],
        10**8,
        2 * 10**6,
        limit=16,
    )(ids, *small)


def attn_fwd_kernel(layer, per, plan, *refs):
    ids, nw = refs[0], plan.count
    xs, refs = (refs[1:2], refs[2:]) if layer == 0 else (refs[1:5], refs[5:])
    w_in, vec_ref, bias_ref, refs = refs[:nw], refs[nw], refs[nw + 1], refs[nw + 2 :]
    if layer == 0:
        x_out = xs[0]
        n1_ref, qkv_ref, p_ref, o_ref, w_ref, sem = refs
    else:
        x_out, n1_ref, qkv_ref, p_ref, o_ref, w_ref, sem, one, two = refs
    start_load(plan, w_in, w_ref, sem, ids)
    if layer == 1:
        for k, ref in enumerate(xs):
            w = ids[0] ^ k
            v = ref[: GROUP * CELLS, :].astype(f32).reshape(GROUP, CELLS, WIDE)
            for i in range(GROUP):
                one[pl.ds((i * 4 + w) * WIN, WIN)] = v[i].reshape(WIN, 8, WIDE)

        def put(p):
            v = one[pl.ds(p * 2 * WIN, 2 * WIN)].reshape(PAIR, WIDE)
            x_out[pl.ds(pl.multiple_of(p * PAIR, 16), PAIR), :] = v.astype(bf16)

        loop(NPAIR, put)
        x_out[ROWS:, :] = jnp.zeros((TOK - ROWS, WIDE), bf16)

    gain = vec_ref[layer, 0:1, :]
    shift = vec_ref[layer, 1:2, :]
    if layer == 0:

        def norm(c):
            rows = pl.ds(pl.multiple_of(c * STRIP, STRIP), STRIP)
            cen, rstd = centred(x_out[rows, :].astype(f32))
            n1_ref[rows, :] = (cen * rstd * gain + shift).astype(bf16)

        loop(NCH, norm)
    else:

        def norm(p):
            rows = pl.ds(p * QUADS, QUADS)
            cen, rstd = centred(one[rows].reshape(FOUR, WIDE))
            one[rows] = (cen * rstd * gain + shift).reshape(QUADS, 8, WIDE)

        loop(GROUP, norm)
        swap_into(one, n1_ref, two)
        n1_ref[ROWS:, :] = jnp.zeros((TOK - ROWS, WIDE), bf16)

    wait_all(w_ref, sem)
    for j in range(3):
        for half in range(2):
            c0 = half * 256
            r = dot(n1_ref[...], gather_rows(w_ref, j * per, per, 0, WIDE, c0, 256))
            if j != 1:
                row = 2 if j == 0 else 3
                r = r + vec_ref[layer, row : row + 1, c0 : c0 + 256]
            qkv_ref[:, j * WIDE + c0 : j * WIDE + c0 + 256] = r.astype(bf16)

    masks = head_masks()

    def pair(p):
        rows = pl.ds(pl.multiple_of(p * PAIR, 16), PAIR)
        kind = 0 if layer == 0 else p & 1
        lanes = [slice(t * 128, t * 128 + 128) for t in range(4)]

        def tile(t, part):
            c = part * WIDE + t * 128
            v = qkv_ref[rows, c : c + 128].astype(f32)
            return v[:CELLS], v[CELLS:]

        ks = [stacked(*tile(t, 1), masks) for t in range(4)]
        qs = [diagonal(*tile(t, 0)) for t in range(4)]
        vs = [stacked(*tile(t, 2), masks) for t in range(4)]
        sc = [dot_nt(ks[t], qs[t]) for t in range(4)]
        prs = []
        for t in range(4):
            v = scale * sc[t] + bias_ref[kind, t * QT : (t + 1) * QT, :]
            v = v.reshape(4, CELLS, 128)
            e = jnp.exp(v - jnp.max(v, axis=1, keepdims=True))
            pr = e * (1.0 / jnp.sum(e, axis=1, keepdims=True))
            prs.append(pr.reshape(QT, 128).astype(bf16))
        os = [from_diagonal(dot_tn(prs[t], vs[t])) for t in range(4)]
        for t in range(4):
            p_ref[p, t * QT : (t + 1) * QT, :] = prs[t]
            if layer == 0:
                o_ref[rows, lanes[t]] = os[t].astype(bf16)
            else:
                one[pl.ds(p * 2 * WIN, 2 * WIN), :, lanes[t]] = os[t].reshape(2 * WIN, 8, 128)

    loop(NPAIR, pair)
    if layer == 1:
        swap_into(one, o_ref, two)
    o_ref[ROWS:, :] = jnp.zeros((TOK - ROWS, WIDE), bf16)


def attn_fwd(layer, per, plan, ids, xs, w, vec, bias):
    act = sds((TOK, WIDE), bf16)
    saved = (act, sds((TOK, 3 * WIDE), bf16), sds((NPAIR, HEADS * CELLS, 128), bf16), act)
    kernel = functools.partial(attn_fwd_kernel, layer, per, plan)
    scratch = plan.scratch()
    outs = saved
    if layer == 1:
        tile = pltpu.VMEM((NWIN * WIN, 8, WIDE), f32)
        scratch = scratch + [tile, tile]
        outs = (act,) + saved
    return call(
        kernel,
        outs,
        [SM] + [VM] * len(xs) + [HB] * plan.count + [VM, VM],
        scratch,
        2 * TOK * WIDE * 3 * WIDE,
        12 * 10**6,
        limit=30,
    )(ids, *xs, *w, vec, bias)


def mlp_forward(layer, per, pc, load, x_ref, o_ref, w1, vec_ref, f_ref, y_ref, n2_ref, h_ref, g_ref, emit):
    load()
    for half in range(2):
        c0 = half * 256
        r = dot(o_ref[...], gather_rows(w1, 0, per, 0, WIDE, c0, 256))
        x = x_ref[:, c0 : c0 + 256].astype(f32)
        y_ref[:, c0 : c0 + 256] = x + (r + vec_ref[layer, 4:5, c0 : c0 + 256])
    gain = vec_ref[layer, 5:6, :]
    shift = vec_ref[layer, 6:7, :]

    def norm(c):
        rows = pl.ds(pl.multiple_of(c * STRIP, STRIP), STRIP)
        cen, rstd = centred(y_ref[rows, :])
        n2_ref[rows, :] = (cen * rstd * gain + shift).astype(bf16)

    loop(NCH, norm)

    def act(j):
        c0 = pl.multiple_of((j & 1) * 256, 256)
        v = w1[:, pl.ds(pl.multiple_of(per + pc + (j >> 1) * per, 16), per), pl.ds(c0, 256)]
        u = dot(n2_ref[...], v.reshape(WIDE, 256)) + f_ref[layer, j]
        h, g = gelu_pair(u)
        cols = pl.ds(pl.multiple_of(j * 256, 256), 256)
        h_ref[:, cols] = h.astype(bf16)
        g_ref[:, cols] = g.astype(bf16)

    loop(HIDE // 256, act)
    for half in range(2):
        c0 = half * 256
        v = w1[:, per : per + pc, c0 : c0 + 256].reshape(HIDE, 256)
        r = dot(h_ref[...], v)
        emit(c0, y_ref[:, c0 : c0 + 256] + (r + vec_ref[layer, 7:8, c0 : c0 + 256]))


def mlp_load(plan, w_in, w1, s1, ids):
    start_load(plan, w_in, w1, s1, ids)
    return lambda: wait_all(w1, s1)


def mlp_fwd_kernel(per, pc, plan, *refs):
    nw = plan.count
    ids, x_ref, o_ref = refs[:3]
    w_in, refs = refs[3 : 3 + nw], refs[3 + nw :]
    vec_ref, f_ref, y_ref, n2_ref, h_ref, g_ref, xa, xb, xc, xd, nxt, w1, s1 = refs
    load = mlp_load(plan, w_in, w1, s1, ids)

    def emit(c0, v):
        nxt[:, c0 : c0 + 256] = v

    mlp_forward(
        0, per, pc, load, x_ref, o_ref, w1, vec_ref, f_ref, y_ref, n2_ref, h_ref, g_ref, emit
    )
    size = GROUP * CELLS
    for k, out in enumerate((xa, xb, xc, xd)):
        v = nxt[pl.ds(pl.multiple_of((ids[0] ^ k) * size, 8), size), :]
        out[:size, :] = v.astype(bf16)
        out[size:, :] = jnp.zeros((BLOCK - size, WIDE), bf16)


def mlp_fwd(per, pc, plan, ids, x, o, w, vec, f):
    act = sds((TOK, WIDE), bf16)
    wide = sds((TOK, HIDE), bf16)
    return call(
        functools.partial(mlp_fwd_kernel, per, pc, plan),
        (sds((TOK, WIDE), f32), act, wide, wide) + (sds((BLOCK, WIDE), bf16),) * 4,
        [SM, VM, VM] + [HB] * len(w) + [VM, VM],
        [pltpu.VMEM((TOK, WIDE), f32)] + plan.scratch(),
        2 * TOK * WIDE * (WIDE + 2 * HIDE),
        25 * 10**6,
        limit=40,
    )(ids, x, o, *w, vec, f)


def rows_sum(v):
    return jnp.sum(v, axis=0, keepdims=True)


def mlp_back(per, pc, plan, ids, dm_ref, wc, n2_ref, h_ref, g_ref, du, df_ref, dm_sum, outs, scratch):
    turned, g1, t1 = scratch
    shards = WIDE // per
    turned[...] = n2_ref[...].T
    grows = WIDE // pc

    def step(j):
        cols = pl.ds(pl.multiple_of(j * WIDE, WIDE), WIDE)
        w = wc[pl.ds(j * grows, grows)].reshape(WIDE, WIDE)
        dm = dm_ref[...]
        dh = dot_nt(dm, w)
        d = (dh * g_ref[:, cols].astype(f32)).astype(bf16)
        du[:, cols] = d
        total = rows_sum(d.astype(f32))
        for half in range(2):
            df_ref[2 * j + half] = total[:, half * 256 : half * 256 + 256]
        gc = dot_tn(h_ref[:, cols], dm)
        g1[pl.ds(j * grows, grows), 0:pc, :] = gc.astype(bf16).reshape(grows, pc, WIDE)
        ge = dot(turned[...], d)
        g1[:, pl.ds(pl.multiple_of(pc + j * per, 16), per), :] = ge.astype(bf16).reshape(
            shards, per, WIDE
        )

    loop(HIDE // WIDE, step)
    start_grads(plan, g1, outs, t1, ids)
    dm_sum[...] = rows_sum(dm_ref[...].astype(f32))
    return lambda: wait_all(g1, t1)


def mlp_back_scratch(gplan):
    return [pltpu.VMEM((WIDE, TOK), bf16)] + gplan.scratch()


def mlp_back_outs(gplan):
    outs = (
        sds((TOK, WIDE), bf16),
        sds((TOK, HIDE), bf16),
        sds((8, 1, 256), f32),
        sds((1, WIDE), f32),
    )
    return outs + grad_shapes(gplan)


def mlp_both_kernel(per, pc, plan, gplan, *refs):
    nw = plan.count
    ids, x_ref, o_ref = refs[:3]
    w_in, refs = refs[3 : 3 + nw], refs[3 + nw :]
    vec_ref, f_ref = refs[:2]
    cots, blocks, refs = refs[2:6], refs[6:10], refs[10:]
    do_ref, dy_ref, da_ref, gv_ref, df_ref, dm_sum = refs[:6]
    outs, refs = refs[6:8], refs[8:]
    y_ref, dm_ref, du, n2_ref, h_ref, g_ref, nxt, tmp, w1, s1 = refs[:10]
    scratch = refs[10:]
    load = mlp_load(plan, w_in, w1, s1, ids)

    def emit(c0, v):
        nxt[:, c0 : c0 + 256] = v

    mlp_forward(
        1, per, pc, load, x_ref, o_ref, w1, vec_ref, f_ref, y_ref, n2_ref, h_ref, g_ref, emit
    )
    s = ids[0]
    size = GROUP * CELLS
    for k, out in enumerate(blocks):
        for i in range(GROUP):
            row = pl.multiple_of((i * 4 + (s ^ k)) * CELLS, 8)
            tmp[i * CELLS : (i + 1) * CELLS, :] = nxt[pl.ds(row, CELLS), :]
        out[:size, :] = tmp[:size, :].astype(bf16)
        out[size:, :] = jnp.zeros((BLOCK - size, WIDE), bf16)
    for k, ref in enumerate(cots):
        v = ref[:size, :].astype(f32)
        for i in range(GROUP):
            row = pl.multiple_of((i * 4 + (s ^ k)) * CELLS, 8)
            nxt[pl.ds(row, CELLS), :] = v[i * CELLS : (i + 1) * CELLS, :]
    dm_ref[:ROWS, :] = nxt[:ROWS, :].astype(bf16)
    dm_ref[ROWS:, :] = jnp.zeros((TOK - ROWS, WIDE), bf16)
    wc = w1.at[:, per : per + pc, :]
    done = mlp_back(
        per, pc, gplan, ids, dm_ref, wc, n2_ref, h_ref, g_ref, du, df_ref, dm_sum, outs, scratch
    )
    mid_body(1, per, pc, w1, vec_ref, y_ref, dm_ref, du, do_ref, dy_ref, da_ref, gv_ref, nxt)
    done()


def mlp_both(per, pc, plan, gplan, ids, x, o, w, vec, f, cots):
    block = sds((BLOCK, WIDE), bf16)
    outs = (block,) * 4 + mid_outs() + mlp_back_outs(gplan)[2:]
    scratch = [
        pltpu.VMEM((TOK, WIDE), f32),
        pltpu.VMEM((TOK, WIDE), bf16),
        pltpu.VMEM((TOK, HIDE), bf16),
        pltpu.VMEM((TOK, WIDE), bf16),
        pltpu.VMEM((TOK, HIDE), bf16),
        pltpu.VMEM((TOK, HIDE), bf16),
        pltpu.VMEM((TOK, WIDE), f32),
        pltpu.VMEM((BLOCK, WIDE), f32),
    ]
    return call(
        functools.partial(mlp_both_kernel, per, pc, plan, gplan),
        outs,
        [SM, VM, VM] + [HB] * len(w) + [VM] * 6,
        scratch + plan.scratch() + mlp_back_scratch(gplan),
        5 * TOK * WIDE * (WIDE + 2 * HIDE),
        25 * 10**6,
        (VM,) * 10 + (HB,) * 2,
    )(ids, x, o, *w, vec, f, *cots)


def mlp_bwd_kernel(per, pc, plan, gplan, *refs):
    nw = plan.count
    ids, w_in, refs = refs[0], refs[1 : 1 + nw], refs[1 + nw :]
    n2_ref, h_ref, g_ref = refs[:3]
    grads, refs = refs[3:7], refs[7:]
    dm_ref, du, df_ref, dm_sum = refs[:4]
    outs, refs = refs[4:6], refs[6:]
    tmp, w1, s1 = refs[:3]
    scratch = refs[3:]
    start_load(plan, w_in, w1, s1, ids, ((per, per + pc),))
    s = ids[0]
    size = GROUP * CELLS
    for k, ref in enumerate(grads):
        tmp[pl.ds(pl.multiple_of((s ^ k) * size, 8), size), :] = ref[:size, :].astype(f32)
    dm_ref[:ROWS, :] = tmp[:ROWS, :].astype(bf16)
    dm_ref[ROWS:, :] = jnp.zeros((TOK - ROWS, WIDE), bf16)
    wc = w1.at[:, per : per + pc, :]
    wait_all(wc, s1)
    mlp_back(
        per, pc, gplan, ids, dm_ref, wc, n2_ref, h_ref, g_ref, du, df_ref, dm_sum, outs, scratch
    )()


def mlp_bwd(per, pc, plan, gplan, ids, w, n2, h, g, grads):
    return call(
        functools.partial(mlp_bwd_kernel, per, pc, plan, gplan),
        mlp_back_outs(gplan),
        [SM] + [HB] * len(w) + [VM] * 7,
        [pltpu.VMEM((TOK, WIDE), f32)] + plan.scratch() + mlp_back_scratch(gplan),
        3 * TOK * WIDE * 2 * HIDE,
        25 * 10**6,
        (VM,) * 4 + (HB,) * 2,
        limit=48,
    )(ids, *w, n2, h, g, *grads)


def mid_kernel(layer, per, pc, plan, *refs):
    nw = plan.count
    ids, w_in, refs = refs[0], refs[1 : 1 + nw], refs[1 + nw :]
    vec_ref, y_ref, dm_ref, du, do_ref, dy_ref, da_ref, gv_ref, dn2, w1, s1, s2 = refs
    spans = ((0, per), (per + pc, 5 * per + pc))
    start_load(plan, w_in, w1, s1, ids, spans[:1])
    start_load(plan, w_in, w1, s2, ids, spans[1:])
    for (lo, hi), sem in zip(spans, (s1, s2)):
        wait_all(w1.at[:, lo:hi, :], sem)
    mid_body(layer, per, pc, w1, vec_ref, y_ref, dm_ref, du, do_ref, dy_ref, da_ref, gv_ref, dn2)


def mid_outs():
    act = sds((TOK, WIDE), bf16)
    return (act, sds((TOK, WIDE), f32), act, sds((8, WIDE), f32))


def mid_body(layer, per, pc, w1, vec_ref, y_ref, dm_ref, du, do_ref, dy_ref, da_ref, gv_ref, dn2):
    gv_ref[...] = jnp.zeros_like(gv_ref)
    for half in range(2):
        total = None
        for c in range(4):
            w = gather_rows(w1, per + pc + c * per, per, half, 256, 0, WIDE)
            part = dot_nt(du[:, c * WIDE : (c + 1) * WIDE], w)
            total = part if total is None else total + part
        dn2[:, half * 256 : half * 256 + 256] = total
    gain = vec_ref[layer, 5:6, :]

    def norm(c):
        rows = pl.ds(pl.multiple_of(c * STRIP, STRIP), STRIP)
        cen, rstd = centred(y_ref[rows, :])
        xhat = cen * rstd
        dn = dn2[rows, :]
        gv_ref[5:6, :] += rows_sum(dn * xhat)
        gv_ref[6:7, :] += rows_sum(dn)
        dx = dn * gain
        m1 = jnp.mean(dx, axis=-1, keepdims=True)
        m2 = jnp.mean(dx * xhat, axis=-1, keepdims=True)
        dy = dm_ref[rows, :].astype(f32) + rstd * (dx - m1 - xhat * m2)
        dy_ref[rows, :] = dy
        da = dy.astype(bf16)
        gv_ref[4:5, :] += rows_sum(da.astype(f32))
        da_ref[rows, :] = da

    loop(NCH, norm)
    for half in range(2):
        c0 = half * 256
        w = gather_rows(w1, 0, per, half, 256, 0, WIDE)
        do_ref[:, c0 : c0 + 256] = dot_nt(da_ref[...], w).astype(bf16)


def mid_bwd(layer, per, pc, plan, ids, w, vec, y, dm, du):
    return call(
        functools.partial(mid_kernel, layer, per, pc, plan),
        mid_outs(),
        [SM] + [HB] * len(w) + [VM] * 4,
        [pltpu.VMEM((TOK, WIDE), f32)] + plan.scratch() + [pltpu.SemaphoreType.DMA],
        2 * TOK * WIDE * (WIDE + HIDE),
        16 * 10**6,
        limit=34,
    )(ids, *w, vec, y, dm, du)


def attn_bwd_kernel(layer, do_ref, qkv_ref, p_ref, dqkv, gv_ref, gt_ref, *rest):
    dsum = rest[0]
    if layer == 1:
        one, two = rest[1:]

        def widen(p):
            v = do_ref[pl.ds(pl.multiple_of(p * PAIR, 16), PAIR), :].astype(f32)
            one[pl.ds(p * 2 * WIN, 2 * WIN)] = v.reshape(2 * WIN, 8, WIDE)

        loop(NPAIR, widen)

        def emit(w, tile):
            two[pl.ds(w * WIN, WIN)] = tile

        swap_windows(one, emit)
    gv_ref[...] = jnp.zeros_like(gv_ref)
    dsum[...] = jnp.zeros_like(dsum)
    dqkv[ROWS:, :] = jnp.zeros((TOK - ROWS, 3 * WIDE), bf16)
    masks = head_masks()

    def pair(p):
        rows = pl.ds(pl.multiple_of(p * PAIR, 16), PAIR)
        def tile(t, part):
            c = part * WIDE + t * 128
            v = qkv_ref[rows, c : c + 128].astype(f32)
            return v[:CELLS], v[CELLS:]

        def grad(t):
            c = t * 128
            if layer == 0:
                d = do_ref[rows, c : c + 128].astype(f32)
            else:
                d = two[pl.ds(p * 2 * WIN, 2 * WIN), :, c : c + 128].reshape(PAIR, 128)
            return d[:CELLS], d[CELLS:]

        four = range(4)
        vs = [stacked(*tile(t, 2), masks) for t in four]
        dd = [diagonal(*grad(t)) for t in four]
        ks = [stacked(*tile(t, 1), masks) for t in four]
        qs = [diagonal(*tile(t, 0)) for t in four]
        pb = [p_ref[p, t * QT : (t + 1) * QT, :] for t in four]
        dp = [dot_nt(vs[t], dd[t]) for t in four]
        dv = [from_stacked(dot(pb[t], dd[t]), masks).astype(bf16) for t in four]
        ds = []
        for t in four:
            pf = pb[t].astype(f32).reshape(4, CELLS, 128)
            g = dp[t].reshape(4, CELLS, 128)
            tot = jnp.sum(g * pf, axis=1, keepdims=True)
            ds.append((pf * (g - tot)).reshape(QT, 128).astype(bf16))
        dq = [(scale * from_diagonal(dot_tn(ds[t], ks[t]))).astype(bf16) for t in four]
        dk = [(scale * from_stacked(dot(ds[t], qs[t]), masks)).astype(bf16) for t in four]
        for t in four:
            c = t * 128
            dsum[4 * t : 4 * t + 4] += ds[t].astype(f32).reshape(4, CELLS, 128)
            dqkv[rows, c : c + 128] = dq[t]
            dqkv[rows, WIDE + c : WIDE + c + 128] = dk[t]
            dqkv[rows, 2 * WIDE + c : 2 * WIDE + c + 128] = dv[t]
            gv_ref[2:3, c : c + 128] += rows_sum(dq[t].astype(f32))
            gv_ref[3:4, c : c + 128] += rows_sum(dv[t].astype(f32))

    loop(NPAIR, pair)
    total = jnp.zeros((HEADS, 256), f32)
    for rb in range(WIN):
        x = jnp.concatenate([dsum[:, rb * 8 + cb, :] for cb in range(8)], axis=1)
        hi = x.astype(bf16)
        lo = (x - hi.astype(f32)).astype(bf16)
        oh = onehot(rb, layer == 1)
        total = total + (dot_nt(hi, oh) + dot_nt(lo, oh))
    gt_ref[...] = total


def attn_bwd(layer, do, qkv, probs):
    tile = pltpu.VMEM((NWIN * WIN, 8, WIDE), f32)
    return call(
        functools.partial(attn_bwd_kernel, layer),
        (sds((TOK, 3 * WIDE), bf16), sds((8, WIDE), f32), sds((HEADS, 256), f32)),
        [VM] * 3,
        [pltpu.VMEM((HEADS, CELLS, 128), f32)] + [tile, tile] * layer,
        2 * TOK * WIDE * 3 * WIDE,
        12 * 10**6,
        limit=28,
    )(do, qkv, probs)


def qkv_grad_kernel(per, plan, ids, n1_ref, dqkv, o_ref, da_ref, keep, send, turned, gq, sem):
    shards = WIDE // per
    turned[...] = o_ref[...].T
    for half in range(2):
        c0 = half * 256
        g = dot(turned[...], da_ref[:, c0 : c0 + 256])
        gq[:, 3 * per : 4 * per, c0 : c0 + 256] = g.astype(bf16).reshape(shards, per, 256)
    turned[...] = n1_ref[...].T
    for j in range(3):
        for half in range(2):
            c0 = half * 256
            g = dot(turned[...], dqkv[:, j * WIDE + c0 : j * WIDE + c0 + 256])
            gq[:, j * per : (j + 1) * per, c0 : c0 + 256] = g.astype(bf16).reshape(
                shards, per, 256
            )
    start_grads(plan, gq, (keep, send), sem, ids)
    wait_all(gq, sem)


def qkv_grad(per, plan, ids, n1, dqkv, o, da):
    return call(
        functools.partial(qkv_grad_kernel, per, plan),
        grad_shapes(plan),
        [SM, VM, VM, VM, VM],
        [pltpu.VMEM((WIDE, TOK), bf16)] + plan.scratch(),
        2 * TOK * WIDE * 4 * WIDE,
        9 * 10**6,
        (HB, HB),
        limit=24,
    )(ids, n1, dqkv, o, da)


def dx_kernel(layer, per, plan, *refs):
    nw = plan.count
    ids, dqkv, dy_ref, x_ref = refs[:4]
    w_in, vec_ref, refs = refs[4 : 4 + nw], refs[4 + nw], refs[5 + nw :]
    nout = 1 if layer == 0 else 4
    dx_refs, gv_ref, refs = refs[:nout], refs[nout], refs[nout + 1 :]
    dn, one, w_ref, sem = refs
    start_load(plan, w_in, w_ref, sem, ids)
    gv_ref[...] = jnp.zeros_like(gv_ref)
    wait_all(w_ref, sem)
    for half in range(2):
        total = None
        for c in range(3):
            w = gather_rows(w_ref, c * per, per, half, 256, 0, WIDE)
            part = dot_nt(dqkv[:, c * WIDE : (c + 1) * WIDE], w)
            total = part if total is None else total + part
        dn[:, half * 256 : half * 256 + 256] = total
    gain = vec_ref[layer, 0:1, :]
    if layer == 1:

        def widen_dn(p):
            v = dn[pl.ds(pl.multiple_of(p * PAIR, 8), PAIR), :].astype(bf16).astype(f32)
            one[pl.ds(p * 2 * WIN, 2 * WIN)] = v.reshape(2 * WIN, 8, WIDE)

        loop(NPAIR, widen_dn)

        def emit_dn(w, tile):
            dn[pl.ds(pl.multiple_of(w * CELLS, 8), CELLS), :] = tile.reshape(CELLS, WIDE)

        swap_windows(one, emit_dn)

    def norm(p):
        rows = pl.ds(pl.multiple_of(p * FOUR, 16), FOUR)
        cen, rstd = centred(x_ref[rows, :].astype(f32))
        xhat = cen * rstd
        d = dn[rows, :]
        gv_ref[0:1, :] += rows_sum(d * xhat)
        gv_ref[1:2, :] += rows_sum(d)
        dx = d * gain
        m1 = jnp.mean(dx, axis=-1, keepdims=True)
        m2 = jnp.mean(dx * xhat, axis=-1, keepdims=True)
        out = dy_ref[rows, :] + rstd * (dx - m1 - xhat * m2)
        one[pl.ds(p * QUADS, QUADS)] = out.reshape(QUADS, 8, WIDE)

    loop(GROUP, norm)
    if layer == 0:
        put_dense(dx_refs[0], one)
    else:
        s = ids[0]
        size = GROUP * CELLS
        for k, out in enumerate(dx_refs):
            for i in range(GROUP):
                tile = one[pl.ds((i * 4 + (s ^ k)) * WIN, WIN)]
                dn[i * CELLS : (i + 1) * CELLS, :] = tile.reshape(CELLS, WIDE)
            out[:size, :] = dn[:size, :].astype(bf16)
            out[size:, :] = jnp.zeros((BLOCK - size, WIDE), bf16)


def dx_step(layer, per, plan, ids, dqkv, dy, x, w, vec):
    if layer == 0:
        outs = (sds((NWIN * WIN * WIN * 4, QUAD), f32),)
    else:
        outs = (sds((BLOCK, WIDE), bf16),) * 4
    tile = pltpu.VMEM((NWIN * WIN, 8, WIDE), f32)
    return call(
        functools.partial(dx_kernel, layer, per, plan),
        outs + (sds((8, WIDE), f32),),
        [SM, VM, VM, VM] + [HB] * plan.count + [VM],
        [pltpu.VMEM((TOK, WIDE), f32), tile] + plan.scratch(),
        2 * TOK * WIDE * 3 * WIDE,
        12 * 10**6,
        limit=28,
    )(ids, dqkv, dy, x, *w, vec)


def join_kernel(ids, xa, xb, xc, xd, out_ref, pad):
    s = ids[0]
    size = GROUP * CELLS
    for k, ref in enumerate((xa, xb, xc, xd)):
        v = ref[:size, :].astype(f32).reshape(GROUP * WIN, 8, WIDE)
        pad[pl.ds((s ^ k) * GROUP * WIN, GROUP * WIN)] = v
    put_dense(out_ref, pad)


def join_blocks(ids, blocks):
    return call(
        join_kernel,
        (sds((NWIN * WIN * WIN * 4, QUAD), f32),),
        [SM] + [VM] * 4,
        [pltpu.VMEM((NWIN * WIN, 8, WIDE), f32)],
        10**6,
        5 * 10**6,
        limit=16,
    )(ids, *blocks)[0]


def hop(value, way):
    axes = {"c": ("core",), "cy": ("y", "core"), "xy": ("y", "x")}.get(way, (way[0],))
    mask = {"z2": 2, "z3": 3, "cy": 3, "xy": 3}.get(way, 1)
    size = math.prod(lax.axis_size(a) for a in axes)
    return lax.ppermute(value, axes, [(i, i ^ mask) for i in range(size)])


def tie(*values):
    return lax.optimization_barrier(values)


def exchange(blocks):
    return [blocks[0]] + [hop(b, way) for b, way in zip(blocks[1:], ("c", "y", "cy"))]


def swap_all(value, axes):
    return lax.all_to_all(value, axes, 0, 0)


def share(value, axes):
    n = math.prod(lax.axis_size(a) for a in axes)
    return swap_all(jnp.stack([value] * n), axes)


def gather_c(gs):
    return gs + [hop(g, "c") for g in gs]


def add16(*terms):
    total = terms[0].astype(f32)
    for t in terms[1:]:
        total = total + t.astype(f32)
    return total.astype(bf16)


def step_core(grads, r):
    keep = grads[0]
    return add16(keep[0], r[0]), hop(add16(keep[1], r[1]), "x")


def step_next(own, r, way):
    return add16(own[0], r[0]), hop(add16(own[1], r[1]), way)


def step_last(own, r):
    f = add16(own, r)
    return f, hop(f, "y")


def step_spread(f, r):
    f = add16(f, r)
    return [f, hop(f, "c")]


def half_reduce(grads, shard):
    total = add16(grads[0], hop(grads[1], "c"))
    total = total.reshape((-1,) + total.shape[2:])
    f = lax.psum_scatter(total, ("y",) + shard, scatter_dimension=0, tiled=False)
    return [f, hop(f, "y"), hop(f, "c"), hop(f, "cy")]


def adam_math(weight, moment_one, moment_two, gradient, step_rate, decay_rate):
    first_new = beta_one * moment_one + (1.0 - beta_one) * gradient
    second_new = beta_two * moment_two + (1.0 - beta_two) * gradient * gradient
    correct_one = 1.0 - beta_one**ADAM_STEP
    correct_two = 1.0 - beta_two**ADAM_STEP
    update = first_new / correct_one / (jnp.sqrt(second_new / correct_two) + adam_eps)
    weight_new = weight * (1.0 - step_rate * decay_rate) - step_rate * update
    return (first_new, second_new, weight_new)


def adam_kernel(segments, members, old, count, ids, *refs):
    n = len(members)
    blocks, refs = refs[:count], refs[count:]
    ins, outs, tot = refs[: 3 * n], refs[3 * n + old : 6 * n + old], refs[-1]
    c, y, x, z = place(ids)
    for k, ref in enumerate(blocks):
        if count == 2:
            lane = pl.multiple_of((c ^ k) * HALF, HALF)
        else:
            lane = pl.multiple_of((c ^ (k >> 1)) * HALF + (y ^ (k & 1)) * QUAD, QUAD)
        tot[:, pl.ds(lane, WIDE // count)] = ref[...].astype(f32)
    for row, m, count, col in segments:
        at = (0, slice(0, count), slice(col, col + WIDE))
        pos = members[m]
        new = adam_math(
            ins[3 * m][at],
            ins[3 * m + 1][at],
            ins[3 * m + 2][at],
            tot[row : row + count, :],
            step_rates[pos],
            decay_rates[pos],
        )
        for k in range(3):
            outs[3 * m + k][at] = new[k]


def adam_step(layer, segments, members, ids, blocks, params, old):
    ins = [a for pos in members for a in (params[0][pos], params[1][pos], params[2][pos])]
    rows = blocks[0].shape[0]

    def spec(a):
        return pl.BlockSpec((1,) + a.shape[1:], lambda i: (layer, 0, 0))

    outs = tuple(sds(a.shape, f32) for a in ins)
    held = list(old or [])
    base = 1 + len(blocks) + len(ins)
    return pl.pallas_call(
        functools.partial(adam_kernel, segments, members, len(held), len(blocks)),
        grid=(1,),
        out_shape=outs,
        in_specs=[SM]
        + [pl.BlockSpec(b.shape, lambda i: (0, 0)) for b in blocks]
        + [spec(a) for a in ins]
        + [HB] * len(held),
        out_specs=tuple(spec(a) for a in ins),
        scratch_shapes=[pltpu.VMEM((rows, WIDE), f32)],
        input_output_aliases={base + k: k for k in range(len(held))},
        compiler_params=pltpu.CompilerParams(vmem_limit_bytes=24 * MIB),
        cost_estimate=pl.CostEstimate(
            flops=20 * rows * WIDE, bytes_accessed=24 * rows * WIDE, transcendentals=0
        ),
    )(ids, *blocks, *ins, *held)


def body(shard, *args):
    inputs, cotangent, image_valid = args[:3]
    masters, firsts, seconds = args[3:9], args[9:15], args[15:21]
    params = (masters, firsts, seconds)
    per = masters[0].shape[1]
    pc = masters[3].shape[1]
    own = masters[5].shape[0]
    shards = WIDE // per
    fast = len(shard) == 2
    seq = lax.axis_index(("y", "core")).astype(jnp.int32)
    me = lax.axis_index(shard).astype(jnp.int32)
    ids = jnp.stack([seq, me])

    nq, nm = 3 * per, 5 * per + pc
    whole = ((0, nq + nm, HALF),)
    wide = "wide" if fast else "half"
    pq0 = Plan(wide, shards, nq)
    pm0 = Plan("near" if fast else "half", shards, nm, 0 if fast else nq)
    part = "part" if fast else "half"
    pq1, pm1 = Plan(part, shards, nq), Plan(part, shards, nm, nq)
    gqp, gmp = Plan(wide, shards, 4 * per), Plan(wide, shards, 4 * per + pc)
    x_in = inputs.reshape(NWIN * WIN, WIN, WIDE)
    cot = cotangent.reshape(NWIN * WIN * WIN * 4, QUAD)
    seg_q = [(j * per, 0, per, j * WIDE) for j in range(3)] + [(3 * per, 1, per, 0)]
    seg_m = [(0, 1, pc, 0)] + [(pc + j * per, 0, per, j * WIDE) for j in range(4)]

    def adam_q(layer, blocks, old=None):
        return adam_step(layer, seg_q, (0, 1), ids, blocks, params, old)

    def adam_m(layer, blocks, old=None):
        return adam_step(layer, seg_m, (2, 3), ids, blocks, params, old)

    def all_smalls(parts):
        rows = []
        for gvm, dms, df, gva, gvx, gt in parts:
            total = gvm + gva + gvx
            rows += [total[:7], dms, df.reshape(4, WIDE), gt.reshape(8, WIDE)]
        return jnp.concatenate(rows, axis=0).astype(bf16)

    if fast:
        em0, eq0 = pack(0, per, pc, ((nq, nq + nm, QUAD), (0, nq, HALF)), "row", ids, masters)
        zq1, zq2 = hop(eq0, "z1"), hop(eq0, "z2")
        (e1,) = pack(1, per, pc, whole, "", ids, masters)
        zq2, e1 = tie(zq2, e1)
        zq3 = hop(zq2, "z1")
        x0, *cots = prep(ids, image_valid, x_in, cot)
        zq1, zq2, zq3, x0, em0 = tie(zq1, zq2, zq3, x0, em0)
        g = jnp.stack([eq0, zq1, zq2, zq3])
        gx = hop(g, "x")
        zm = [hop(em0, way) for way in ("z1", "z2", "z3")]
        vec, hide, bias0, bias1 = expand_smalls(per, own, False, ids, [g, gx])
        vec, zm = tie(vec, zm)
        gm = jnp.stack([em0] + zm)
        wm0 = [gm] + [hop(gm, way) for way in ("x", "y", "xy")]
        wq0 = gather_c([g, gx])
        e1, wq0, gm = tie(e1, wq0, gm)
        z1, z2 = hop(e1, "z1"), hop(e1, "z2")
        n1a, qkva, pa, oa = attn_fwd(0, per, pq0, ids, [x0], wq0, vec, bias0)
        oa, z1, z2, wm0 = tie(oa, z1, z2, wm0)
        z3 = hop(z2, "z1")
        gaq = jnp.stack([v[:nq] for v in (e1, z1, z2)])
        gam = jnp.stack([v[nq:] for v in (e1, z1, z2)])
        gaqx = hop(gaq, "x")
        wm0 = gather_c(wm0)
        wm0, gaq, gam = tie(wm0, gaq, gam)
        gamx = hop(gam, "x")
        gaqc, gamc = hop(gaq, "c"), hop(gam, "c")
        ya, n2a, ha, ga, *x1s = mlp_fwd(per, pc, pm0, ids, x0, oa, wm0, vec, hide)
        x1s, z3, gaqx, gaqc, gamc = tie(x1s, z3, gaqx, gaqc, gamc)
        x1s = exchange(x1s)
        z3x = hop(z3, "x")
        z3c, gaqxc = hop(z3, "c"), hop(gaqx, "c")
        x1s, z3x, z3c, gaqxc = tie(x1s, z3x, z3c, gaqxc)
        z3xc = hop(z3x, "c")
        w1q = [gaq, z3, gaqx, z3x, gaqc, z3c, gaqxc, z3xc]
        cots = exchange(cots)
        x1, n1b, qkvb, pb, ob = attn_fwd(1, per, pq1, ids, x1s, w1q, vec, bias1)
        ob, cots, gamx = tie(ob, cots, gamx)
        w1 = [gam, z3, gamx, z3x, gamc, z3c, hop(gamx, "c"), z3xc]
        res = mlp_both(per, pc, pm1, gmp, ids, x1, ob, w1, vec, hide, cots)
        outs, (dob, dyb, dab, gvm1, df1, dms1), gm1 = res[:4], res[4:10], res[10:12]
        rm1 = hop(gm1[1], "c")
        outs = exchange(outs)
        dqkvb, gva1, gt1 = attn_bwd(1, dob, qkvb, pb)
        dqkvb, rm1, outs = tie(dqkvb, rm1, outs)
        sm1 = step_core(gm1, rm1)
        *dx1s, gvx1 = dx_step(1, per, pq1, ids, dqkvb, dyb, x1, w1q, vec)
        dx1s, dqkvb = tie(dx1s, dqkvb)
        dx1s = exchange(dx1s)
        gq1 = qkv_grad(per, gqp, ids, n1b, dqkvb, ob, dab)
        gq1, dx1s, sm1 = tie(gq1, dx1s, sm1)
        rq1 = hop(gq1[1], "c")
        sm1 = step_next(*sm1, "z1")
        dma, dua, df0, dms0, *gm0 = mlp_bwd(per, pc, pm0, gmp, ids, wm0, n2a, ha, ga, dx1s)
        dua, rq1, sm1, gm0 = tie(dua, rq1, sm1, gm0)
        rm0 = hop(gm0[1], "c")
        sq1 = step_core(gq1, rq1)
        sm1 = step_next(*sm1, "z2")
        doa, dya, daa, gvm0 = mid_bwd(0, per, pc, pm0, ids, wm0, vec, ya, dma, dua)
        doa, rm0, sq1, sm1 = tie(doa, rm0, sq1, sm1)
        sm0 = step_core(gm0, rm0)
        sq1 = step_next(*sq1, "z1")
        sm1 = step_last(*sm1)
        dqkva, gva0, gt0 = attn_bwd(0, doa, qkva, pa)
        dqkva, sq1, sm1 = tie(dqkva, sq1, sm1)
        sq1 = step_next(*sq1, "z2")
        fm1 = step_spread(*sm1)
        gq0 = qkv_grad(per, gqp, ids, n1a, dqkva, oa, daa)
        gq0, sm0, sq1, fm1, outs = tie(gq0, sm0, sq1, fm1, outs)
        rq0 = hop(gq0[1], "c")
        sm0 = step_next(*sm0, "z1")
        output = join_blocks(ids, outs)
        output, rq0 = tie(output, rq0)
        sq0 = step_core(gq0, rq0)
        sq1 = step_last(*sq1)
        dx0, gvx0 = dx_step(0, per, pq0, ids, dqkva, dya, x0, wq0, vec)
        dx0, gvx0, sq0, sm0, sq1 = tie(dx0, gvx0, sq0, sm0, sq1)
        sq0 = step_next(*sq0, "z1")
        sm0 = step_next(*sm0, "z2")
        smalls = all_smalls(
            ((gvm0, dms0, df0, gva0, gvx0, gt0), (gvm1, dms1, df1, gva1, gvx1, gt1))
        )
        fq1 = step_spread(*sq1)
        sc = hop(smalls, "c")
        new_m = adam_m(1, fm1)
        new_m, sq0, sc, fq1 = tie(new_m, sq0, sc, fq1)
        sq0 = step_next(*sq0, "z2")
        smalls = add16(smalls, sc)
        sc = hop(smalls, "x")
        new_q = adam_q(1, fq1)
        new_q, sq0, sm0, sc = tie(new_q, sq0, sm0, sc)
        sq0 = step_last(*sq0)
        fm0 = step_spread(*step_last(*sm0))
        smalls = add16(smalls, sc)
        sc = hop(smalls, "z1")
        new_m = adam_m(0, fm0, new_m)
        new_m, sq0, sc = tie(new_m, sq0, sc)
        fq0 = step_spread(*sq0)
        smalls = add16(smalls, sc)
        sc = hop(smalls, "z2")
        fq0, sc = tie(fq0, sc)
        smalls = add16(smalls, sc)
        sc = hop(smalls, "y")
        new_q = adam_q(0, fq0, new_q)
        new_q, sc = tie(new_q, sc)
        smalls = add16(smalls, sc)
    else:
        half0, small = pack(0, per, pc, whole, "own", ids, masters)
        (e1,) = pack(1, per, pc, whole, "", ids, masters)
        x0, *cots = prep(ids, image_valid, x_in, cot)
        cots = exchange(cots)
        small = lax.all_gather(small, shard, axis=0, tiled=False)
        vec, hide, bias0, bias1 = expand_smalls(per, own, True, ids, [small])
        own0 = lax.all_gather(half0, shard, axis=0, tiled=False)
        own1 = lax.all_gather(e1, shard, axis=0, tiled=False)
        w0 = [own0, hop(own0, "c")]
        w1 = [own1, hop(own1, "c")]
        n1a, qkva, pa, oa = attn_fwd(0, per, pq0, ids, [x0], w0, vec, bias0)
        ya, n2a, ha, ga, *x1s = mlp_fwd(per, pc, pm0, ids, x0, oa, w0, vec, hide)
        x1s = exchange(x1s)
        x1, n1b, qkvb, pb, ob = attn_fwd(1, per, pq1, ids, x1s, w1, vec, bias1)
        res = mlp_both(per, pc, pm1, gmp, ids, x1, ob, w1, vec, hide, cots)
        outs, (dob, dyb, dab, gvm1, df1, dms1), gm1 = res[:4], res[4:10], res[10:12]
        output = join_blocks(ids, exchange(outs))
        dqkvb, gva1, gt1 = attn_bwd(1, dob, qkvb, pb)
        *dx1s, gvx1 = dx_step(1, per, pq1, ids, dqkvb, dyb, x1, w1, vec)
        dx1s = exchange(dx1s)
        gq1 = qkv_grad(per, gqp, ids, n1b, dqkvb, ob, dab)
        dma, dua, df0, dms0, *gm0 = mlp_bwd(per, pc, pm0, gmp, ids, w0, n2a, ha, ga, dx1s)
        doa, dya, daa, gvm0 = mid_bwd(0, per, pc, pm0, ids, w0, vec, ya, dma, dua)
        dqkva, gva0, gt0 = attn_bwd(0, doa, qkva, pa)
        gq0 = qkv_grad(per, gqp, ids, n1a, dqkva, oa, daa)
        dx0, gvx0 = dx_step(0, per, pq0, ids, dqkva, dya, x0, w0, vec)
        smalls = all_smalls(
            ((gvm0, dms0, df0, gva0, gvx0, gt0), (gvm1, dms1, df1, gva1, gvx1, gt1))
        )
        smalls = lax.psum(smalls, ("y", "core") + shard)
        fq1, fm1, fq0, fm0 = [half_reduce(g, shard) for g in (gq1, gm1, gq0, gm0)]
        new_m = adam_m(0, fm0, adam_m(1, fm1))
        new_q = adam_q(0, fq0, adam_q(1, fq1))

    smalls = smalls.astype(f32).reshape(2, 20, WIDE)
    g_vec = lax.dynamic_slice_in_dim(smalls[:, :12], me * per, per, axis=2)
    g_tab = smalls[:, 12:20].reshape(2 * HEADS, 256)
    g_tab = lax.dynamic_slice_in_dim(g_tab, me * own, own, axis=0)[:, :SPAN]
    flat = [*new_q, *new_m]
    for pos, g in ((4, g_vec), (5, g_tab)):
        flat += adam_math(
            masters[pos], firsts[pos], seconds[pos], g, step_rates[pos], decay_rates[pos]
        )
    return (output.reshape(inputs.shape), dx0.reshape(inputs.shape), *flat, g_vec[:, 7])


def solution(mesh):
    count = mesh.shape["shard"]
    if count == 8:
        mesh = Mesh(mesh.devices.reshape(2, 2, 4, 2), ("y", "core", "z", "x"))
        shard = ("z", "x")
    else:
        mesh = Mesh(mesh.devices.reshape(2, 2, count), ("y", "core", "s"))
        shard = ("s",)
    tokens = P(shard, ("y", "core"), None, None, None)
    params = (P(None, shard, None),) * 4 + (P(None, None, shard), P(shard, None))
    in_specs = (tokens, tokens, P(shard)) + params * 3
    out_specs = (tokens, tokens)
    for spec in params:
        out_specs = out_specs + (spec,) * 3
    out_specs = out_specs + (P(None, shard),)
    return jax.shard_map(
        functools.partial(body, shard),
        mesh=mesh,
        in_specs=in_specs,
        out_specs=out_specs,
        check_vma=False,
    )
```

```python
import functools
import math

import jax
import jax.numpy as jnp
from jax import lax
from jax.experimental import pallas as pl
from jax.experimental.pallas import tpu as pltpu
from jax.sharding import Mesh
from jax.sharding import PartitionSpec as P

HEADS = 16
WIN = 7
SHIFT = 3
ADAM_STEP = 10
WIDE = 512
HIDE = 2048
HEAD_DIM = 32
SPAN = 169
CELLS = 56
SEQ = 4
NWIN = 20
ROWS = NWIN * CELLS
TOK = 1152
GROUP = NWIN // SEQ
BLOCK = 288
PAIR = 2 * CELLS
NPAIR = NWIN // 2
STRIP = 384
NCH = TOK // STRIP
QUADS = 4 * WIN
FOUR = 4 * CELLS
QT = 4 * CELLS
SMALL = 32
HALF = 256
QUAD = 128

bf16 = jnp.bfloat16
f32 = jnp.float32
norm_eps = 1e-05
mask_fill = -100.0
pad_fill = -1e30
beta_one = 0.9
beta_two = 0.999
adam_eps = 1e-08
step_rates = (0.09, 0.35, 0.09, 0.045, 0.5, 2.0)
decay_rates = (0.05, 0.05, 0.05, 0.05, 0.0, 0.0)
scale = HEAD_DIM ** (-0.5)

VM = pl.BlockSpec(memory_space=pltpu.VMEM)
SM = pl.BlockSpec(memory_space=pltpu.SMEM)
HB = pl.BlockSpec(memory_space=pl.ANY)
MIB = 1024 * 1024


def call(kernel, outs, in_specs, scratch, flops, moved, out_specs=None, limit=58):
    return pl.pallas_call(
        kernel,
        out_shape=outs,
        in_specs=in_specs,
        out_specs=out_specs or tuple(VM for _ in outs),
        scratch_shapes=scratch,
        compiler_params=pltpu.CompilerParams(vmem_limit_bytes=limit * MIB),
        cost_estimate=pl.CostEstimate(flops=flops, bytes_accessed=moved, transcendentals=0),
    )


def sds(shape, dtype):
    return jax.ShapeDtypeStruct(shape, dtype)


def dot(a, b):
    return lax.dot_general(a, b, (((1,), (0,)), ((), ())), preferred_element_type=f32)


def dot_nt(a, b):
    return lax.dot_general(a, b, (((1,), (1,)), ((), ())), preferred_element_type=f32)


def dot_tn(a, b):
    return lax.dot_general(a, b, (((0,), (0,)), ((), ())), preferred_element_type=f32)


def loop(count, body):
    lax.fori_loop(0, count, lambda i, c: (body(i), c)[1], 0)


def centred(x):
    mean = jnp.mean(x, axis=-1, keepdims=True)
    cen = x - mean
    var = jnp.mean(cen * cen, axis=-1, keepdims=True)
    return cen, lax.rsqrt(var + norm_eps)


def gelu_pair(u):
    phi = 0.5 + 0.5 * lax.erf(u * math.sqrt(0.5))
    e = jnp.exp2((u * u) * (-0.5 / math.log(2.0)))
    return u * phi, phi + (u * (1.0 / math.sqrt(2.0 * math.pi))) * e


def head_masks():
    lane = lax.broadcasted_iota(jnp.int32, (1, 128), 1)
    return [(lane >> 5) == h for h in range(4)]


def stacked(t0, t1, masks):
    left = jnp.concatenate([jnp.where(m, t0, 0.0) for m in masks], axis=0)
    right = jnp.concatenate([jnp.where(m, t1, 0.0) for m in masks], axis=0)
    return jnp.concatenate([left, right], axis=1).astype(bf16)


def diagonal(t0, t1):
    z8 = jnp.zeros((64 - CELLS, 128), f32)
    z64 = jnp.zeros((64, 128), f32)
    left = jnp.concatenate([t0, z8, z64], axis=0)
    right = jnp.concatenate([z64, t1, z8], axis=0)
    return jnp.concatenate([left, right], axis=1).astype(bf16)


def from_diagonal(o):
    return jnp.concatenate([o[:CELLS, :128], o[64 : 64 + CELLS, 128:]], axis=0)


def from_stacked(o, masks):
    total = None
    for h, m in enumerate(masks):
        part = o[h * CELLS : (h + 1) * CELLS]
        part = jnp.concatenate(
            [jnp.where(m, part[:, :128], 0.0), jnp.where(m, part[:, 128:], 0.0)], axis=1
        )
        total = part if total is None else total + part
    return jnp.concatenate([total[:, :128], total[:, 128:]], axis=0)


def swap_windows(src, emit):
    col = lax.broadcasted_iota(jnp.int32, (1, 8, 1), 1)
    first = col < SHIFT

    def image(i):
        tiles = [src[pl.ds((i * 4 + w) * WIN, WIN)] for w in range(4)]
        for r in range(2):
            rows = [
                jnp.concatenate([tiles[(1 - r) * 2 + c][:SHIFT], tiles[r * 2 + c][SHIFT:]], axis=0)
                for c in range(2)
            ]
            for c in range(2):
                emit(i * 4 + r * 2 + c, jnp.where(first, rows[1 - c], rows[c]))

    loop(GROUP, image)


def swap_into(src, dst, keep):
    def emit(w, tile):
        keep[pl.ds(w * WIN, WIN)] = tile

    swap_windows(src, emit)

    def copy(p):
        v = keep[pl.ds(p * 2 * WIN, 2 * WIN)].reshape(PAIR, WIDE)
        dst[pl.ds(pl.multiple_of(p * PAIR, 16), PAIR), :] = v.astype(bf16)

    loop(NPAIR, copy)


def gather_rows(ref, off, per, first, count, c0, width):
    n = count // per
    v = ref[pl.ds(first * n, n), off : off + per, pl.ds(c0, width)]
    return v.reshape(count, width)


class Plan:
    def __init__(self, kind, shards, rows, row0=0):
        self.kind = kind
        self.shards = shards
        self.rows = rows
        self.row0 = row0

    @property
    def count(self):
        return {"near": 8, "wide": 4, "part": 8, "half": 2}[self.kind]

    def scratch(self):
        return [pltpu.VMEM((self.shards, self.rows, WIDE), bf16), pltpu.SemaphoreType.DMA]


def place(ids):
    s, m = ids[0], ids[1]
    return s & 1, s >> 1, m & 1, m >> 1


def start_load(plan, refs, dst, sem, ids, spans=None):
    c, y, x, z = place(ids)
    for lo, hi in spans or ((0, plan.rows),):
        for kc in range(2):
            if plan.kind == "half":
                lane = pl.multiple_of((c ^ kc) * HALF, HALF)
                pltpu.make_async_copy(
                    refs[kc].at[:, plan.row0 + lo : plan.row0 + hi, :],
                    dst.at[:, lo:hi, pl.ds(lane, HALF)],
                    sem,
                ).start()
                continue
            if plan.kind in ("wide", "part"):
                lane = pl.multiple_of((c ^ kc) * HALF, HALF)
                for k in range(8):
                    owner = (z ^ (k & 3)) * 2 + (x ^ (k >> 2))
                    row = 0
                    if plan.kind == "wide":
                        src = refs[kc * 2 + (k >> 2)].at[k & 3]
                    elif k & 3 == 3:
                        src = refs[kc * 4 + (k >> 2) * 2 + 1]
                        row = plan.row0
                    else:
                        src = refs[kc * 4 + (k >> 2) * 2].at[k & 3]
                    pltpu.make_async_copy(
                        src.at[row + lo : row + hi],
                        dst.at[owner, lo:hi, pl.ds(lane, HALF)],
                        sem,
                    ).start()
                continue
            for k in range(16):
                kxy, kz = k >> 2, k & 3
                owner = (z ^ kz) * 2 + (x ^ (kxy & 1))
                lane = pl.multiple_of((c ^ kc) * HALF + (y ^ (kxy >> 1)) * QUAD, QUAD)
                src = refs[kc * 4 + kxy].at[kz, lo:hi]
                pltpu.make_async_copy(src, dst.at[owner, lo:hi, pl.ds(lane, QUAD)], sem).start()


def wait_all(ref, sem):
    pltpu.make_async_copy(ref, ref, sem).wait()


def grad_shapes(plan):
    if plan.kind == "near":
        shape = (4, 4, plan.rows, QUAD)
    elif plan.kind == "wide":
        shape = (2, 2, 2, plan.rows, HALF)
    else:
        shape = (2, plan.shards, plan.rows, QUAD)
    return (sds(shape, bf16), sds(shape, bf16))


def start_grads(plan, src, outs, sem, ids):
    c, y, x, z = place(ids)
    for kc in range(2):
        if plan.kind == "near":
            for k in range(16):
                kxy, kz = k >> 2, k & 3
                owner = (z ^ kz) * 2 + (x ^ (kxy & 1))
                lane = pl.multiple_of((c ^ kc) * HALF + (y ^ (kxy >> 1)) * QUAD, QUAD)
                pltpu.make_async_copy(
                    src.at[owner, :, pl.ds(lane, QUAD)], outs[kc].at[kxy, kz], sem
                ).start()
        elif plan.kind == "wide":
            lane = pl.multiple_of((c ^ kc) * HALF, HALF)
            for k in range(8):
                owner = (z ^ (k & 3)) * 2 + (x ^ (k >> 2))
                pltpu.make_async_copy(
                    src.at[owner, :, pl.ds(lane, HALF)],
                    outs[kc].at[k >> 2, k & 1, (k >> 1) & 1],
                    sem,
                ).start()
        else:
            for part in range(2):
                lane = pl.multiple_of((c ^ kc) * HALF + part * QUAD, QUAD)
                pltpu.make_async_copy(
                    src.at[:, :, pl.ds(lane, QUAD)], outs[kc].at[part], sem
                ).start()


def put_dense(dst, pad):
    def group(i):
        for q in range(4):
            tile = pad[i, :WIN, q * QUAD : (q + 1) * QUAD]
            dst[pl.ds(4 * WIN * i + q, WIN, stride=4), :] = tile

    loop(NWIN * WIN, group)


def prep_kernel(ids, valid_ref, x_ref, cot_ref, x_out, c0, c1, c2, c3, pad):
    s = ids[0]
    pad[...] = jnp.zeros_like(pad)
    x_out[ROWS:, :] = jnp.zeros((TOK - ROWS, WIDE), bf16)

    def xrow(i):
        pad[pl.ds(i * WIN, WIN), :WIN, :] = x_ref[pl.ds(i * WIN, WIN)].astype(f32)

    loop(NWIN, xrow)

    def xpair(i):
        v = pad[pl.ds(i * 2 * WIN, 2 * WIN)].reshape(PAIR, WIDE)
        x_out[pl.ds(pl.multiple_of(i * PAIR, 16), PAIR), :] = v.astype(bf16)

    loop(NPAIR, xpair)

    def image(i):
        v = valid_ref[i].astype(f32)

        def row(r):
            g = i * WIN + r
            for q in range(4):
                tile = cot_ref[pl.ds(4 * WIN * g + q, WIN, stride=4), :]
                pad[g, :WIN, q * QUAD : (q + 1) * QUAD] = tile * v

        loop(WIN, row)

    loop(NWIN, image)
    for k, out in enumerate((c0, c1, c2, c3)):
        d = s ^ k
        v = pad[pl.ds(d * GROUP * WIN, GROUP * WIN)].reshape(GROUP * CELLS, WIDE)
        out[: GROUP * CELLS, :] = v.astype(bf16)
        out[GROUP * CELLS :, :] = jnp.zeros((BLOCK - GROUP * CELLS, WIDE), bf16)


def prep(ids, valid, x, cot):
    block = sds((BLOCK, WIDE), bf16)
    return call(
        prep_kernel,
        (sds((TOK, WIDE), bf16), block, block, block, block),
        [SM, SM, VM, VM],
        [pltpu.VMEM((NWIN * WIN, 8, WIDE), f32)],
        10**6,
        10**7,
        limit=16,
    )(ids, valid, x, cot)


def pack_rows(per, pc, q, p, e, k):
    parts = [(q, 0, per, j * WIDE) for j in range(3)]
    parts += [(p, 0, per, 0), (k, 0, pc, 0)]
    parts += [(e, 0, per, j * WIDE) for j in range(4)]
    return parts


def pack_kernel(per, pc, widths, count, ids, q, p, e, k, vec, tab, *refs):
    outs, tmp = refs[:count], refs[count:]
    c = ids[0] & 1
    y = ids[0] >> 1
    row = 0
    for ref, r0, n, col in pack_rows(per, pc, q, p, e, k):
        at = row
        for out, (lo, hi, wide) in zip(outs, widths):
            if lo <= row < hi:
                off = c * HALF + (y * QUAD if wide == QUAD else 0)
                lane = pl.multiple_of(col + off, QUAD)
                at = row - lo
                out[at : at + n, :] = ref[0, r0 : r0 + n, pl.ds(lane, wide)].astype(bf16)
        row += n
    if tmp:
        small = tmp[0]
        small[...] = jnp.zeros_like(small)
        small[0:12, :per] = vec[0]
        small[12:24, :per] = vec[1]
        small[24 : 24 + tab.shape[0], :SPAN] = tab[...]
        n = outs[-1].shape[0]
        outs[-1][n - SMALL :, :] = small[...].astype(bf16)


def pack(layer, per, pc, pieces, small, ids, masters):
    q, p, e, k, vec, tab = masters
    outs = tuple(sds((hi - lo, wide), bf16) for lo, hi, wide in pieces)
    if small == "row":
        outs = outs[:-1] + (sds((outs[-1].shape[0] + SMALL, HALF), bf16),)
    if small == "own":
        outs = outs + (sds((SMALL, HALF), bf16),)

    def spec(a):
        return pl.BlockSpec((1,) + a.shape[1:], lambda i: (layer, 0, 0))

    def whole(shape):
        return pl.BlockSpec(shape, lambda i: (0,) * len(shape))

    return pl.pallas_call(
        functools.partial(pack_kernel, per, pc, pieces, len(outs)),
        grid=(1,),
        scratch_shapes=[pltpu.VMEM((SMALL, HALF), f32)] if small else [],
        out_shape=outs,
        in_specs=[SM, spec(q), spec(p), spec(e), spec(k), whole(vec.shape), whole(tab.shape)],
        out_specs=tuple(whole(o.shape) for o in outs),
        compiler_params=pltpu.CompilerParams(vmem_limit_bytes=58 * MIB),
        cost_estimate=pl.CostEstimate(flops=10**5, bytes_accessed=3 * 10**6, transcendentals=0),
    )(ids, q, p, e, k, vec, tab)


def onehot(rb, shifted):
    lane = lax.broadcasted_iota(jnp.int32, (1, 1024), 1)
    cb = lane >> 7
    a = lane & 63
    ra = a >> 3
    ca = a & 7

    def moved(v):
        return jnp.where(v >= SHIFT, v - SHIFT, v + WIN - SHIFT) if shifted else v

    rbm = (rb - SHIFT if rb >= SHIFT else rb + WIN - SHIFT) if shifted else rb
    idx = (moved(ra) - rbm + WIN - 1) * (2 * WIN - 1) + moved(ca) - moved(cb) + WIN - 1
    good = (ra < WIN) & (ca < WIN) & (cb < WIN)
    idx = jnp.where(good, idx, -1)
    entry = lax.broadcasted_iota(jnp.int32, (256, 1024), 0)
    return jnp.where(entry == idx, 1.0, 0.0).astype(bf16)


def smalls_kernel(per, own, natural, ids, *refs):
    vec_ref, hide_ref, b0_ref, b1_ref, nat, tmp = refs[-6:]
    shards = WIDE // per
    for k in range(shards):
        if natural:
            nat[k] = refs[0][k].astype(f32)
        else:
            i = ids[1] ^ ((k & 3) * 2 + (k >> 2))
            nat[i] = refs[k >> 2][k & 3, 3 * per :, :].astype(f32)
    for l in range(2):
        rows = jnp.concatenate(
            [nat[i, 12 * l : 12 * l + 12, :per] for i in range(shards)], axis=1
        )
        vec_ref[l] = rows[:8]
        for r in range(4):
            for half in range(2):
                hide_ref[l, 2 * r + half] = rows[8 + r : 9 + r, half * HALF : (half + 1) * HALF]
    for layer in range(2):
        first = layer * (HEADS // own)
        table = jnp.concatenate(
            [nat[first + i, 24 : 24 + own, :] for i in range(HEADS // own)], axis=0
        ).astype(bf16)
        for rb in range(WIN):
            r = dot(table, onehot(rb, layer == 1))
            for cb in range(8):
                tmp[:, rb * 8 + cb, :] = r[:, cb * 128 : (cb + 1) * 128]
        b = lax.broadcasted_iota(jnp.int32, (CELLS, 128), 0)
        lane = lax.broadcasted_iota(jnp.int32, (CELLS, 128), 1)
        a = lane & 63
        gone = (b & 7) == 7
        if layer == 0:
            add = jnp.where(gone, pad_fill, 0.0)
            for h in range(HEADS):
                b0_ref[0, h * CELLS : (h + 1) * CELLS, :] = tmp[h] + add
        else:
            rows = ((b >> 3) < SHIFT) != ((a >> 3) < SHIFT)
            cols = (((b & 7) < SHIFT) != ((a & 7) < SHIFT)) & (lane >= 64)
            for r in range(2):
                cut = cols | rows if r else cols
                add = jnp.where(gone, pad_fill, jnp.where(cut, mask_fill, 0.0))
                for h in range(HEADS):
                    b1_ref[r, h * CELLS : (h + 1) * CELLS, :] = tmp[h] + add


def expand_smalls(per, own, natural, ids, small):
    shards = WIDE // per
    return call(
        functools.partial(smalls_kernel, per, own, natural),
        (
            sds((2, 8, WIDE), f32),
            sds((2, 8, 1, HALF), f32),
            sds((1, HEADS * CELLS, 128), f32),
            sds((2, HEADS * CELLS, 128), f32),
        ),
        [SM] + [VM] * len(small),
        [pltpu.VMEM((shards, SMALL, HALF), f32), pltpu.VMEM((HEADS, CELLS, 128), f32)],
        10**8,
        2 * 10**6,
        limit=16,
    )(ids, *small)


def attn_fwd_kernel(layer, per, plan, *refs):
    ids, nw = refs[0], plan.count
    xs, refs = (refs[1:2], refs[2:]) if layer == 0 else (refs[1:5], refs[5:])
    w_in, vec_ref, bias_ref, refs = refs[:nw], refs[nw], refs[nw + 1], refs[nw + 2 :]
    if layer == 0:
        x_out = xs[0]
        n1_ref, qkv_ref, p_ref, o_ref, w_ref, sem = refs
    else:
        x_out, n1_ref, qkv_ref, p_ref, o_ref, w_ref, sem, one, two = refs
    start_load(plan, w_in, w_ref, sem, ids)
    if layer == 1:
        for k, ref in enumerate(xs):
            w = ids[0] ^ k
            v = ref[: GROUP * CELLS, :].astype(f32).reshape(GROUP, CELLS, WIDE)
            for i in range(GROUP):
                one[pl.ds((i * 4 + w) * WIN, WIN)] = v[i].reshape(WIN, 8, WIDE)

        def put(p):
            v = one[pl.ds(p * 2 * WIN, 2 * WIN)].reshape(PAIR, WIDE)
            x_out[pl.ds(pl.multiple_of(p * PAIR, 16), PAIR), :] = v.astype(bf16)

        loop(NPAIR, put)
        x_out[ROWS:, :] = jnp.zeros((TOK - ROWS, WIDE), bf16)

    gain = vec_ref[layer, 0:1, :]
    shift = vec_ref[layer, 1:2, :]
    if layer == 0:

        def norm(c):
            rows = pl.ds(pl.multiple_of(c * STRIP, STRIP), STRIP)
            cen, rstd = centred(x_out[rows, :].astype(f32))
            n1_ref[rows, :] = (cen * rstd * gain + shift).astype(bf16)

        loop(NCH, norm)
    else:

        def norm(p):
            rows = pl.ds(p * QUADS, QUADS)
            cen, rstd = centred(one[rows].reshape(FOUR, WIDE))
            one[rows] = (cen * rstd * gain + shift).reshape(QUADS, 8, WIDE)

        loop(GROUP, norm)
        swap_into(one, n1_ref, two)
        n1_ref[ROWS:, :] = jnp.zeros((TOK - ROWS, WIDE), bf16)

    wait_all(w_ref, sem)
    for j in range(3):
        for half in range(2):
            c0 = half * 256
            r = dot(n1_ref[...], gather_rows(w_ref, j * per, per, 0, WIDE, c0, 256))
            if j != 1:
                row = 2 if j == 0 else 3
                r = r + vec_ref[layer, row : row + 1, c0 : c0 + 256]
            qkv_ref[:, j * WIDE + c0 : j * WIDE + c0 + 256] = r.astype(bf16)

    masks = head_masks()

    def pair(p):
        rows = pl.ds(pl.multiple_of(p * PAIR, 16), PAIR)
        kind = 0 if layer == 0 else p & 1
        lanes = [slice(t * 128, t * 128 + 128) for t in range(4)]

        def tile(t, part):
            c = part * WIDE + t * 128
            v = qkv_ref[rows, c : c + 128].astype(f32)
            return v[:CELLS], v[CELLS:]

        ks = [stacked(*tile(t, 1), masks) for t in range(4)]
        qs = [diagonal(*tile(t, 0)) for t in range(4)]
        vs = [stacked(*tile(t, 2), masks) for t in range(4)]
        sc = [dot_nt(ks[t], qs[t]) for t in range(4)]
        prs = []
        for t in range(4):
            v = scale * sc[t] + bias_ref[kind, t * QT : (t + 1) * QT, :]
            v = v.reshape(4, CELLS, 128)
            e = jnp.exp(v - jnp.max(v, axis=1, keepdims=True))
            pr = e * (1.0 / jnp.sum(e, axis=1, keepdims=True))
            prs.append(pr.reshape(QT, 128).astype(bf16))
        os = [from_diagonal(dot_tn(prs[t], vs[t])) for t in range(4)]
        for t in range(4):
            p_ref[p, t * QT : (t + 1) * QT, :] = prs[t]
            if layer == 0:
                o_ref[rows, lanes[t]] = os[t].astype(bf16)
            else:
                one[pl.ds(p * 2 * WIN, 2 * WIN), :, lanes[t]] = os[t].reshape(2 * WIN, 8, 128)

    loop(NPAIR, pair)
    if layer == 1:
        swap_into(one, o_ref, two)
    o_ref[ROWS:, :] = jnp.zeros((TOK - ROWS, WIDE), bf16)


def attn_fwd(layer, per, plan, ids, xs, w, vec, bias):
    act = sds((TOK, WIDE), bf16)
    saved = (act, sds((TOK, 3 * WIDE), bf16), sds((NPAIR, HEADS * CELLS, 128), bf16), act)
    kernel = functools.partial(attn_fwd_kernel, layer, per, plan)
    scratch = plan.scratch()
    outs = saved
    if layer == 1:
        tile = pltpu.VMEM((NWIN * WIN, 8, WIDE), f32)
        scratch = scratch + [tile, tile]
        outs = (act,) + saved
    return call(
        kernel,
        outs,
        [SM] + [VM] * len(xs) + [HB] * plan.count + [VM, VM],
        scratch,
        2 * TOK * WIDE * 3 * WIDE,
        12 * 10**6,
        limit=30,
    )(ids, *xs, *w, vec, bias)


def mlp_forward(layer, per, pc, load, x_ref, o_ref, w1, vec_ref, f_ref, y_ref, n2_ref, h_ref, g_ref, emit):
    load()
    for half in range(2):
        c0 = half * 256
        r = dot(o_ref[...], gather_rows(w1, 0, per, 0, WIDE, c0, 256))
        x = x_ref[:, c0 : c0 + 256].astype(f32)
        y_ref[:, c0 : c0 + 256] = x + (r + vec_ref[layer, 4:5, c0 : c0 + 256])
    gain = vec_ref[layer, 5:6, :]
    shift = vec_ref[layer, 6:7, :]

    def norm(c):
        rows = pl.ds(pl.multiple_of(c * STRIP, STRIP), STRIP)
        cen, rstd = centred(y_ref[rows, :])
        n2_ref[rows, :] = (cen * rstd * gain + shift).astype(bf16)

    loop(NCH, norm)

    def act(j):
        c0 = pl.multiple_of((j & 1) * 256, 256)
        v = w1[:, pl.ds(pl.multiple_of(per + pc + (j >> 1) * per, 16), per), pl.ds(c0, 256)]
        u = dot(n2_ref[...], v.reshape(WIDE, 256)) + f_ref[layer, j]
        h, g = gelu_pair(u)
        cols = pl.ds(pl.multiple_of(j * 256, 256), 256)
        h_ref[:, cols] = h.astype(bf16)
        g_ref[:, cols] = g.astype(bf16)

    loop(HIDE // 256, act)
    for half in range(2):
        c0 = half * 256
        v = w1[:, per : per + pc, c0 : c0 + 256].reshape(HIDE, 256)
        r = dot(h_ref[...], v)
        emit(c0, y_ref[:, c0 : c0 + 256] + (r + vec_ref[layer, 7:8, c0 : c0 + 256]))


def mlp_load(plan, w_in, w1, s1, ids):
    start_load(plan, w_in, w1, s1, ids)
    return lambda: wait_all(w1, s1)


def mlp_fwd_kernel(per, pc, plan, *refs):
    nw = plan.count
    ids, x_ref, o_ref = refs[:3]
    w_in, refs = refs[3 : 3 + nw], refs[3 + nw :]
    vec_ref, f_ref, y_ref, n2_ref, h_ref, g_ref, xa, xb, xc, xd, nxt, w1, s1 = refs
    load = mlp_load(plan, w_in, w1, s1, ids)

    def emit(c0, v):
        nxt[:, c0 : c0 + 256] = v

    mlp_forward(
        0, per, pc, load, x_ref, o_ref, w1, vec_ref, f_ref, y_ref, n2_ref, h_ref, g_ref, emit
    )
    size = GROUP * CELLS
    for k, out in enumerate((xa, xb, xc, xd)):
        v = nxt[pl.ds(pl.multiple_of((ids[0] ^ k) * size, 8), size), :]
        out[:size, :] = v.astype(bf16)
        out[size:, :] = jnp.zeros((BLOCK - size, WIDE), bf16)


def mlp_fwd(per, pc, plan, ids, x, o, w, vec, f):
    act = sds((TOK, WIDE), bf16)
    wide = sds((TOK, HIDE), bf16)
    return call(
        functools.partial(mlp_fwd_kernel, per, pc, plan),
        (sds((TOK, WIDE), f32), act, wide, wide) + (sds((BLOCK, WIDE), bf16),) * 4,
        [SM, VM, VM] + [HB] * len(w) + [VM, VM],
        [pltpu.VMEM((TOK, WIDE), f32)] + plan.scratch(),
        2 * TOK * WIDE * (WIDE + 2 * HIDE),
        25 * 10**6,
        limit=40,
    )(ids, x, o, *w, vec, f)


def rows_sum(v):
    return jnp.sum(v, axis=0, keepdims=True)


def mlp_back(per, pc, plan, ids, dm_ref, wc, n2_ref, h_ref, g_ref, du, df_ref, dm_sum, outs, scratch):
    turned, g1, t1 = scratch
    shards = WIDE // per
    turned[...] = n2_ref[...].T
    grows = WIDE // pc

    def step(j):
        cols = pl.ds(pl.multiple_of(j * WIDE, WIDE), WIDE)
        w = wc[pl.ds(j * grows, grows)].reshape(WIDE, WIDE)
        dm = dm_ref[...]
        dh = dot_nt(dm, w)
        d = (dh * g_ref[:, cols].astype(f32)).astype(bf16)
        du[:, cols] = d
        total = rows_sum(d.astype(f32))
        for half in range(2):
            df_ref[2 * j + half] = total[:, half * 256 : half * 256 + 256]
        gc = dot_tn(h_ref[:, cols], dm)
        g1[pl.ds(j * grows, grows), 0:pc, :] = gc.astype(bf16).reshape(grows, pc, WIDE)
        ge = dot(turned[...], d)
        g1[:, pl.ds(pl.multiple_of(pc + j * per, 16), per), :] = ge.astype(bf16).reshape(
            shards, per, WIDE
        )

    loop(HIDE // WIDE, step)
    start_grads(plan, g1, outs, t1, ids)
    dm_sum[...] = rows_sum(dm_ref[...].astype(f32))
    return lambda: wait_all(g1, t1)


def mlp_back_scratch(gplan):
    return [pltpu.VMEM((WIDE, TOK), bf16)] + gplan.scratch()


def mlp_back_outs(gplan):
    outs = (
        sds((TOK, WIDE), bf16),
        sds((TOK, HIDE), bf16),
        sds((8, 1, 256), f32),
        sds((1, WIDE), f32),
    )
    return outs + grad_shapes(gplan)


def mlp_both_kernel(per, pc, plan, gplan, *refs):
    nw = plan.count
    ids, x_ref, o_ref = refs[:3]
    w_in, refs = refs[3 : 3 + nw], refs[3 + nw :]
    vec_ref, f_ref = refs[:2]
    cots, blocks, refs = refs[2:6], refs[6:10], refs[10:]
    do_ref, dy_ref, da_ref, gv_ref, df_ref, dm_sum = refs[:6]
    outs, refs = refs[6:8], refs[8:]
    y_ref, dm_ref, du, n2_ref, h_ref, g_ref, nxt, tmp, w1, s1 = refs[:10]
    scratch = refs[10:]
    load = mlp_load(plan, w_in, w1, s1, ids)

    def emit(c0, v):
        nxt[:, c0 : c0 + 256] = v

    mlp_forward(
        1, per, pc, load, x_ref, o_ref, w1, vec_ref, f_ref, y_ref, n2_ref, h_ref, g_ref, emit
    )
    s = ids[0]
    size = GROUP * CELLS
    for k, out in enumerate(blocks):
        for i in range(GROUP):
            row = pl.multiple_of((i * 4 + (s ^ k)) * CELLS, 8)
            tmp[i * CELLS : (i + 1) * CELLS, :] = nxt[pl.ds(row, CELLS), :]
        out[:size, :] = tmp[:size, :].astype(bf16)
        out[size:, :] = jnp.zeros((BLOCK - size, WIDE), bf16)
    for k, ref in enumerate(cots):
        v = ref[:size, :].astype(f32)
        for i in range(GROUP):
            row = pl.multiple_of((i * 4 + (s ^ k)) * CELLS, 8)
            nxt[pl.ds(row, CELLS), :] = v[i * CELLS : (i + 1) * CELLS, :]
    dm_ref[:ROWS, :] = nxt[:ROWS, :].astype(bf16)
    dm_ref[ROWS:, :] = jnp.zeros((TOK - ROWS, WIDE), bf16)
    wc = w1.at[:, per : per + pc, :]
    done = mlp_back(
        per, pc, gplan, ids, dm_ref, wc, n2_ref, h_ref, g_ref, du, df_ref, dm_sum, outs, scratch
    )
    mid_body(1, per, pc, w1, vec_ref, y_ref, dm_ref, du, do_ref, dy_ref, da_ref, gv_ref, nxt)
    done()


def mlp_both(per, pc, plan, gplan, ids, x, o, w, vec, f, cots):
    block = sds((BLOCK, WIDE), bf16)
    outs = (block,) * 4 + mid_outs() + mlp_back_outs(gplan)[2:]
    scratch = [
        pltpu.VMEM((TOK, WIDE), f32),
        pltpu.VMEM((TOK, WIDE), bf16),
        pltpu.VMEM((TOK, HIDE), bf16),
        pltpu.VMEM((TOK, WIDE), bf16),
        pltpu.VMEM((TOK, HIDE), bf16),
        pltpu.VMEM((TOK, HIDE), bf16),
        pltpu.VMEM((TOK, WIDE), f32),
        pltpu.VMEM((BLOCK, WIDE), f32),
    ]
    return call(
        functools.partial(mlp_both_kernel, per, pc, plan, gplan),
        outs,
        [SM, VM, VM] + [HB] * len(w) + [VM] * 6,
        scratch + plan.scratch() + mlp_back_scratch(gplan),
        5 * TOK * WIDE * (WIDE + 2 * HIDE),
        25 * 10**6,
        (VM,) * 10 + (HB,) * 2,
        50,
    )(ids, x, o, *w, vec, f, *cots)


def mlp_bwd_kernel(per, pc, plan, gplan, *refs):
    nw = plan.count
    ids, w_in, refs = refs[0], refs[1 : 1 + nw], refs[1 + nw :]
    n2_ref, h_ref, g_ref = refs[:3]
    grads, refs = refs[3:7], refs[7:]
    dm_ref, du, df_ref, dm_sum = refs[:4]
    outs, refs = refs[4:6], refs[6:]
    tmp, w1, s1 = refs[:3]
    scratch = refs[3:]
    start_load(plan, w_in, w1, s1, ids, ((per, per + pc),))
    s = ids[0]
    size = GROUP * CELLS
    for k, ref in enumerate(grads):
        tmp[pl.ds(pl.multiple_of((s ^ k) * size, 8), size), :] = ref[:size, :].astype(f32)
    dm_ref[:ROWS, :] = tmp[:ROWS, :].astype(bf16)
    dm_ref[ROWS:, :] = jnp.zeros((TOK - ROWS, WIDE), bf16)
    wc = w1.at[:, per : per + pc, :]
    wait_all(wc, s1)
    mlp_back(
        per, pc, gplan, ids, dm_ref, wc, n2_ref, h_ref, g_ref, du, df_ref, dm_sum, outs, scratch
    )()


def mlp_bwd(per, pc, plan, gplan, ids, w, n2, h, g, grads):
    return call(
        functools.partial(mlp_bwd_kernel, per, pc, plan, gplan),
        mlp_back_outs(gplan),
        [SM] + [HB] * len(w) + [VM] * 7,
        [pltpu.VMEM((TOK, WIDE), f32)] + plan.scratch() + mlp_back_scratch(gplan),
        3 * TOK * WIDE * 2 * HIDE,
        25 * 10**6,
        (VM,) * 4 + (HB,) * 2,
        limit=48,
    )(ids, *w, n2, h, g, *grads)


def mid_kernel(layer, per, pc, plan, *refs):
    nw = plan.count
    ids, w_in, refs = refs[0], refs[1 : 1 + nw], refs[1 + nw :]
    vec_ref, y_ref, dm_ref, du, do_ref, dy_ref, da_ref, gv_ref, dn2, w1, s1, s2 = refs
    spans = ((0, per), (per + pc, 5 * per + pc))
    start_load(plan, w_in, w1, s1, ids, spans[:1])
    start_load(plan, w_in, w1, s2, ids, spans[1:])
    for (lo, hi), sem in zip(spans, (s1, s2)):
        wait_all(w1.at[:, lo:hi, :], sem)
    mid_body(layer, per, pc, w1, vec_ref, y_ref, dm_ref, du, do_ref, dy_ref, da_ref, gv_ref, dn2)


def mid_outs():
    act = sds((TOK, WIDE), bf16)
    return (act, sds((TOK, WIDE), f32), act, sds((8, WIDE), f32))


def mid_body(layer, per, pc, w1, vec_ref, y_ref, dm_ref, du, do_ref, dy_ref, da_ref, gv_ref, dn2):
    gv_ref[...] = jnp.zeros_like(gv_ref)
    for half in range(2):
        total = None
        for c in range(4):
            w = gather_rows(w1, per + pc + c * per, per, half, 256, 0, WIDE)
            part = dot_nt(du[:, c * WIDE : (c + 1) * WIDE], w)
            total = part if total is None else total + part
        dn2[:, half * 256 : half * 256 + 256] = total
    gain = vec_ref[layer, 5:6, :]

    def norm(c):
        rows = pl.ds(pl.multiple_of(c * STRIP, STRIP), STRIP)
        cen, rstd = centred(y_ref[rows, :])
        xhat = cen * rstd
        dn = dn2[rows, :]
        gv_ref[5:6, :] += rows_sum(dn * xhat)
        gv_ref[6:7, :] += rows_sum(dn)
        dx = dn * gain
        m1 = jnp.mean(dx, axis=-1, keepdims=True)
        m2 = jnp.mean(dx * xhat, axis=-1, keepdims=True)
        dy = dm_ref[rows, :].astype(f32) + rstd * (dx - m1 - xhat * m2)
        dy_ref[rows, :] = dy
        da = dy.astype(bf16)
        gv_ref[4:5, :] += rows_sum(da.astype(f32))
        da_ref[rows, :] = da

    loop(NCH, norm)
    for half in range(2):
        c0 = half * 256
        w = gather_rows(w1, 0, per, half, 256, 0, WIDE)
        do_ref[:, c0 : c0 + 256] = dot_nt(da_ref[...], w).astype(bf16)


def mid_bwd(layer, per, pc, plan, ids, w, vec, y, dm, du):
    return call(
        functools.partial(mid_kernel, layer, per, pc, plan),
        mid_outs(),
        [SM] + [HB] * len(w) + [VM] * 4,
        [pltpu.VMEM((TOK, WIDE), f32)] + plan.scratch() + [pltpu.SemaphoreType.DMA],
        2 * TOK * WIDE * (WIDE + HIDE),
        16 * 10**6,
        limit=34,
    )(ids, *w, vec, y, dm, du)


def attn_bwd_kernel(layer, do_ref, qkv_ref, p_ref, dqkv, gv_ref, gt_ref, *rest):
    dsum = rest[0]
    if layer == 1:
        one, two = rest[1:]

        def widen(p):
            v = do_ref[pl.ds(pl.multiple_of(p * PAIR, 16), PAIR), :].astype(f32)
            one[pl.ds(p * 2 * WIN, 2 * WIN)] = v.reshape(2 * WIN, 8, WIDE)

        loop(NPAIR, widen)

        def emit(w, tile):
            two[pl.ds(w * WIN, WIN)] = tile

        swap_windows(one, emit)
    gv_ref[...] = jnp.zeros_like(gv_ref)
    dsum[...] = jnp.zeros_like(dsum)
    dqkv[ROWS:, :] = jnp.zeros((TOK - ROWS, 3 * WIDE), bf16)
    masks = head_masks()

    def pair(p):
        rows = pl.ds(pl.multiple_of(p * PAIR, 16), PAIR)
        def tile(t, part):
            c = part * WIDE + t * 128
            v = qkv_ref[rows, c : c + 128].astype(f32)
            return v[:CELLS], v[CELLS:]

        def grad(t):
            c = t * 128
            if layer == 0:
                d = do_ref[rows, c : c + 128].astype(f32)
            else:
                d = two[pl.ds(p * 2 * WIN, 2 * WIN), :, c : c + 128].reshape(PAIR, 128)
            return d[:CELLS], d[CELLS:]

        four = range(4)
        vs = [stacked(*tile(t, 2), masks) for t in four]
        dd = [diagonal(*grad(t)) for t in four]
        ks = [stacked(*tile(t, 1), masks) for t in four]
        qs = [diagonal(*tile(t, 0)) for t in four]
        pb = [p_ref[p, t * QT : (t + 1) * QT, :] for t in four]
        dp = [dot_nt(vs[t], dd[t]) for t in four]
        dv = [from_stacked(dot(pb[t], dd[t]), masks).astype(bf16) for t in four]
        ds = []
        for t in four:
            pf = pb[t].astype(f32).reshape(4, CELLS, 128)
            g = dp[t].reshape(4, CELLS, 128)
            tot = jnp.sum(g * pf, axis=1, keepdims=True)
            ds.append((pf * (g - tot)).reshape(QT, 128).astype(bf16))
        dq = [(scale * from_diagonal(dot_tn(ds[t], ks[t]))).astype(bf16) for t in four]
        dk = [(scale * from_stacked(dot(ds[t], qs[t]), masks)).astype(bf16) for t in four]
        for t in four:
            c = t * 128
            dsum[4 * t : 4 * t + 4] += ds[t].astype(f32).reshape(4, CELLS, 128)
            dqkv[rows, c : c + 128] = dq[t]
            dqkv[rows, WIDE + c : WIDE + c + 128] = dk[t]
            dqkv[rows, 2 * WIDE + c : 2 * WIDE + c + 128] = dv[t]
            gv_ref[2:3, c : c + 128] += rows_sum(dq[t].astype(f32))
            gv_ref[3:4, c : c + 128] += rows_sum(dv[t].astype(f32))

    loop(NPAIR, pair)
    total = jnp.zeros((HEADS, 256), f32)
    for rb in range(WIN):
        x = jnp.concatenate([dsum[:, rb * 8 + cb, :] for cb in range(8)], axis=1)
        hi = x.astype(bf16)
        lo = (x - hi.astype(f32)).astype(bf16)
        oh = onehot(rb, layer == 1)
        total = total + (dot_nt(hi, oh) + dot_nt(lo, oh))
    gt_ref[...] = total


def attn_bwd(layer, do, qkv, probs):
    tile = pltpu.VMEM((NWIN * WIN, 8, WIDE), f32)
    return call(
        functools.partial(attn_bwd_kernel, layer),
        (sds((TOK, 3 * WIDE), bf16), sds((8, WIDE), f32), sds((HEADS, 256), f32)),
        [VM] * 3,
        [pltpu.VMEM((HEADS, CELLS, 128), f32)] + [tile, tile] * layer,
        2 * TOK * WIDE * 3 * WIDE,
        12 * 10**6,
        limit=28,
    )(do, qkv, probs)


def qkv_grad_kernel(per, plan, ids, n1_ref, dqkv, o_ref, da_ref, keep, send, turned, gq, sem):
    shards = WIDE // per
    turned[...] = o_ref[...].T
    for half in range(2):
        c0 = half * 256
        g = dot(turned[...], da_ref[:, c0 : c0 + 256])
        gq[:, 3 * per : 4 * per, c0 : c0 + 256] = g.astype(bf16).reshape(shards, per, 256)
    turned[...] = n1_ref[...].T
    for j in range(3):
        for half in range(2):
            c0 = half * 256
            g = dot(turned[...], dqkv[:, j * WIDE + c0 : j * WIDE + c0 + 256])
            gq[:, j * per : (j + 1) * per, c0 : c0 + 256] = g.astype(bf16).reshape(
                shards, per, 256
            )
    start_grads(plan, gq, (keep, send), sem, ids)
    wait_all(gq, sem)


def qkv_grad(per, plan, ids, n1, dqkv, o, da):
    return call(
        functools.partial(qkv_grad_kernel, per, plan),
        grad_shapes(plan),
        [SM, VM, VM, VM, VM],
        [pltpu.VMEM((WIDE, TOK), bf16)] + plan.scratch(),
        2 * TOK * WIDE * 4 * WIDE,
        9 * 10**6,
        (HB, HB),
        limit=24,
    )(ids, n1, dqkv, o, da)


def dx_kernel(layer, per, plan, *refs):
    nw = plan.count
    ids, dqkv, dy_ref, x_ref = refs[:4]
    w_in, vec_ref, refs = refs[4 : 4 + nw], refs[4 + nw], refs[5 + nw :]
    nout = 1 if layer == 0 else 4
    dx_refs, gv_ref, refs = refs[:nout], refs[nout], refs[nout + 1 :]
    dn, one, w_ref, sem = refs
    start_load(plan, w_in, w_ref, sem, ids)
    gv_ref[...] = jnp.zeros_like(gv_ref)
    wait_all(w_ref, sem)
    for half in range(2):
        total = None
        for c in range(3):
            w = gather_rows(w_ref, c * per, per, half, 256, 0, WIDE)
            part = dot_nt(dqkv[:, c * WIDE : (c + 1) * WIDE], w)
            total = part if total is None else total + part
        dn[:, half * 256 : half * 256 + 256] = total
    gain = vec_ref[layer, 0:1, :]
    if layer == 1:

        def widen_dn(p):
            v = dn[pl.ds(pl.multiple_of(p * PAIR, 8), PAIR), :].astype(bf16).astype(f32)
            one[pl.ds(p * 2 * WIN, 2 * WIN)] = v.reshape(2 * WIN, 8, WIDE)

        loop(NPAIR, widen_dn)

        def emit_dn(w, tile):
            dn[pl.ds(pl.multiple_of(w * CELLS, 8), CELLS), :] = tile.reshape(CELLS, WIDE)

        swap_windows(one, emit_dn)

    def norm(p):
        rows = pl.ds(pl.multiple_of(p * FOUR, 16), FOUR)
        cen, rstd = centred(x_ref[rows, :].astype(f32))
        xhat = cen * rstd
        d = dn[rows, :]
        gv_ref[0:1, :] += rows_sum(d * xhat)
        gv_ref[1:2, :] += rows_sum(d)
        dx = d * gain
        m1 = jnp.mean(dx, axis=-1, keepdims=True)
        m2 = jnp.mean(dx * xhat, axis=-1, keepdims=True)
        out = dy_ref[rows, :] + rstd * (dx - m1 - xhat * m2)
        one[pl.ds(p * QUADS, QUADS)] = out.reshape(QUADS, 8, WIDE)

    loop(GROUP, norm)
    if layer == 0:
        put_dense(dx_refs[0], one)
    else:
        s = ids[0]
        size = GROUP * CELLS
        for k, out in enumerate(dx_refs):
            for i in range(GROUP):
                tile = one[pl.ds((i * 4 + (s ^ k)) * WIN, WIN)]
                dn[i * CELLS : (i + 1) * CELLS, :] = tile.reshape(CELLS, WIDE)
            out[:size, :] = dn[:size, :].astype(bf16)
            out[size:, :] = jnp.zeros((BLOCK - size, WIDE), bf16)


def dx_step(layer, per, plan, ids, dqkv, dy, x, w, vec):
    if layer == 0:
        outs = (sds((NWIN * WIN * WIN * 4, QUAD), f32),)
    else:
        outs = (sds((BLOCK, WIDE), bf16),) * 4
    tile = pltpu.VMEM((NWIN * WIN, 8, WIDE), f32)
    return call(
        functools.partial(dx_kernel, layer, per, plan),
        outs + (sds((8, WIDE), f32),),
        [SM, VM, VM, VM] + [HB] * plan.count + [VM],
        [pltpu.VMEM((TOK, WIDE), f32), tile] + plan.scratch(),
        2 * TOK * WIDE * 3 * WIDE,
        12 * 10**6,
        limit=28,
    )(ids, dqkv, dy, x, *w, vec)


def join_kernel(ids, xa, xb, xc, xd, out_ref, pad):
    s = ids[0]
    size = GROUP * CELLS
    for k, ref in enumerate((xa, xb, xc, xd)):
        v = ref[:size, :].astype(f32).reshape(GROUP * WIN, 8, WIDE)
        pad[pl.ds((s ^ k) * GROUP * WIN, GROUP * WIN)] = v
    put_dense(out_ref, pad)


def join_blocks(ids, blocks):
    return call(
        join_kernel,
        (sds((NWIN * WIN * WIN * 4, QUAD), f32),),
        [SM] + [VM] * 4,
        [pltpu.VMEM((NWIN * WIN, 8, WIDE), f32)],
        10**6,
        5 * 10**6,
        limit=16,
    )(ids, *blocks)[0]


def hop(value, way):
    axes = {"c": ("core",), "cy": ("y", "core"), "xy": ("y", "x")}.get(way, (way[0],))
    mask = {"z2": 2, "z3": 3, "cy": 3, "xy": 3}.get(way, 1)
    size = math.prod(lax.axis_size(a) for a in axes)
    return lax.ppermute(value, axes, [(i, i ^ mask) for i in range(size)])


def tie(*values):
    return lax.optimization_barrier(values)


def exchange(blocks):
    return [blocks[0]] + [hop(b, way) for b, way in zip(blocks[1:], ("c", "y", "cy"))]


def swap_all(value, axes):
    return lax.all_to_all(value, axes, 0, 0)


def share(value, axes):
    n = math.prod(lax.axis_size(a) for a in axes)
    return swap_all(jnp.stack([value] * n), axes)


def gather_c(gs):
    return gs + [hop(g, "c") for g in gs]


def add16(*terms):
    total = terms[0].astype(f32)
    for t in terms[1:]:
        total = total + t.astype(f32)
    return total.astype(bf16)


def near_xy(keep, r):
    own, *others = [add16(keep[k], r[k]) for k in range(4)]
    return own, [hop(t, way) for t, way in zip(others, ("x", "y", "xy"))]


def near_z(own, got):
    own, *others = [add16(own[k], *[g[k] for g in got]) for k in range(4)]
    return own, [hop(t, way) for t, way in zip(others, ("z1", "z2", "z3"))]


def near_spread(own, got):
    f = add16(own, *got)
    return [f, hop(f, "y"), hop(f, "c"), hop(f, "cy")]


def step_core(grads, r):
    keep = grads[0]
    return add16(keep[0], r[0]), hop(add16(keep[1], r[1]), "x")


def step_next(own, r, way):
    return add16(own[0], r[0]), hop(add16(own[1], r[1]), way)


def step_last(own, r):
    f = add16(own, r)
    return f, hop(f, "y")


def step_spread(f, r):
    f = add16(f, r)
    return [f, hop(f, "c")]


def half_reduce(grads, shard):
    total = add16(grads[0], hop(grads[1], "c"))
    total = total.reshape((-1,) + total.shape[2:])
    f = lax.psum_scatter(total, ("y",) + shard, scatter_dimension=0, tiled=False)
    return [f, hop(f, "y"), hop(f, "c"), hop(f, "cy")]


def adam_math(weight, moment_one, moment_two, gradient, step_rate, decay_rate):
    first_new = beta_one * moment_one + (1.0 - beta_one) * gradient
    second_new = beta_two * moment_two + (1.0 - beta_two) * gradient * gradient
    correct_one = 1.0 - beta_one**ADAM_STEP
    correct_two = 1.0 - beta_two**ADAM_STEP
    update = first_new / correct_one / (jnp.sqrt(second_new / correct_two) + adam_eps)
    weight_new = weight * (1.0 - step_rate * decay_rate) - step_rate * update
    return (first_new, second_new, weight_new)


def adam_kernel(segments, members, old, count, ids, *refs):
    n = len(members)
    blocks, refs = refs[:count], refs[count:]
    ins, outs, tot = refs[: 3 * n], refs[3 * n + old : 6 * n + old], refs[-1]
    c, y, x, z = place(ids)
    for k, ref in enumerate(blocks):
        if count == 2:
            lane = pl.multiple_of((c ^ k) * HALF, HALF)
        else:
            lane = pl.multiple_of((c ^ (k >> 1)) * HALF + (y ^ (k & 1)) * QUAD, QUAD)
        tot[:, pl.ds(lane, WIDE // count)] = ref[...].astype(f32)
    for row, m, count, col in segments:
        at = (0, slice(0, count), slice(col, col + WIDE))
        pos = members[m]
        new = adam_math(
            ins[3 * m][at],
            ins[3 * m + 1][at],
            ins[3 * m + 2][at],
            tot[row : row + count, :],
            step_rates[pos],
            decay_rates[pos],
        )
        for k in range(3):
            outs[3 * m + k][at] = new[k]


def adam_step(layer, segments, members, ids, blocks, params, old):
    ins = [a for pos in members for a in (params[0][pos], params[1][pos], params[2][pos])]
    rows = blocks[0].shape[0]

    def spec(a):
        return pl.BlockSpec((1,) + a.shape[1:], lambda i: (layer, 0, 0))

    outs = tuple(sds(a.shape, f32) for a in ins)
    held = list(old or [])
    base = 1 + len(blocks) + len(ins)
    return pl.pallas_call(
        functools.partial(adam_kernel, segments, members, len(held), len(blocks)),
        grid=(1,),
        out_shape=outs,
        in_specs=[SM]
        + [pl.BlockSpec(b.shape, lambda i: (0, 0)) for b in blocks]
        + [spec(a) for a in ins]
        + [HB] * len(held),
        out_specs=tuple(spec(a) for a in ins),
        scratch_shapes=[pltpu.VMEM((rows, WIDE), f32)],
        input_output_aliases={base + k: k for k in range(len(held))},
        compiler_params=pltpu.CompilerParams(vmem_limit_bytes=58 * MIB),
        cost_estimate=pl.CostEstimate(
            flops=20 * rows * WIDE, bytes_accessed=24 * rows * WIDE, transcendentals=0
        ),
    )(ids, *blocks, *ins, *held)


def body(shard, *args):
    inputs, cotangent, image_valid = args[:3]
    masters, firsts, seconds = args[3:9], args[9:15], args[15:21]
    params = (masters, firsts, seconds)
    per = masters[0].shape[1]
    pc = masters[3].shape[1]
    own = masters[5].shape[0]
    shards = WIDE // per
    fast = len(shard) == 2
    seq = lax.axis_index(("y", "core")).astype(jnp.int32)
    me = lax.axis_index(shard).astype(jnp.int32)
    ids = jnp.stack([seq, me])

    nq, nm = 3 * per, 5 * per + pc
    whole = ((0, nq + nm, HALF),)
    wide = "wide" if fast else "half"
    pq0 = Plan(wide, shards, nq)
    pm0 = Plan("near" if fast else "half", shards, nm, 0 if fast else nq)
    part = "part" if fast else "half"
    pq1, pm1 = Plan(part, shards, nq), Plan(part, shards, nm, nq)
    gqp, gmp = Plan(wide, shards, 4 * per), Plan(wide, shards, 4 * per + pc)
    gmp0 = Plan("near" if fast else "half", shards, 4 * per + pc)
    x_in = inputs.reshape(NWIN * WIN, WIN, WIDE)
    cot = cotangent.reshape(NWIN * WIN * WIN * 4, QUAD)
    seg_q = [(j * per, 0, per, j * WIDE) for j in range(3)] + [(3 * per, 1, per, 0)]
    seg_m = [(0, 1, pc, 0)] + [(pc + j * per, 0, per, j * WIDE) for j in range(4)]

    def adam_q(layer, blocks, old=None):
        return adam_step(layer, seg_q, (0, 1), ids, blocks, params, old)

    def adam_m(layer, blocks, old=None):
        return adam_step(layer, seg_m, (2, 3), ids, blocks, params, old)

    def all_smalls(parts):
        rows = []
        for gvm, dms, df, gva, gvx, gt in parts:
            total = gvm + gva + gvx
            rows += [total[:7], dms, df.reshape(4, WIDE), gt.reshape(8, WIDE)]
        return jnp.concatenate(rows, axis=0).astype(bf16)

    if fast:
        em0, eq0 = pack(0, per, pc, ((nq, nq + nm, QUAD), (0, nq, HALF)), "row", ids, masters)
        zq = [hop(eq0, "z1"), hop(eq0, "z2")]
        zm = [hop(em0, "z1"), hop(em0, "z2")]
        x0, *cots = prep(ids, image_valid, x_in, cot)
        zq, zm, x0 = tie(zq, zm, x0)
        zq.append(hop(zq[1], "z1"))
        zm.append(hop(zm[1], "z1"))
        (e1,) = pack(1, per, pc, whole, "", ids, masters)
        zq, zm, e1 = tie(zq, zm, e1)
        g = jnp.stack([eq0] + zq)
        gx = hop(g, "x")
        gm = jnp.stack([em0] + zm)
        wm0 = [gm] + [hop(gm, way) for way in ("x", "y", "xy")]
        z1, z2 = hop(e1, "z1"), hop(e1, "z2")
        vec, hide, bias0, bias1 = expand_smalls(per, own, False, ids, [g, gx])
        wq0 = gather_c([g, gx])
        n1a, qkva, pa, oa = attn_fwd(0, per, pq0, ids, [x0], wq0, vec, bias0)
        oa, z1, z2, wm0 = tie(oa, z1, z2, wm0)
        z3 = hop(z2, "z1")
        gaq = jnp.stack([v[:nq] for v in (e1, z1, z2)])
        gam = jnp.stack([v[nq:] for v in (e1, z1, z2)])
        gaqx = hop(gaq, "x")
        wm0 = gather_c(wm0)
        wm0, gaq, gam = tie(wm0, gaq, gam)
        gamx = hop(gam, "x")
        gaqc, gamc = hop(gaq, "c"), hop(gam, "c")
        ya, n2a, ha, ga, *x1s = mlp_fwd(per, pc, pm0, ids, x0, oa, wm0, vec, hide)
        x1s, z3, gaqx, gaqc, gamc = tie(x1s, z3, gaqx, gaqc, gamc)
        x1s = exchange(x1s)
        z3x = hop(z3, "x")
        z3c, gaqxc = hop(z3, "c"), hop(gaqx, "c")
        x1s, z3x, z3c, gaqxc = tie(x1s, z3x, z3c, gaqxc)
        z3xc = hop(z3x, "c")
        w1q = [gaq, z3, gaqx, z3x, gaqc, z3c, gaqxc, z3xc]
        cots = exchange(cots)
        x1, n1b, qkvb, pb, ob = attn_fwd(1, per, pq1, ids, x1s, w1q, vec, bias1)
        ob, cots, gamx = tie(ob, cots, gamx)
        w1 = [gam, z3, gamx, z3x, gamc, z3c, hop(gamx, "c"), z3xc]
        res = mlp_both(per, pc, pm1, gmp, ids, x1, ob, w1, vec, hide, cots)
        outs, (dob, dyb, dab, gvm1, df1, dms1), gm1 = res[:4], res[4:10], res[10:12]
        rm1 = hop(gm1[1], "c")
        outs = exchange(outs)
        dqkvb, gva1, gt1 = attn_bwd(1, dob, qkvb, pb)
        dqkvb, rm1, outs = tie(dqkvb, rm1, outs)
        sm1 = step_core(gm1, rm1)
        *dx1s, gvx1 = dx_step(1, per, pq1, ids, dqkvb, dyb, x1, w1q, vec)
        dx1s, dqkvb = tie(dx1s, dqkvb)
        dx1s = exchange(dx1s)
        gq1 = qkv_grad(per, gqp, ids, n1b, dqkvb, ob, dab)
        gq1, dx1s, sm1 = tie(gq1, dx1s, sm1)
        rq1 = hop(gq1[1], "c")
        sm1 = step_next(*sm1, "z1")
        dma, dua, df0, dms0, *gm0 = mlp_bwd(per, pc, pm0, gmp0, ids, wm0, n2a, ha, ga, dx1s)
        dua, rq1, sm1, gm0 = tie(dua, rq1, sm1, gm0)
        rm0 = hop(gm0[1], "c")
        sq1 = step_core(gq1, rq1)
        sm1 = step_next(*sm1, "z2")
        doa, dya, daa, gvm0 = mid_bwd(0, per, pc, pm0, ids, wm0, vec, ya, dma, dua)
        doa, rm0, sq1, sm1 = tie(doa, rm0, sq1, sm1)
        sm0 = near_xy(gm0[0], rm0)
        sq1 = step_next(*sq1, "z1")
        sm1 = step_last(*sm1)
        dqkva, gva0, gt0 = attn_bwd(0, doa, qkva, pa)
        dqkva, sq1, sm1 = tie(dqkva, sq1, sm1)
        sq1 = step_next(*sq1, "z2")
        fm1 = step_spread(*sm1)
        gq0 = qkv_grad(per, gqp, ids, n1a, dqkva, oa, daa)
        gq0, sm0, sq1, fm1, outs = tie(gq0, sm0, sq1, fm1, outs)
        rq0 = hop(gq0[1], "c")
        sm0 = near_z(*sm0)
        output = join_blocks(ids, outs)
        output, rq0 = tie(output, rq0)
        sq0 = step_core(gq0, rq0)
        sq1 = step_last(*sq1)
        dx0, gvx0 = dx_step(0, per, pq0, ids, dqkva, dya, x0, wq0, vec)
        dx0, gvx0, sq0, sm0, sq1 = tie(dx0, gvx0, sq0, sm0, sq1)
        sq0 = step_next(*sq0, "z1")
        fm0 = near_spread(*sm0)
        smalls = all_smalls(
            ((gvm0, dms0, df0, gva0, gvx0, gt0), (gvm1, dms1, df1, gva1, gvx1, gt1))
        )
        fq1 = step_spread(*sq1)
        sc = hop(smalls, "c")
        new_m = adam_m(1, fm1)
        new_m, sq0, sc, fq1 = tie(new_m, sq0, sc, fq1)
        sq0 = step_next(*sq0, "z2")
        smalls = add16(smalls, sc)
        sc = hop(smalls, "x")
        new_q = adam_q(1, fq1)
        new_q, sq0, fm0, sc = tie(new_q, sq0, fm0, sc)
        sq0 = step_last(*sq0)
        smalls = add16(smalls, sc)
        sc = hop(smalls, "z1")
        new_m = adam_m(0, fm0, new_m)
        new_m, sq0, sc = tie(new_m, sq0, sc)
        fq0 = step_spread(*sq0)
        smalls = add16(smalls, sc)
        sc = hop(smalls, "z2")
        fq0, sc = tie(fq0, sc)
        smalls = add16(smalls, sc)
        sc = hop(smalls, "y")
        new_q = adam_q(0, fq0, new_q)
        new_q, sc = tie(new_q, sc)
        smalls = add16(smalls, sc)
    else:
        half0, small = pack(0, per, pc, whole, "own", ids, masters)
        (e1,) = pack(1, per, pc, whole, "", ids, masters)
        x0, *cots = prep(ids, image_valid, x_in, cot)
        cots = exchange(cots)
        small = lax.all_gather(small, shard, axis=0, tiled=False)
        vec, hide, bias0, bias1 = expand_smalls(per, own, True, ids, [small])
        own0 = lax.all_gather(half0, shard, axis=0, tiled=False)
        own1 = lax.all_gather(e1, shard, axis=0, tiled=False)
        w0 = [own0, hop(own0, "c")]
        w1 = [own1, hop(own1, "c")]
        n1a, qkva, pa, oa = attn_fwd(0, per, pq0, ids, [x0], w0, vec, bias0)
        ya, n2a, ha, ga, *x1s = mlp_fwd(per, pc, pm0, ids, x0, oa, w0, vec, hide)
        x1s = exchange(x1s)
        x1, n1b, qkvb, pb, ob = attn_fwd(1, per, pq1, ids, x1s, w1, vec, bias1)
        res = mlp_both(per, pc, pm1, gmp, ids, x1, ob, w1, vec, hide, cots)
        outs, (dob, dyb, dab, gvm1, df1, dms1), gm1 = res[:4], res[4:10], res[10:12]
        output = join_blocks(ids, exchange(outs))
        dqkvb, gva1, gt1 = attn_bwd(1, dob, qkvb, pb)
        *dx1s, gvx1 = dx_step(1, per, pq1, ids, dqkvb, dyb, x1, w1, vec)
        dx1s = exchange(dx1s)
        gq1 = qkv_grad(per, gqp, ids, n1b, dqkvb, ob, dab)
        dma, dua, df0, dms0, *gm0 = mlp_bwd(per, pc, pm0, gmp0, ids, w0, n2a, ha, ga, dx1s)
        doa, dya, daa, gvm0 = mid_bwd(0, per, pc, pm0, ids, w0, vec, ya, dma, dua)
        dqkva, gva0, gt0 = attn_bwd(0, doa, qkva, pa)
        gq0 = qkv_grad(per, gqp, ids, n1a, dqkva, oa, daa)
        dx0, gvx0 = dx_step(0, per, pq0, ids, dqkva, dya, x0, w0, vec)
        smalls = all_smalls(
            ((gvm0, dms0, df0, gva0, gvx0, gt0), (gvm1, dms1, df1, gva1, gvx1, gt1))
        )
        smalls = lax.psum(smalls, ("y", "core") + shard)
        fq1, fm1, fq0, fm0 = [half_reduce(g, shard) for g in (gq1, gm1, gq0, gm0)]
        new_m = adam_m(0, fm0, adam_m(1, fm1))
        new_q = adam_q(0, fq0, adam_q(1, fq1))

    smalls = smalls.astype(f32).reshape(2, 20, WIDE)
    g_vec = lax.dynamic_slice_in_dim(smalls[:, :12], me * per, per, axis=2)
    g_tab = smalls[:, 12:20].reshape(2 * HEADS, 256)
    g_tab = lax.dynamic_slice_in_dim(g_tab, me * own, own, axis=0)[:, :SPAN]
    flat = [*new_q, *new_m]
    for pos, g in ((4, g_vec), (5, g_tab)):
        flat += adam_math(
            masters[pos], firsts[pos], seconds[pos], g, step_rates[pos], decay_rates[pos]
        )
    return (output.reshape(inputs.shape), dx0.reshape(inputs.shape), *flat, g_vec[:, 7])


def solution(mesh):
    count = mesh.shape["shard"]
    if count == 8:
        mesh = Mesh(mesh.devices.reshape(2, 2, 4, 2), ("y", "core", "z", "x"))
        shard = ("z", "x")
    else:
        mesh = Mesh(mesh.devices.reshape(2, 2, count), ("y", "core", "s"))
        shard = ("s",)
    tokens = P(shard, ("y", "core"), None, None, None)
    params = (P(None, shard, None),) * 4 + (P(None, None, shard), P(shard, None))
    in_specs = (tokens, tokens, P(shard)) + params * 3
    out_specs = (tokens, tokens)
    for spec in params:
        out_specs = out_specs + (spec,) * 3
    out_specs = out_specs + (P(None, shard),)
    return jax.shard_map(
        functools.partial(body, shard),
        mesh=mesh,
        in_specs=in_specs,
        out_specs=out_specs,
        check_vma=False,
    )
```

```python
import functools
import math

import jax
import jax.numpy as jnp
from jax import lax
from jax.experimental import pallas as pl
from jax.experimental.pallas import tpu as pltpu
from jax.sharding import Mesh
from jax.sharding import PartitionSpec as P

HEADS = 16
WIN = 7
SHIFT = 3
ADAM_STEP = 10
WIDE = 512
HIDE = 2048
HEAD_DIM = 32
SPAN = 169
CELLS = 56
SEQ = 4
NWIN = 20
ROWS = NWIN * CELLS
TOK = 1152
GROUP = NWIN // SEQ
BLOCK = 288
PAIR = 2 * CELLS
NPAIR = NWIN // 2
STRIP = 384
NCH = TOK // STRIP
QUADS = 4 * WIN
FOUR = 4 * CELLS
QT = 4 * CELLS
SMALL = 32
HALF = 256
QUAD = 128

bf16 = jnp.bfloat16
f32 = jnp.float32
norm_eps = 1e-05
mask_fill = -100.0
pad_fill = -1e30
beta_one = 0.9
beta_two = 0.999
adam_eps = 1e-08
step_rates = (0.09, 0.35, 0.09, 0.045, 0.5, 2.0)
decay_rates = (0.05, 0.05, 0.05, 0.05, 0.0, 0.0)
scale = HEAD_DIM ** (-0.5)

VM = pl.BlockSpec(memory_space=pltpu.VMEM)
SM = pl.BlockSpec(memory_space=pltpu.SMEM)
HB = pl.BlockSpec(memory_space=pltpu.HBM)
MIB = 1024 * 1024


def call(kernel, outs, in_specs, scratch, flops, moved, out_specs=None, limit=58):
    return pl.pallas_call(
        kernel,
        out_shape=outs,
        in_specs=in_specs,
        out_specs=out_specs or tuple(VM for _ in outs),
        scratch_shapes=scratch,
        compiler_params=pltpu.CompilerParams(vmem_limit_bytes=limit * MIB),
        cost_estimate=pl.CostEstimate(flops=flops, bytes_accessed=moved, transcendentals=0),
    )


def sds(shape, dtype):
    return jax.ShapeDtypeStruct(shape, dtype)


def dot(a, b):
    return lax.dot_general(a, b, (((1,), (0,)), ((), ())), preferred_element_type=f32)


def dot_nt(a, b):
    return lax.dot_general(a, b, (((1,), (1,)), ((), ())), preferred_element_type=f32)


def dot_tn(a, b):
    return lax.dot_general(a, b, (((0,), (0,)), ((), ())), preferred_element_type=f32)


def loop(count, body):
    lax.fori_loop(0, count, lambda i, c: (body(i), c)[1], 0)


def centred(x):
    mean = jnp.mean(x, axis=-1, keepdims=True)
    cen = x - mean
    var = jnp.mean(cen * cen, axis=-1, keepdims=True)
    return cen, lax.rsqrt(var + norm_eps)


def gelu_pair(u):
    phi = 0.5 + 0.5 * lax.erf(u * math.sqrt(0.5))
    e = jnp.exp2((u * u) * (-0.5 / math.log(2.0)))
    return u * phi, phi + (u * (1.0 / math.sqrt(2.0 * math.pi))) * e


def head_masks():
    lane = lax.broadcasted_iota(jnp.int32, (1, 128), 1)
    return [(lane >> 5) == h for h in range(4)]


def stacked(t0, t1, masks):
    left = jnp.concatenate([jnp.where(m, t0, 0.0) for m in masks], axis=0)
    right = jnp.concatenate([jnp.where(m, t1, 0.0) for m in masks], axis=0)
    return jnp.concatenate([left, right], axis=1).astype(bf16)


def diagonal(t0, t1):
    z8 = jnp.zeros((64 - CELLS, 128), f32)
    z64 = jnp.zeros((64, 128), f32)
    left = jnp.concatenate([t0, z8, z64], axis=0)
    right = jnp.concatenate([z64, t1, z8], axis=0)
    return jnp.concatenate([left, right], axis=1).astype(bf16)


def from_diagonal(o):
    return jnp.concatenate([o[:CELLS, :128], o[64 : 64 + CELLS, 128:]], axis=0)


def from_stacked(o, masks):
    total = None
    for h, m in enumerate(masks):
        part = o[h * CELLS : (h + 1) * CELLS]
        part = jnp.concatenate(
            [jnp.where(m, part[:, :128], 0.0), jnp.where(m, part[:, 128:], 0.0)], axis=1
        )
        total = part if total is None else total + part
    return jnp.concatenate([total[:, :128], total[:, 128:]], axis=0)


def swap_windows(src, emit):
    col = lax.broadcasted_iota(jnp.int32, (1, 8, 1), 1)
    first = col < SHIFT

    def image(i):
        tiles = [src[pl.ds((i * 4 + w) * WIN, WIN)] for w in range(4)]
        for r in range(2):
            rows = [
                jnp.concatenate([tiles[(1 - r) * 2 + c][:SHIFT], tiles[r * 2 + c][SHIFT:]], axis=0)
                for c in range(2)
            ]
            for c in range(2):
                emit(i * 4 + r * 2 + c, jnp.where(first, rows[1 - c], rows[c]))

    loop(GROUP, image)


def swap_into(src, dst, keep):
    def emit(w, tile):
        keep[pl.ds(w * WIN, WIN)] = tile

    swap_windows(src, emit)

    def copy(p):
        v = keep[pl.ds(p * 2 * WIN, 2 * WIN)].reshape(PAIR, WIDE)
        dst[pl.ds(pl.multiple_of(p * PAIR, 16), PAIR), :] = v.astype(bf16)

    loop(NPAIR, copy)


def gather_rows(ref, off, per, first, count, c0, width):
    n = count // per
    v = ref[pl.ds(first * n, n), off : off + per, pl.ds(c0, width)]
    return v.reshape(count, width)


class Plan:
    def __init__(self, kind, shards, rows, row0=0):
        self.kind = kind
        self.shards = shards
        self.rows = rows
        self.row0 = row0

    @property
    def count(self):
        return {"near": 8, "wide": 4, "part": 8, "half": 2}[self.kind]

    def scratch(self):
        return [pltpu.VMEM((self.shards, self.rows, WIDE), bf16), pltpu.SemaphoreType.DMA]


def place(ids):
    s, m = ids[0], ids[1]
    return s & 1, s >> 1, m & 1, m >> 1


def start_load(plan, refs, dst, sem, ids, spans=None):
    c, y, x, z = place(ids)
    for lo, hi in spans or ((0, plan.rows),):
        for kc in range(2):
            if plan.kind == "half":
                lane = pl.multiple_of((c ^ kc) * HALF, HALF)
                pltpu.make_async_copy(
                    refs[kc].at[:, plan.row0 + lo : plan.row0 + hi, :],
                    dst.at[:, lo:hi, pl.ds(lane, HALF)],
                    sem,
                ).start()
                continue
            if plan.kind in ("wide", "part"):
                lane = pl.multiple_of((c ^ kc) * HALF, HALF)
                for k in range(8):
                    owner = (z ^ (k & 3)) * 2 + (x ^ (k >> 2))
                    row = 0
                    if plan.kind == "wide":
                        src = refs[kc * 2 + (k >> 2)].at[k & 3]
                    elif k & 3 == 3:
                        src = refs[kc * 4 + (k >> 2) * 2 + 1]
                        row = plan.row0
                    else:
                        src = refs[kc * 4 + (k >> 2) * 2].at[k & 3]
                    pltpu.make_async_copy(
                        src.at[row + lo : row + hi],
                        dst.at[owner, lo:hi, pl.ds(lane, HALF)],
                        sem,
                    ).start()
                continue
            for k in range(16):
                kxy, kz = k >> 2, k & 3
                owner = (z ^ kz) * 2 + (x ^ (kxy & 1))
                lane = pl.multiple_of((c ^ kc) * HALF + (y ^ (kxy >> 1)) * QUAD, QUAD)
                src = refs[kc * 4 + kxy].at[kz, lo:hi]
                pltpu.make_async_copy(src, dst.at[owner, lo:hi, pl.ds(lane, QUAD)], sem).start()


def wait_all(ref, sem):
    pltpu.make_async_copy(ref, ref, sem).wait()


def grad_shapes(plan):
    if plan.kind == "near":
        shape = (4, 4, plan.rows, QUAD)
    elif plan.kind == "wide":
        shape = (2, 2, 2, plan.rows, HALF)
    else:
        shape = (2, plan.shards, plan.rows, QUAD)
    return (sds(shape, bf16), sds(shape, bf16))


def start_grads(plan, src, outs, sem, ids):
    c, y, x, z = place(ids)
    for kc in range(2):
        if plan.kind == "near":
            for k in range(16):
                kxy, kz = k >> 2, k & 3
                owner = (z ^ kz) * 2 + (x ^ (kxy & 1))
                lane = pl.multiple_of((c ^ kc) * HALF + (y ^ (kxy >> 1)) * QUAD, QUAD)
                pltpu.make_async_copy(
                    src.at[owner, :, pl.ds(lane, QUAD)], outs[kc].at[kxy, kz], sem
                ).start()
        elif plan.kind == "wide":
            lane = pl.multiple_of((c ^ kc) * HALF, HALF)
            for k in range(8):
                owner = (z ^ (k & 3)) * 2 + (x ^ (k >> 2))
                pltpu.make_async_copy(
                    src.at[owner, :, pl.ds(lane, HALF)],
                    outs[kc].at[k >> 2, k & 1, (k >> 1) & 1],
                    sem,
                ).start()
        else:
            for part in range(2):
                lane = pl.multiple_of((c ^ kc) * HALF + part * QUAD, QUAD)
                pltpu.make_async_copy(
                    src.at[:, :, pl.ds(lane, QUAD)], outs[kc].at[part], sem
                ).start()


def put_dense(dst, pad):
    def group(i):
        for q in range(4):
            tile = pad[i, :WIN, q * QUAD : (q + 1) * QUAD]
            dst[pl.ds(4 * WIN * i + q, WIN, stride=4), :] = tile

    loop(NWIN * WIN, group)


def prep_kernel(ids, valid_ref, x_ref, cot_ref, x_out, c0, c1, c2, c3, pad):
    s = ids[0]
    pad[...] = jnp.zeros_like(pad)
    x_out[ROWS:, :] = jnp.zeros((TOK - ROWS, WIDE), bf16)

    def xrow(i):
        pad[pl.ds(i * WIN, WIN), :WIN, :] = x_ref[pl.ds(i * WIN, WIN)].astype(f32)

    loop(NWIN, xrow)

    def xpair(i):
        v = pad[pl.ds(i * 2 * WIN, 2 * WIN)].reshape(PAIR, WIDE)
        x_out[pl.ds(pl.multiple_of(i * PAIR, 16), PAIR), :] = v.astype(bf16)

    loop(NPAIR, xpair)

    def image(i):
        v = valid_ref[i].astype(f32)

        def row(r):
            g = i * WIN + r
            for q in range(4):
                tile = cot_ref[pl.ds(4 * WIN * g + q, WIN, stride=4), :]
                pad[g, :WIN, q * QUAD : (q + 1) * QUAD] = tile * v

        loop(WIN, row)

    loop(NWIN, image)
    for k, out in enumerate((c0, c1, c2, c3)):
        d = s ^ k
        v = pad[pl.ds(d * GROUP * WIN, GROUP * WIN)].reshape(GROUP * CELLS, WIDE)
        out[: GROUP * CELLS, :] = v.astype(bf16)
        out[GROUP * CELLS :, :] = jnp.zeros((BLOCK - GROUP * CELLS, WIDE), bf16)


def prep(ids, valid, x, cot):
    block = sds((BLOCK, WIDE), bf16)
    return call(
        prep_kernel,
        (sds((TOK, WIDE), bf16), block, block, block, block),
        [SM, SM, VM, VM],
        [pltpu.VMEM((NWIN * WIN, 8, WIDE), f32)],
        10**6,
        10**7,
        limit=16,
    )(ids, valid, x, cot)


def pack_rows(per, pc, q, p, e, k):
    parts = [(q, 0, per, j * WIDE) for j in range(3)]
    parts += [(p, 0, per, 0), (k, 0, pc, 0)]
    parts += [(e, 0, per, j * WIDE) for j in range(4)]
    return parts


def pack_kernel(per, pc, widths, count, ids, q, p, e, k, vec, tab, *refs):
    outs, tmp = refs[:count], refs[count:]
    c = ids[0] & 1
    y = ids[0] >> 1
    row = 0
    for ref, r0, n, col in pack_rows(per, pc, q, p, e, k):
        at = row
        for out, (lo, hi, wide) in zip(outs, widths):
            if lo <= row < hi:
                off = c * HALF + (y * QUAD if wide == QUAD else 0)
                lane = pl.multiple_of(col + off, QUAD)
                at = row - lo
                out[at : at + n, :] = ref[0, r0 : r0 + n, pl.ds(lane, wide)].astype(bf16)
        row += n
    if tmp:
        small = tmp[0]
        small[...] = jnp.zeros_like(small)
        small[0:12, :per] = vec[0]
        small[12:24, :per] = vec[1]
        small[24 : 24 + tab.shape[0], :SPAN] = tab[...]
        n = outs[-1].shape[0]
        outs[-1][n - SMALL :, :] = small[...].astype(bf16)


def pack(layer, per, pc, pieces, small, ids, masters):
    q, p, e, k, vec, tab = masters
    outs = tuple(sds((hi - lo, wide), bf16) for lo, hi, wide in pieces)
    if small == "row":
        outs = outs[:-1] + (sds((outs[-1].shape[0] + SMALL, HALF), bf16),)
    if small == "own":
        outs = outs + (sds((SMALL, HALF), bf16),)

    def spec(a):
        return pl.BlockSpec((1,) + a.shape[1:], lambda i: (layer, 0, 0))

    def whole(shape):
        return pl.BlockSpec(shape, lambda i: (0,) * len(shape))

    return pl.pallas_call(
        functools.partial(pack_kernel, per, pc, pieces, len(outs)),
        grid=(1,),
        scratch_shapes=[pltpu.VMEM((SMALL, HALF), f32)] if small else [],
        out_shape=outs,
        in_specs=[SM, spec(q), spec(p), spec(e), spec(k), whole(vec.shape), whole(tab.shape)],
        out_specs=tuple(whole(o.shape) for o in outs),
        compiler_params=pltpu.CompilerParams(vmem_limit_bytes=58 * MIB),
        cost_estimate=pl.CostEstimate(flops=10**5, bytes_accessed=3 * 10**6, transcendentals=0),
    )(ids, q, p, e, k, vec, tab)


def onehot(rb, shifted):
    lane = lax.broadcasted_iota(jnp.int32, (1, 1024), 1)
    cb = lane >> 7
    a = lane & 63
    ra = a >> 3
    ca = a & 7

    def moved(v):
        return jnp.where(v >= SHIFT, v - SHIFT, v + WIN - SHIFT) if shifted else v

    rbm = (rb - SHIFT if rb >= SHIFT else rb + WIN - SHIFT) if shifted else rb
    idx = (moved(ra) - rbm + WIN - 1) * (2 * WIN - 1) + moved(ca) - moved(cb) + WIN - 1
    good = (ra < WIN) & (ca < WIN) & (cb < WIN)
    idx = jnp.where(good, idx, -1)
    entry = lax.broadcasted_iota(jnp.int32, (256, 1024), 0)
    return jnp.where(entry == idx, 1.0, 0.0).astype(bf16)


def smalls_kernel(per, own, natural, ids, *refs):
    vec_ref, hide_ref, b0_ref, b1_ref, nat, tmp = refs[-6:]
    shards = WIDE // per
    for k in range(shards):
        if natural:
            nat[k] = refs[0][k].astype(f32)
        else:
            i = ids[1] ^ ((k & 3) * 2 + (k >> 2))
            nat[i] = refs[k >> 2][k & 3, 3 * per :, :].astype(f32)
    for l in range(2):
        rows = jnp.concatenate(
            [nat[i, 12 * l : 12 * l + 12, :per] for i in range(shards)], axis=1
        )
        vec_ref[l] = rows[:8]
        for r in range(4):
            for half in range(2):
                hide_ref[l, 2 * r + half] = rows[8 + r : 9 + r, half * HALF : (half + 1) * HALF]
    for layer in range(2):
        first = layer * (HEADS // own)
        table = jnp.concatenate(
            [nat[first + i, 24 : 24 + own, :] for i in range(HEADS // own)], axis=0
        ).astype(bf16)
        for rb in range(WIN):
            r = dot(table, onehot(rb, layer == 1))
            for cb in range(8):
                tmp[:, rb * 8 + cb, :] = r[:, cb * 128 : (cb + 1) * 128]
        b = lax.broadcasted_iota(jnp.int32, (CELLS, 128), 0)
        lane = lax.broadcasted_iota(jnp.int32, (CELLS, 128), 1)
        a = lane & 63
        gone = (b & 7) == 7
        if layer == 0:
            add = jnp.where(gone, pad_fill, 0.0)
            for h in range(HEADS):
                b0_ref[0, h * CELLS : (h + 1) * CELLS, :] = tmp[h] + add
        else:
            rows = ((b >> 3) < SHIFT) != ((a >> 3) < SHIFT)
            cols = (((b & 7) < SHIFT) != ((a & 7) < SHIFT)) & (lane >= 64)
            for r in range(2):
                cut = cols | rows if r else cols
                add = jnp.where(gone, pad_fill, jnp.where(cut, mask_fill, 0.0))
                for h in range(HEADS):
                    b1_ref[r, h * CELLS : (h + 1) * CELLS, :] = tmp[h] + add


def expand_smalls(per, own, natural, ids, small):
    shards = WIDE // per
    return call(
        functools.partial(smalls_kernel, per, own, natural),
        (
            sds((2, 8, WIDE), f32),
            sds((2, 8, 1, HALF), f32),
            sds((1, HEADS * CELLS, 128), f32),
            sds((2, HEADS * CELLS, 128), f32),
        ),
        [SM] + [VM] * len(small),
        [pltpu.VMEM((shards, SMALL, HALF), f32), pltpu.VMEM((HEADS, CELLS, 128), f32)],
        10**8,
        2 * 10**6,
        limit=16,
    )(ids, *small)


def attn_fwd_kernel(layer, per, plan, *refs):
    ids, nw = refs[0], plan.count
    xs, refs = (refs[1:2], refs[2:]) if layer == 0 else (refs[1:5], refs[5:])
    w_in, vec_ref, bias_ref, refs = refs[:nw], refs[nw], refs[nw + 1], refs[nw + 2 :]
    if layer == 0:
        x_out = xs[0]
        n1_ref, qkv_ref, p_ref, o_ref, w_ref, sem = refs
    else:
        x_out, n1_ref, qkv_ref, p_ref, o_ref, w_ref, sem, one, two = refs
    start_load(plan, w_in, w_ref, sem, ids)
    if layer == 1:
        for k, ref in enumerate(xs):
            w = ids[0] ^ k
            v = ref[: GROUP * CELLS, :].astype(f32).reshape(GROUP, CELLS, WIDE)
            for i in range(GROUP):
                one[pl.ds((i * 4 + w) * WIN, WIN)] = v[i].reshape(WIN, 8, WIDE)

        def put(p):
            v = one[pl.ds(p * 2 * WIN, 2 * WIN)].reshape(PAIR, WIDE)
            x_out[pl.ds(pl.multiple_of(p * PAIR, 16), PAIR), :] = v.astype(bf16)

        loop(NPAIR, put)
        x_out[ROWS:, :] = jnp.zeros((TOK - ROWS, WIDE), bf16)

    gain = vec_ref[layer, 0:1, :]
    shift = vec_ref[layer, 1:2, :]
    if layer == 0:

        def norm(c):
            rows = pl.ds(pl.multiple_of(c * STRIP, STRIP), STRIP)
            cen, rstd = centred(x_out[rows, :].astype(f32))
            n1_ref[rows, :] = (cen * rstd * gain + shift).astype(bf16)

        loop(NCH, norm)
    else:

        def norm(p):
            rows = pl.ds(p * QUADS, QUADS)
            cen, rstd = centred(one[rows].reshape(FOUR, WIDE))
            one[rows] = (cen * rstd * gain + shift).reshape(QUADS, 8, WIDE)

        loop(GROUP, norm)
        swap_into(one, n1_ref, two)
        n1_ref[ROWS:, :] = jnp.zeros((TOK - ROWS, WIDE), bf16)

    wait_all(w_ref, sem)
    for j in range(3):
        for half in range(2):
            c0 = half * 256
            r = dot(n1_ref[...], gather_rows(w_ref, j * per, per, 0, WIDE, c0, 256))
            if j != 1:
                row = 2 if j == 0 else 3
                r = r + vec_ref[layer, row : row + 1, c0 : c0 + 256]
            qkv_ref[:, j * WIDE + c0 : j * WIDE + c0 + 256] = r.astype(bf16)

    masks = head_masks()

    def pair(p):
        rows = pl.ds(pl.multiple_of(p * PAIR, 16), PAIR)
        kind = 0 if layer == 0 else p & 1
        lanes = [slice(t * 128, t * 128 + 128) for t in range(4)]

        def tile(t, part):
            c = part * WIDE + t * 128
            v = qkv_ref[rows, c : c + 128].astype(f32)
            return v[:CELLS], v[CELLS:]

        ks = [stacked(*tile(t, 1), masks) for t in range(4)]
        qs = [diagonal(*tile(t, 0)) for t in range(4)]
        vs = [stacked(*tile(t, 2), masks) for t in range(4)]
        sc = [dot_nt(ks[t], qs[t]) for t in range(4)]
        prs = []
        for t in range(4):
            v = scale * sc[t] + bias_ref[kind, t * QT : (t + 1) * QT, :]
            v = v.reshape(4, CELLS, 128)
            e = jnp.exp(v - jnp.max(v, axis=1, keepdims=True))
            pr = e * (1.0 / jnp.sum(e, axis=1, keepdims=True))
            prs.append(pr.reshape(QT, 128).astype(bf16))
        os = [from_diagonal(dot_tn(prs[t], vs[t])) for t in range(4)]
        for t in range(4):
            p_ref[p, t * QT : (t + 1) * QT, :] = prs[t]
            if layer == 0:
                o_ref[rows, lanes[t]] = os[t].astype(bf16)
            else:
                one[pl.ds(p * 2 * WIN, 2 * WIN), :, lanes[t]] = os[t].reshape(2 * WIN, 8, 128)

    loop(NPAIR, pair)
    if layer == 1:
        swap_into(one, o_ref, two)
    o_ref[ROWS:, :] = jnp.zeros((TOK - ROWS, WIDE), bf16)


def attn_fwd(layer, per, plan, ids, xs, w, vec, bias):
    act = sds((TOK, WIDE), bf16)
    saved = (act, sds((TOK, 3 * WIDE), bf16), sds((NPAIR, HEADS * CELLS, 128), bf16), act)
    kernel = functools.partial(attn_fwd_kernel, layer, per, plan)
    scratch = plan.scratch()
    outs = saved
    if layer == 1:
        tile = pltpu.VMEM((NWIN * WIN, 8, WIDE), f32)
        scratch = scratch + [tile, tile]
        outs = (act,) + saved
    return call(
        kernel,
        outs,
        [SM] + [VM] * len(xs) + [HB] * plan.count + [VM, VM],
        scratch,
        2 * TOK * WIDE * 3 * WIDE,
        12 * 10**6,
        limit=30,
    )(ids, *xs, *w, vec, bias)


def mlp_forward(layer, per, pc, load, x_ref, o_ref, w1, vec_ref, f_ref, y_ref, n2_ref, h_ref, g_ref, emit):
    load()
    for half in range(2):
        c0 = half * 256
        r = dot(o_ref[...], gather_rows(w1, 0, per, 0, WIDE, c0, 256))
        x = x_ref[:, c0 : c0 + 256].astype(f32)
        y_ref[:, c0 : c0 + 256] = x + (r + vec_ref[layer, 4:5, c0 : c0 + 256])
    gain = vec_ref[layer, 5:6, :]
    shift = vec_ref[layer, 6:7, :]

    def norm(c):
        rows = pl.ds(pl.multiple_of(c * STRIP, STRIP), STRIP)
        cen, rstd = centred(y_ref[rows, :])
        n2_ref[rows, :] = (cen * rstd * gain + shift).astype(bf16)

    loop(NCH, norm)

    def act(j):
        c0 = pl.multiple_of((j & 1) * 256, 256)
        v = w1[:, pl.ds(pl.multiple_of(per + pc + (j >> 1) * per, 16), per), pl.ds(c0, 256)]
        u = dot(n2_ref[...], v.reshape(WIDE, 256)) + f_ref[layer, j]
        h, g = gelu_pair(u)
        cols = pl.ds(pl.multiple_of(j * 256, 256), 256)
        h_ref[:, cols] = h.astype(bf16)
        g_ref[:, cols] = g.astype(bf16)

    loop(HIDE // 256, act)
    for half in range(2):
        c0 = half * 256
        v = w1[:, per : per + pc, c0 : c0 + 256].reshape(HIDE, 256)
        r = dot(h_ref[...], v)
        emit(c0, y_ref[:, c0 : c0 + 256] + (r + vec_ref[layer, 7:8, c0 : c0 + 256]))


def mlp_load(plan, w_in, w1, s1, ids):
    start_load(plan, w_in, w1, s1, ids)
    return lambda: wait_all(w1, s1)


def mlp_fwd_kernel(per, pc, plan, *refs):
    nw = plan.count
    ids, x_ref, o_ref = refs[:3]
    w_in, refs = refs[3 : 3 + nw], refs[3 + nw :]
    vec_ref, f_ref, y_ref, n2_ref, h_ref, g_ref, xa, xb, xc, xd, nxt, w1, s1 = refs
    load = mlp_load(plan, w_in, w1, s1, ids)

    def emit(c0, v):
        nxt[:, c0 : c0 + 256] = v

    mlp_forward(
        0, per, pc, load, x_ref, o_ref, w1, vec_ref, f_ref, y_ref, n2_ref, h_ref, g_ref, emit
    )
    size = GROUP * CELLS
    for k, out in enumerate((xa, xb, xc, xd)):
        v = nxt[pl.ds(pl.multiple_of((ids[0] ^ k) * size, 8), size), :]
        out[:size, :] = v.astype(bf16)
        out[size:, :] = jnp.zeros((BLOCK - size, WIDE), bf16)


def mlp_fwd(per, pc, plan, ids, x, o, w, vec, f):
    act = sds((TOK, WIDE), bf16)
    wide = sds((TOK, HIDE), bf16)
    return call(
        functools.partial(mlp_fwd_kernel, per, pc, plan),
        (sds((TOK, WIDE), f32), act, wide, wide) + (sds((BLOCK, WIDE), bf16),) * 4,
        [SM, VM, VM] + [HB] * len(w) + [VM, VM],
        [pltpu.VMEM((TOK, WIDE), f32)] + plan.scratch(),
        2 * TOK * WIDE * (WIDE + 2 * HIDE),
        25 * 10**6,
        limit=40,
    )(ids, x, o, *w, vec, f)


def rows_sum(v):
    return jnp.sum(v, axis=0, keepdims=True)


def mlp_back(per, pc, plan, ids, dm_ref, wc, n2_ref, h_ref, g_ref, du, df_ref, dm_sum, outs, scratch):
    turned, g1, t1 = scratch
    shards = WIDE // per
    turned[...] = n2_ref[...].T
    grows = WIDE // pc

    def step(j):
        cols = pl.ds(pl.multiple_of(j * WIDE, WIDE), WIDE)
        w = wc[pl.ds(j * grows, grows)].reshape(WIDE, WIDE)
        dm = dm_ref[...]
        dh = dot_nt(dm, w)
        d = (dh * g_ref[:, cols].astype(f32)).astype(bf16)
        du[:, cols] = d
        total = rows_sum(d.astype(f32))
        for half in range(2):
            df_ref[2 * j + half] = total[:, half * 256 : half * 256 + 256]
        gc = dot_tn(h_ref[:, cols], dm)
        g1[pl.ds(j * grows, grows), 0:pc, :] = gc.astype(bf16).reshape(grows, pc, WIDE)
        ge = dot(turned[...], d)
        g1[:, pl.ds(pl.multiple_of(pc + j * per, 16), per), :] = ge.astype(bf16).reshape(
            shards, per, WIDE
        )

    loop(HIDE // WIDE, step)
    start_grads(plan, g1, outs, t1, ids)
    dm_sum[...] = rows_sum(dm_ref[...].astype(f32))
    return lambda: wait_all(g1, t1)


def mlp_back_scratch(gplan):
    return [pltpu.VMEM((WIDE, TOK), bf16)] + gplan.scratch()


def mlp_back_outs(gplan):
    outs = (
        sds((TOK, WIDE), bf16),
        sds((TOK, HIDE), bf16),
        sds((8, 1, 256), f32),
        sds((1, WIDE), f32),
    )
    return outs + grad_shapes(gplan)


def mlp_both_kernel(per, pc, plan, gplan, *refs):
    nw = plan.count
    ids, x_ref, o_ref = refs[:3]
    w_in, refs = refs[3 : 3 + nw], refs[3 + nw :]
    vec_ref, f_ref = refs[:2]
    cots, blocks, refs = refs[2:6], refs[6:10], refs[10:]
    do_ref, dy_ref, da_ref, gv_ref, df_ref, dm_sum = refs[:6]
    outs, refs = refs[6:8], refs[8:]
    y_ref, dm_ref, du, n2_ref, h_ref, g_ref, nxt, tmp, w1, s1 = refs[:10]
    scratch = refs[10:]
    load = mlp_load(plan, w_in, w1, s1, ids)

    def emit(c0, v):
        nxt[:, c0 : c0 + 256] = v

    mlp_forward(
        1, per, pc, load, x_ref, o_ref, w1, vec_ref, f_ref, y_ref, n2_ref, h_ref, g_ref, emit
    )
    s = ids[0]
    size = GROUP * CELLS
    for k, out in enumerate(blocks):
        for i in range(GROUP):
            row = pl.multiple_of((i * 4 + (s ^ k)) * CELLS, 8)
            tmp[i * CELLS : (i + 1) * CELLS, :] = nxt[pl.ds(row, CELLS), :]
        out[:size, :] = tmp[:size, :].astype(bf16)
        out[size:, :] = jnp.zeros((BLOCK - size, WIDE), bf16)
    for k, ref in enumerate(cots):
        v = ref[:size, :].astype(f32)
        for i in range(GROUP):
            row = pl.multiple_of((i * 4 + (s ^ k)) * CELLS, 8)
            nxt[pl.ds(row, CELLS), :] = v[i * CELLS : (i + 1) * CELLS, :]
    dm_ref[:ROWS, :] = nxt[:ROWS, :].astype(bf16)
    dm_ref[ROWS:, :] = jnp.zeros((TOK - ROWS, WIDE), bf16)
    wc = w1.at[:, per : per + pc, :]
    done = mlp_back(
        per, pc, gplan, ids, dm_ref, wc, n2_ref, h_ref, g_ref, du, df_ref, dm_sum, outs, scratch
    )
    mid_body(1, per, pc, w1, vec_ref, y_ref, dm_ref, du, do_ref, dy_ref, da_ref, gv_ref, nxt)
    done()


def mlp_both(per, pc, plan, gplan, ids, x, o, w, vec, f, cots):
    block = sds((BLOCK, WIDE), bf16)
    outs = (block,) * 4 + mid_outs() + mlp_back_outs(gplan)[2:]
    scratch = [
        pltpu.VMEM((TOK, WIDE), f32),
        pltpu.VMEM((TOK, WIDE), bf16),
        pltpu.VMEM((TOK, HIDE), bf16),
        pltpu.VMEM((TOK, WIDE), bf16),
        pltpu.VMEM((TOK, HIDE), bf16),
        pltpu.VMEM((TOK, HIDE), bf16),
        pltpu.VMEM((TOK, WIDE), f32),
        pltpu.VMEM((BLOCK, WIDE), f32),
    ]
    return call(
        functools.partial(mlp_both_kernel, per, pc, plan, gplan),
        outs,
        [SM, VM, VM] + [HB] * len(w) + [VM] * 6,
        scratch + plan.scratch() + mlp_back_scratch(gplan),
        5 * TOK * WIDE * (WIDE + 2 * HIDE),
        25 * 10**6,
        (VM,) * 10 + (HB,) * 2,
        50,
    )(ids, x, o, *w, vec, f, *cots)


def mlp_bwd_kernel(per, pc, plan, gplan, *refs):
    nw = plan.count
    ids, w_in, refs = refs[0], refs[1 : 1 + nw], refs[1 + nw :]
    n2_ref, h_ref, g_ref = refs[:3]
    grads, refs = refs[3:7], refs[7:]
    dm_ref, du, df_ref, dm_sum = refs[:4]
    outs, refs = refs[4:6], refs[6:]
    tmp, w1, s1 = refs[:3]
    scratch = refs[3:]
    start_load(plan, w_in, w1, s1, ids, ((per, per + pc),))
    s = ids[0]
    size = GROUP * CELLS
    for k, ref in enumerate(grads):
        tmp[pl.ds(pl.multiple_of((s ^ k) * size, 8), size), :] = ref[:size, :].astype(f32)
    dm_ref[:ROWS, :] = tmp[:ROWS, :].astype(bf16)
    dm_ref[ROWS:, :] = jnp.zeros((TOK - ROWS, WIDE), bf16)
    wc = w1.at[:, per : per + pc, :]
    wait_all(wc, s1)
    mlp_back(
        per, pc, gplan, ids, dm_ref, wc, n2_ref, h_ref, g_ref, du, df_ref, dm_sum, outs, scratch
    )()


def mlp_bwd(per, pc, plan, gplan, ids, w, n2, h, g, grads):
    return call(
        functools.partial(mlp_bwd_kernel, per, pc, plan, gplan),
        mlp_back_outs(gplan),
        [SM] + [HB] * len(w) + [VM] * 7,
        [pltpu.VMEM((TOK, WIDE), f32)] + plan.scratch() + mlp_back_scratch(gplan),
        3 * TOK * WIDE * 2 * HIDE,
        25 * 10**6,
        (VM,) * 4 + (HB,) * 2,
        limit=48,
    )(ids, *w, n2, h, g, *grads)


def mid_kernel(layer, per, pc, plan, *refs):
    nw = plan.count
    ids, w_in, refs = refs[0], refs[1 : 1 + nw], refs[1 + nw :]
    vec_ref, y_ref, dm_ref, du, do_ref, dy_ref, da_ref, gv_ref, dn2, w1, s1, s2 = refs
    spans = ((0, per), (per + pc, 5 * per + pc))
    start_load(plan, w_in, w1, s1, ids, spans[:1])
    start_load(plan, w_in, w1, s2, ids, spans[1:])
    for (lo, hi), sem in zip(spans, (s1, s2)):
        wait_all(w1.at[:, lo:hi, :], sem)
    mid_body(layer, per, pc, w1, vec_ref, y_ref, dm_ref, du, do_ref, dy_ref, da_ref, gv_ref, dn2)


def mid_outs():
    act = sds((TOK, WIDE), bf16)
    return (act, sds((TOK, WIDE), f32), act, sds((8, WIDE), f32))


def mid_body(layer, per, pc, w1, vec_ref, y_ref, dm_ref, du, do_ref, dy_ref, da_ref, gv_ref, dn2):
    gv_ref[...] = jnp.zeros_like(gv_ref)
    for half in range(2):
        total = None
        for c in range(4):
            w = gather_rows(w1, per + pc + c * per, per, half, 256, 0, WIDE)
            part = dot_nt(du[:, c * WIDE : (c + 1) * WIDE], w)
            total = part if total is None else total + part
        dn2[:, half * 256 : half * 256 + 256] = total
    gain = vec_ref[layer, 5:6, :]

    def norm(c):
        rows = pl.ds(pl.multiple_of(c * STRIP, STRIP), STRIP)
        cen, rstd = centred(y_ref[rows, :])
        xhat = cen * rstd
        dn = dn2[rows, :]
        gv_ref[5:6, :] += rows_sum(dn * xhat)
        gv_ref[6:7, :] += rows_sum(dn)
        dx = dn * gain
        m1 = jnp.mean(dx, axis=-1, keepdims=True)
        m2 = jnp.mean(dx * xhat, axis=-1, keepdims=True)
        dy = dm_ref[rows, :].astype(f32) + rstd * (dx - m1 - xhat * m2)
        dy_ref[rows, :] = dy
        da = dy.astype(bf16)
        gv_ref[4:5, :] += rows_sum(da.astype(f32))
        da_ref[rows, :] = da

    loop(NCH, norm)
    for half in range(2):
        c0 = half * 256
        w = gather_rows(w1, 0, per, half, 256, 0, WIDE)
        do_ref[:, c0 : c0 + 256] = dot_nt(da_ref[...], w).astype(bf16)


def mid_bwd(layer, per, pc, plan, ids, w, vec, y, dm, du):
    return call(
        functools.partial(mid_kernel, layer, per, pc, plan),
        mid_outs(),
        [SM] + [HB] * len(w) + [VM] * 4,
        [pltpu.VMEM((TOK, WIDE), f32)] + plan.scratch() + [pltpu.SemaphoreType.DMA],
        2 * TOK * WIDE * (WIDE + HIDE),
        16 * 10**6,
        limit=34,
    )(ids, *w, vec, y, dm, du)


def attn_bwd_kernel(layer, do_ref, qkv_ref, p_ref, dqkv, gv_ref, gt_ref, *rest):
    dsum = rest[0]
    if layer == 1:
        one, two = rest[1:]

        def widen(p):
            v = do_ref[pl.ds(pl.multiple_of(p * PAIR, 16), PAIR), :].astype(f32)
            one[pl.ds(p * 2 * WIN, 2 * WIN)] = v.reshape(2 * WIN, 8, WIDE)

        loop(NPAIR, widen)

        def emit(w, tile):
            two[pl.ds(w * WIN, WIN)] = tile

        swap_windows(one, emit)
    gv_ref[...] = jnp.zeros_like(gv_ref)
    dsum[...] = jnp.zeros_like(dsum)
    dqkv[ROWS:, :] = jnp.zeros((TOK - ROWS, 3 * WIDE), bf16)
    masks = head_masks()

    def pair(p):
        rows = pl.ds(pl.multiple_of(p * PAIR, 16), PAIR)
        def tile(t, part):
            c = part * WIDE + t * 128
            v = qkv_ref[rows, c : c + 128].astype(f32)
            return v[:CELLS], v[CELLS:]

        def grad(t):
            c = t * 128
            if layer == 0:
                d = do_ref[rows, c : c + 128].astype(f32)
            else:
                d = two[pl.ds(p * 2 * WIN, 2 * WIN), :, c : c + 128].reshape(PAIR, 128)
            return d[:CELLS], d[CELLS:]

        four = range(4)
        vs = [stacked(*tile(t, 2), masks) for t in four]
        dd = [diagonal(*grad(t)) for t in four]
        ks = [stacked(*tile(t, 1), masks) for t in four]
        qs = [diagonal(*tile(t, 0)) for t in four]
        pb = [p_ref[p, t * QT : (t + 1) * QT, :] for t in four]
        dp = [dot_nt(vs[t], dd[t]) for t in four]
        dv = [from_stacked(dot(pb[t], dd[t]), masks).astype(bf16) for t in four]
        ds = []
        for t in four:
            pf = pb[t].astype(f32).reshape(4, CELLS, 128)
            g = dp[t].reshape(4, CELLS, 128)
            tot = jnp.sum(g * pf, axis=1, keepdims=True)
            ds.append((pf * (g - tot)).reshape(QT, 128).astype(bf16))
        dq = [(scale * from_diagonal(dot_tn(ds[t], ks[t]))).astype(bf16) for t in four]
        dk = [(scale * from_stacked(dot(ds[t], qs[t]), masks)).astype(bf16) for t in four]
        for t in four:
            c = t * 128
            dsum[4 * t : 4 * t + 4] += ds[t].astype(f32).reshape(4, CELLS, 128)
            dqkv[rows, c : c + 128] = dq[t]
            dqkv[rows, WIDE + c : WIDE + c + 128] = dk[t]
            dqkv[rows, 2 * WIDE + c : 2 * WIDE + c + 128] = dv[t]
            gv_ref[2:3, c : c + 128] += rows_sum(dq[t].astype(f32))
            gv_ref[3:4, c : c + 128] += rows_sum(dv[t].astype(f32))

    loop(NPAIR, pair)
    total = jnp.zeros((HEADS, 256), f32)
    for rb in range(WIN):
        x = jnp.concatenate([dsum[:, rb * 8 + cb, :] for cb in range(8)], axis=1)
        hi = x.astype(bf16)
        lo = (x - hi.astype(f32)).astype(bf16)
        oh = onehot(rb, layer == 1)
        total = total + (dot_nt(hi, oh) + dot_nt(lo, oh))
    gt_ref[...] = total


def attn_bwd(layer, do, qkv, probs):
    tile = pltpu.VMEM((NWIN * WIN, 8, WIDE), f32)
    return call(
        functools.partial(attn_bwd_kernel, layer),
        (sds((TOK, 3 * WIDE), bf16), sds((8, WIDE), f32), sds((HEADS, 256), f32)),
        [VM] * 3,
        [pltpu.VMEM((HEADS, CELLS, 128), f32)] + [tile, tile] * layer,
        2 * TOK * WIDE * 3 * WIDE,
        12 * 10**6,
        limit=28,
    )(do, qkv, probs)


def qkv_grad_kernel(per, plan, ids, n1_ref, dqkv, o_ref, da_ref, keep, send, turned, gq, sem):
    shards = WIDE // per
    turned[...] = o_ref[...].T
    for half in range(2):
        c0 = half * 256
        g = dot(turned[...], da_ref[:, c0 : c0 + 256])
        gq[:, 3 * per : 4 * per, c0 : c0 + 256] = g.astype(bf16).reshape(shards, per, 256)
    turned[...] = n1_ref[...].T
    for j in range(3):
        for half in range(2):
            c0 = half * 256
            g = dot(turned[...], dqkv[:, j * WIDE + c0 : j * WIDE + c0 + 256])
            gq[:, j * per : (j + 1) * per, c0 : c0 + 256] = g.astype(bf16).reshape(
                shards, per, 256
            )
    start_grads(plan, gq, (keep, send), sem, ids)
    wait_all(gq, sem)


def qkv_grad(per, plan, ids, n1, dqkv, o, da):
    return call(
        functools.partial(qkv_grad_kernel, per, plan),
        grad_shapes(plan),
        [SM, VM, VM, VM, VM],
        [pltpu.VMEM((WIDE, TOK), bf16)] + plan.scratch(),
        2 * TOK * WIDE * 4 * WIDE,
        9 * 10**6,
        (HB, HB),
        limit=24,
    )(ids, n1, dqkv, o, da)


def dx_kernel(layer, per, plan, *refs):
    nw = plan.count
    ids, dqkv, dy_ref, x_ref = refs[:4]
    w_in, vec_ref, refs = refs[4 : 4 + nw], refs[4 + nw], refs[5 + nw :]
    nout = 1 if layer == 0 else 4
    dx_refs, gv_ref, refs = refs[:nout], refs[nout], refs[nout + 1 :]
    dn, one, w_ref, sem = refs
    start_load(plan, w_in, w_ref, sem, ids)
    gv_ref[...] = jnp.zeros_like(gv_ref)
    wait_all(w_ref, sem)
    for half in range(2):
        total = None
        for c in range(3):
            w = gather_rows(w_ref, c * per, per, half, 256, 0, WIDE)
            part = dot_nt(dqkv[:, c * WIDE : (c + 1) * WIDE], w)
            total = part if total is None else total + part
        dn[:, half * 256 : half * 256 + 256] = total
    gain = vec_ref[layer, 0:1, :]
    if layer == 1:

        def widen_dn(p):
            v = dn[pl.ds(pl.multiple_of(p * PAIR, 8), PAIR), :].astype(bf16).astype(f32)
            one[pl.ds(p * 2 * WIN, 2 * WIN)] = v.reshape(2 * WIN, 8, WIDE)

        loop(NPAIR, widen_dn)

        def emit_dn(w, tile):
            dn[pl.ds(pl.multiple_of(w * CELLS, 8), CELLS), :] = tile.reshape(CELLS, WIDE)

        swap_windows(one, emit_dn)

    def norm(p):
        rows = pl.ds(pl.multiple_of(p * FOUR, 16), FOUR)
        cen, rstd = centred(x_ref[rows, :].astype(f32))
        xhat = cen * rstd
        d = dn[rows, :]
        gv_ref[0:1, :] += rows_sum(d * xhat)
        gv_ref[1:2, :] += rows_sum(d)
        dx = d * gain
        m1 = jnp.mean(dx, axis=-1, keepdims=True)
        m2 = jnp.mean(dx * xhat, axis=-1, keepdims=True)
        out = dy_ref[rows, :] + rstd * (dx - m1 - xhat * m2)
        one[pl.ds(p * QUADS, QUADS)] = out.reshape(QUADS, 8, WIDE)

    loop(GROUP, norm)
    if layer == 0:
        put_dense(dx_refs[0], one)
    else:
        s = ids[0]
        size = GROUP * CELLS
        for k, out in enumerate(dx_refs):
            for i in range(GROUP):
                tile = one[pl.ds((i * 4 + (s ^ k)) * WIN, WIN)]
                dn[i * CELLS : (i + 1) * CELLS, :] = tile.reshape(CELLS, WIDE)
            out[:size, :] = dn[:size, :].astype(bf16)
            out[size:, :] = jnp.zeros((BLOCK - size, WIDE), bf16)


def dx_step(layer, per, plan, ids, dqkv, dy, x, w, vec):
    if layer == 0:
        outs = (sds((NWIN * WIN * WIN * 4, QUAD), f32),)
    else:
        outs = (sds((BLOCK, WIDE), bf16),) * 4
    tile = pltpu.VMEM((NWIN * WIN, 8, WIDE), f32)
    return call(
        functools.partial(dx_kernel, layer, per, plan),
        outs + (sds((8, WIDE), f32),),
        [SM, VM, VM, VM] + [HB] * plan.count + [VM],
        [pltpu.VMEM((TOK, WIDE), f32), tile] + plan.scratch(),
        2 * TOK * WIDE * 3 * WIDE,
        12 * 10**6,
        limit=28,
    )(ids, dqkv, dy, x, *w, vec)


def join_kernel(ids, xa, xb, xc, xd, out_ref, pad):
    s = ids[0]
    size = GROUP * CELLS
    for k, ref in enumerate((xa, xb, xc, xd)):
        v = ref[:size, :].astype(f32).reshape(GROUP * WIN, 8, WIDE)
        pad[pl.ds((s ^ k) * GROUP * WIN, GROUP * WIN)] = v
    put_dense(out_ref, pad)


def join_blocks(ids, blocks):
    return call(
        join_kernel,
        (sds((NWIN * WIN * WIN * 4, QUAD), f32),),
        [SM] + [VM] * 4,
        [pltpu.VMEM((NWIN * WIN, 8, WIDE), f32)],
        10**6,
        5 * 10**6,
        limit=58,
    )(ids, *blocks)[0]


def hop(value, way):
    axes = {"c": ("core",), "cy": ("y", "core"), "xy": ("y", "x")}.get(way, (way[0],))
    mask = {"z2": 2, "z3": 3, "cy": 3, "xy": 3}.get(way, 1)
    size = math.prod(lax.axis_size(a) for a in axes)
    return lax.ppermute(value, axes, [(i, i ^ mask) for i in range(size)])


def tie(*values):
    return lax.optimization_barrier(values)


def exchange(blocks):
    return [blocks[0]] + [hop(b, way) for b, way in zip(blocks[1:], ("c", "y", "cy"))]


def swap_all(value, axes):
    return lax.all_to_all(value, axes, 0, 0)


def share(value, axes):
    n = math.prod(lax.axis_size(a) for a in axes)
    return swap_all(jnp.stack([value] * n), axes)


def gather_c(gs):
    return gs + [hop(g, "c") for g in gs]


def add16(*terms):
    total = terms[0].astype(f32)
    for t in terms[1:]:
        total = total + t.astype(f32)
    return total.astype(bf16)


def near_xy(keep, r):
    own, *others = [add16(keep[k], r[k]) for k in range(4)]
    return own, [hop(t, way) for t, way in zip(others, ("x", "y", "xy"))]


def near_z(own, got):
    own, *others = [add16(own[k], *[g[k] for g in got]) for k in range(4)]
    return own, [hop(t, way) for t, way in zip(others, ("z1", "z2", "z3"))]


def near_spread(own, got):
    f = add16(own, *got)
    return [f, hop(f, "y"), hop(f, "c"), hop(f, "cy")]


def step_core(grads, r):
    keep = grads[0]
    return add16(keep[0], r[0]), hop(add16(keep[1], r[1]), "x")


def step_next(own, r, way):
    return add16(own[0], r[0]), hop(add16(own[1], r[1]), way)


def step_last(own, r):
    f = add16(own, r)
    return f, hop(f, "y")


def step_spread(f, r):
    f = add16(f, r)
    return [f, hop(f, "c")]


def half_reduce(grads, shard):
    total = add16(grads[0], hop(grads[1], "c"))
    total = total.reshape((-1,) + total.shape[2:])
    f = lax.psum_scatter(total, ("y",) + shard, scatter_dimension=0, tiled=False)
    return [f, hop(f, "y"), hop(f, "c"), hop(f, "cy")]


def adam_math(weight, moment_one, moment_two, gradient, step_rate, decay_rate):
    first_new = beta_one * moment_one + (1.0 - beta_one) * gradient
    second_new = beta_two * moment_two + (1.0 - beta_two) * gradient * gradient
    correct_one = 1.0 - beta_one**ADAM_STEP
    correct_two = 1.0 - beta_two**ADAM_STEP
    update = first_new / correct_one / (jnp.sqrt(second_new / correct_two) + adam_eps)
    weight_new = weight * (1.0 - step_rate * decay_rate) - step_rate * update
    return (first_new, second_new, weight_new)


def adam_kernel(segments, members, old, count, ids, *refs):
    n = len(members)
    blocks, refs = refs[:count], refs[count:]
    ins, outs, tot = refs[: 3 * n], refs[3 * n + old : 6 * n + old], refs[-1]
    c, y, x, z = place(ids)
    for k, ref in enumerate(blocks):
        if count == 2:
            lane = pl.multiple_of((c ^ k) * HALF, HALF)
        else:
            lane = pl.multiple_of((c ^ (k >> 1)) * HALF + (y ^ (k & 1)) * QUAD, QUAD)
        tot[:, pl.ds(lane, WIDE // count)] = ref[...].astype(f32)
    for row, m, count, col in segments:
        at = (0, slice(0, count), slice(col, col + WIDE))
        pos = members[m]
        new = adam_math(
            ins[3 * m][at],
            ins[3 * m + 1][at],
            ins[3 * m + 2][at],
            tot[row : row + count, :],
            step_rates[pos],
            decay_rates[pos],
        )
        for k in range(3):
            outs[3 * m + k][at] = new[k]


def adam_step(layer, segments, members, ids, blocks, params, old):
    ins = [a for pos in members for a in (params[0][pos], params[1][pos], params[2][pos])]
    rows = blocks[0].shape[0]

    def spec(a):
        return pl.BlockSpec((1,) + a.shape[1:], lambda i: (layer, 0, 0))

    outs = tuple(sds(a.shape, f32) for a in ins)
    held = list(old or [])
    base = 1 + len(blocks) + len(ins)
    return pl.pallas_call(
        functools.partial(adam_kernel, segments, members, len(held), len(blocks)),
        grid=(1,),
        out_shape=outs,
        in_specs=[SM]
        + [pl.BlockSpec(b.shape, lambda i: (0, 0)) for b in blocks]
        + [spec(a) for a in ins]
        + [HB] * len(held),
        out_specs=tuple(spec(a) for a in ins),
        scratch_shapes=[pltpu.VMEM((rows, WIDE), f32)],
        input_output_aliases={base + k: k for k in range(len(held))},
        compiler_params=pltpu.CompilerParams(vmem_limit_bytes=58 * MIB),
        cost_estimate=pl.CostEstimate(
            flops=20 * rows * WIDE, bytes_accessed=24 * rows * WIDE, transcendentals=0
        ),
    )(ids, *blocks, *ins, *held)


def body(shard, *args):
    inputs, cotangent, image_valid = args[:3]
    masters, firsts, seconds = args[3:9], args[9:15], args[15:21]
    params = (masters, firsts, seconds)
    per = masters[0].shape[1]
    pc = masters[3].shape[1]
    own = masters[5].shape[0]
    shards = WIDE // per
    fast = len(shard) == 2
    seq = lax.axis_index(("y", "core")).astype(jnp.int32)
    me = lax.axis_index(shard).astype(jnp.int32)
    ids = jnp.stack([seq, me])

    nq, nm = 3 * per, 5 * per + pc
    whole = ((0, nq + nm, HALF),)
    wide = "wide" if fast else "half"
    pq0 = Plan(wide, shards, nq)
    pm0 = Plan("near" if fast else "half", shards, nm, 0 if fast else nq)
    pq1, pm1 = Plan(wide, shards, nq), Plan(wide, shards, nm, 0 if fast else nq)
    gqp, gmp = Plan(wide, shards, 4 * per), Plan(wide, shards, 4 * per + pc)
    gmp0 = Plan("near" if fast else "half", shards, 4 * per + pc)
    x_in = inputs.reshape(NWIN * WIN, WIN, WIDE)
    cot = cotangent.reshape(NWIN * WIN * WIN * 4, QUAD)
    seg_q = [(j * per, 0, per, j * WIDE) for j in range(3)] + [(3 * per, 1, per, 0)]
    seg_m = [(0, 1, pc, 0)] + [(pc + j * per, 0, per, j * WIDE) for j in range(4)]

    def adam_q(layer, blocks, old=None):
        return adam_step(layer, seg_q, (0, 1), ids, blocks, params, old)

    def adam_m(layer, blocks, old=None):
        return adam_step(layer, seg_m, (2, 3), ids, blocks, params, old)

    def all_smalls(parts):
        rows = []
        for gvm, dms, df, gva, gvx, gt in parts:
            total = gvm + gva + gvx
            rows += [total[:7], dms, df.reshape(4, WIDE), gt.reshape(8, WIDE)]
        return jnp.concatenate(rows, axis=0).astype(bf16)

    if fast:
        em0, eq0 = pack(0, per, pc, ((nq, nq + nm, QUAD), (0, nq, HALF)), "row", ids, masters)
        zq = [hop(eq0, "z1"), hop(eq0, "z2")]
        zm = [hop(em0, "z1"), hop(em0, "z2")]
        x0, *cots = prep(ids, image_valid, x_in, cot)
        zq, zm, x0 = tie(zq, zm, x0)
        zq.append(hop(zq[1], "z1"))
        zm.append(hop(zm[1], "z1"))
        (e1,) = pack(1, per, pc, whole, "", ids, masters)
        zq, zm, e1 = tie(zq, zm, e1)
        g = jnp.stack([eq0] + zq)
        gx = hop(g, "x")
        gm = jnp.stack([em0] + zm)
        wm0 = [gm] + [hop(gm, way) for way in ("x", "y", "xy")]
        z1, z2 = hop(e1, "z1"), hop(e1, "z2")
        vec, hide, bias0, bias1 = expand_smalls(per, own, False, ids, [g, gx])
        wq0 = gather_c([g, gx])
        n1a, qkva, pa, oa = attn_fwd(0, per, pq0, ids, [x0], wq0, vec, bias0)
        oa, wm0, z1, z2 = tie(oa, wm0, z1, z2)
        z3 = hop(z2, "z1")
        wm0 = gather_c(wm0)
        ya, n2a, ha, ga, *x1s = mlp_fwd(per, pc, pm0, ids, x0, oa, wm0, vec, hide)
        x1s, z3 = tie(x1s, z3)
        ze1 = [e1, z1, z2, z3]
        gq1w = jnp.stack([v[:nq] for v in ze1])
        gq1x = hop(gq1w, "x")
        x1s = exchange(x1s)
        x1s, ze1, gq1x = tie(x1s, ze1, gq1x)
        gm1w = jnp.stack([v[nq:] for v in ze1])
        gm1x = hop(gm1w, "x")
        gm1c = hop(gm1w, "c")
        w1q = gather_c([gq1w, gq1x])
        cots = exchange(cots)
        x1, n1b, qkvb, pb, ob = attn_fwd(1, per, pq1, ids, x1s, w1q, vec, bias1)
        ob, cots, gm1x, gm1c = tie(ob, cots, gm1x, gm1c)
        w1 = [gm1w, gm1x, gm1c, hop(gm1x, "c")]
        res = mlp_both(per, pc, pm1, gmp, ids, x1, ob, w1, vec, hide, cots)
        outs, (dob, dyb, dab, gvm1, df1, dms1), gm1 = res[:4], res[4:10], res[10:12]
        rm1 = hop(gm1[1], "c")
        outs = exchange(outs)
        dqkvb, gva1, gt1 = attn_bwd(1, dob, qkvb, pb)
        dqkvb, rm1, outs = tie(dqkvb, rm1, outs)
        sm1 = step_core(gm1, rm1)
        *dx1s, gvx1 = dx_step(1, per, pq1, ids, dqkvb, dyb, x1, w1q, vec)
        dx1s, dqkvb = tie(dx1s, dqkvb)
        dx1s = exchange(dx1s)
        gq1 = qkv_grad(per, gqp, ids, n1b, dqkvb, ob, dab)
        gq1, dx1s, sm1 = tie(gq1, dx1s, sm1)
        rq1 = hop(gq1[1], "c")
        sm1 = step_next(*sm1, "z1")
        dma, dua, df0, dms0, *gm0 = mlp_bwd(per, pc, pm0, gmp0, ids, wm0, n2a, ha, ga, dx1s)
        dua, rq1, sm1, gm0 = tie(dua, rq1, sm1, gm0)
        rm0 = hop(gm0[1], "c")
        sq1 = step_core(gq1, rq1)
        sm1 = step_next(*sm1, "z2")
        doa, dya, daa, gvm0 = mid_bwd(0, per, pc, pm0, ids, wm0, vec, ya, dma, dua)
        doa, rm0, sq1, sm1 = tie(doa, rm0, sq1, sm1)
        sm0 = near_xy(gm0[0], rm0)
        sq1 = step_next(*sq1, "z1")
        sm1 = step_last(*sm1)
        dqkva, gva0, gt0 = attn_bwd(0, doa, qkva, pa)
        dqkva, sq1, sm1 = tie(dqkva, sq1, sm1)
        sq1 = step_next(*sq1, "z2")
        fm1 = step_spread(*sm1)
        gq0 = qkv_grad(per, gqp, ids, n1a, dqkva, oa, daa)
        gq0, sm0, sq1, fm1, outs = tie(gq0, sm0, sq1, fm1, outs)
        rq0 = hop(gq0[1], "c")
        sm0 = near_z(*sm0)
        output = join_blocks(ids, outs)
        output, rq0 = tie(output, rq0)
        sq0 = step_core(gq0, rq0)
        sq1 = step_last(*sq1)
        dx0, gvx0 = dx_step(0, per, pq0, ids, dqkva, dya, x0, wq0, vec)
        dx0, gvx0, sq0, sm0, sq1 = tie(dx0, gvx0, sq0, sm0, sq1)
        sq0 = step_next(*sq0, "z1")
        fm0 = near_spread(*sm0)
        smalls = all_smalls(
            ((gvm0, dms0, df0, gva0, gvx0, gt0), (gvm1, dms1, df1, gva1, gvx1, gt1))
        )
        fq1 = step_spread(*sq1)
        sc = hop(smalls, "c")
        new_m = adam_m(1, fm1)
        new_m, sq0, sc, fq1 = tie(new_m, sq0, sc, fq1)
        sq0 = step_next(*sq0, "z2")
        smalls = add16(smalls, sc)
        sc = hop(smalls, "x")
        new_q = adam_q(1, fq1)
        new_q, sq0, fm0, sc = tie(new_q, sq0, fm0, sc)
        sq0 = step_last(*sq0)
        smalls = add16(smalls, sc)
        sc = hop(smalls, "z1")
        new_m = adam_m(0, fm0, new_m)
        new_m, sq0, sc = tie(new_m, sq0, sc)
        fq0 = step_spread(*sq0)
        smalls = add16(smalls, sc)
        sc = hop(smalls, "z2")
        fq0, sc = tie(fq0, sc)
        smalls = add16(smalls, sc)
        sc = hop(smalls, "y")
        new_q = adam_q(0, fq0, new_q)
        new_q, sc = tie(new_q, sc)
        smalls = add16(smalls, sc)
    else:
        half0, small = pack(0, per, pc, whole, "own", ids, masters)
        (e1,) = pack(1, per, pc, whole, "", ids, masters)
        x0, *cots = prep(ids, image_valid, x_in, cot)
        cots = exchange(cots)
        small = lax.all_gather(small, shard, axis=0, tiled=False)
        vec, hide, bias0, bias1 = expand_smalls(per, own, True, ids, [small])
        own0 = lax.all_gather(half0, shard, axis=0, tiled=False)
        own1 = lax.all_gather(e1, shard, axis=0, tiled=False)
        w0 = [own0, hop(own0, "c")]
        w1 = [own1, hop(own1, "c")]
        n1a, qkva, pa, oa = attn_fwd(0, per, pq0, ids, [x0], w0, vec, bias0)
        ya, n2a, ha, ga, *x1s = mlp_fwd(per, pc, pm0, ids, x0, oa, w0, vec, hide)
        x1s = exchange(x1s)
        x1, n1b, qkvb, pb, ob = attn_fwd(1, per, pq1, ids, x1s, w1, vec, bias1)
        res = mlp_both(per, pc, pm1, gmp, ids, x1, ob, w1, vec, hide, cots)
        outs, (dob, dyb, dab, gvm1, df1, dms1), gm1 = res[:4], res[4:10], res[10:12]
        output = join_blocks(ids, exchange(outs))
        dqkvb, gva1, gt1 = attn_bwd(1, dob, qkvb, pb)
        *dx1s, gvx1 = dx_step(1, per, pq1, ids, dqkvb, dyb, x1, w1, vec)
        dx1s = exchange(dx1s)
        gq1 = qkv_grad(per, gqp, ids, n1b, dqkvb, ob, dab)
        dma, dua, df0, dms0, *gm0 = mlp_bwd(per, pc, pm0, gmp0, ids, w0, n2a, ha, ga, dx1s)
        doa, dya, daa, gvm0 = mid_bwd(0, per, pc, pm0, ids, w0, vec, ya, dma, dua)
        dqkva, gva0, gt0 = attn_bwd(0, doa, qkva, pa)
        gq0 = qkv_grad(per, gqp, ids, n1a, dqkva, oa, daa)
        dx0, gvx0 = dx_step(0, per, pq0, ids, dqkva, dya, x0, w0, vec)
        smalls = all_smalls(
            ((gvm0, dms0, df0, gva0, gvx0, gt0), (gvm1, dms1, df1, gva1, gvx1, gt1))
        )
        smalls = lax.psum(smalls, ("y", "core") + shard)
        fq1, fm1, fq0, fm0 = [half_reduce(g, shard) for g in (gq1, gm1, gq0, gm0)]
        new_m = adam_m(0, fm0, adam_m(1, fm1))
        new_q = adam_q(0, fq0, adam_q(1, fq1))

    smalls = smalls.astype(f32).reshape(2, 20, WIDE)
    g_vec = lax.dynamic_slice_in_dim(smalls[:, :12], me * per, per, axis=2)
    g_tab = smalls[:, 12:20].reshape(2 * HEADS, 256)
    g_tab = lax.dynamic_slice_in_dim(g_tab, me * own, own, axis=0)[:, :SPAN]
    flat = [*new_q, *new_m]
    for pos, g in ((4, g_vec), (5, g_tab)):
        flat += adam_math(
            masters[pos], firsts[pos], seconds[pos], g, step_rates[pos], decay_rates[pos]
        )
    return (output.reshape(inputs.shape), dx0.reshape(inputs.shape), *flat, g_vec[:, 7])


def solution(mesh):
    count = mesh.shape["shard"]
    if count == 8:
        mesh = Mesh(mesh.devices.reshape(2, 2, 4, 2), ("y", "core", "z", "x"))
        shard = ("z", "x")
    else:
        mesh = Mesh(mesh.devices.reshape(2, 2, count), ("y", "core", "s"))
        shard = ("s",)
    tokens = P(shard, ("y", "core"), None, None, None)
    params = (P(None, shard, None),) * 4 + (P(None, None, shard), P(shard, None))
    in_specs = (tokens, tokens, P(shard)) + params * 3
    out_specs = (tokens, tokens)
    for spec in params:
        out_specs = out_specs + (spec,) * 3
    out_specs = out_specs + (P(None, shard),)
    return jax.shard_map(
        functools.partial(body, shard),
        mesh=mesh,
        in_specs=in_specs,
        out_specs=out_specs,
        check_vma=False,
    )
```

```python
import functools
import math

import jax
import jax.numpy as jnp
from jax import lax
from jax.experimental import pallas as pl
from jax.experimental.pallas import tpu as pltpu
from jax.sharding import Mesh
from jax.sharding import PartitionSpec as P

HEADS = 16
WIN = 7
SHIFT = 3
ADAM_STEP = 10
WIDE = 512
HIDE = 2048
HEAD_DIM = 32
SPAN = 169
CELLS = 56
SEQ = 4
NWIN = 20
ROWS = NWIN * CELLS
TOK = 1152
GROUP = NWIN // SEQ
BLOCK = 288
PAIR = 2 * CELLS
NPAIR = NWIN // 2
STRIP = 384
NCH = TOK // STRIP
QUADS = 4 * WIN
FOUR = 4 * CELLS
QT = 4 * CELLS
SMALL = 32
HALF = 256
QUAD = 128

bf16 = jnp.bfloat16
f32 = jnp.float32
norm_eps = 1e-05
mask_fill = -100.0
pad_fill = -1e30
beta_one = 0.9
beta_two = 0.999
adam_eps = 1e-08
step_rates = (0.09, 0.35, 0.09, 0.045, 0.5, 2.0)
decay_rates = (0.05, 0.05, 0.05, 0.05, 0.0, 0.0)
scale = HEAD_DIM ** (-0.5)

VM = pl.BlockSpec(memory_space=pltpu.VMEM)
SM = pl.BlockSpec(memory_space=pltpu.SMEM)
HB = pl.BlockSpec(memory_space=pltpu.HBM)
MIB = 1024 * 1024


def call(kernel, outs, in_specs, scratch, flops, moved, out_specs=None, limit=58):
    return pl.pallas_call(
        kernel,
        out_shape=outs,
        in_specs=in_specs,
        out_specs=out_specs or tuple(VM for _ in outs),
        scratch_shapes=scratch,
        compiler_params=pltpu.CompilerParams(vmem_limit_bytes=limit * MIB),
        cost_estimate=pl.CostEstimate(flops=flops, bytes_accessed=moved, transcendentals=0),
    )


def sds(shape, dtype):
    return jax.ShapeDtypeStruct(shape, dtype)


def dot(a, b):
    return lax.dot_general(a, b, (((1,), (0,)), ((), ())), preferred_element_type=f32)


def dot_nt(a, b):
    return lax.dot_general(a, b, (((1,), (1,)), ((), ())), preferred_element_type=f32)


def dot_tn(a, b):
    return lax.dot_general(a, b, (((0,), (0,)), ((), ())), preferred_element_type=f32)


def loop(count, body):
    lax.fori_loop(0, count, lambda i, c: (body(i), c)[1], 0)


def centred(x):
    mean = jnp.mean(x, axis=-1, keepdims=True)
    cen = x - mean
    var = jnp.mean(cen * cen, axis=-1, keepdims=True)
    return cen, lax.rsqrt(var + norm_eps)


def gelu_pair(u):
    phi = 0.5 + 0.5 * lax.erf(u * math.sqrt(0.5))
    e = jnp.exp2((u * u) * (-0.5 / math.log(2.0)))
    return u * phi, phi + (u * (1.0 / math.sqrt(2.0 * math.pi))) * e


def head_masks():
    lane = lax.broadcasted_iota(jnp.int32, (1, 128), 1)
    return [(lane >> 5) == h for h in range(4)]


def stacked(t0, t1, masks):
    left = jnp.concatenate([jnp.where(m, t0, 0.0) for m in masks], axis=0)
    right = jnp.concatenate([jnp.where(m, t1, 0.0) for m in masks], axis=0)
    return jnp.concatenate([left, right], axis=1).astype(bf16)


def diagonal(t0, t1):
    z8 = jnp.zeros((64 - CELLS, 128), f32)
    z64 = jnp.zeros((64, 128), f32)
    left = jnp.concatenate([t0, z8, z64], axis=0)
    right = jnp.concatenate([z64, t1, z8], axis=0)
    return jnp.concatenate([left, right], axis=1).astype(bf16)


def from_diagonal(o):
    return jnp.concatenate([o[:CELLS, :128], o[64 : 64 + CELLS, 128:]], axis=0)


def from_stacked(o, masks):
    total = None
    for h, m in enumerate(masks):
        part = o[h * CELLS : (h + 1) * CELLS]
        part = jnp.concatenate(
            [jnp.where(m, part[:, :128], 0.0), jnp.where(m, part[:, 128:], 0.0)], axis=1
        )
        total = part if total is None else total + part
    return jnp.concatenate([total[:, :128], total[:, 128:]], axis=0)


def swap_windows(src, emit):
    col = lax.broadcasted_iota(jnp.int32, (1, 8, 1), 1)
    first = col < SHIFT

    def image(i):
        tiles = [src[pl.ds((i * 4 + w) * WIN, WIN)] for w in range(4)]
        for r in range(2):
            rows = [
                jnp.concatenate([tiles[(1 - r) * 2 + c][:SHIFT], tiles[r * 2 + c][SHIFT:]], axis=0)
                for c in range(2)
            ]
            for c in range(2):
                emit(i * 4 + r * 2 + c, jnp.where(first, rows[1 - c], rows[c]))

    loop(GROUP, image)


def swap_into(src, dst, keep):
    def emit(w, tile):
        keep[pl.ds(w * WIN, WIN)] = tile

    swap_windows(src, emit)

    def copy(p):
        v = keep[pl.ds(p * 2 * WIN, 2 * WIN)].reshape(PAIR, WIDE)
        dst[pl.ds(pl.multiple_of(p * PAIR, 16), PAIR), :] = v.astype(bf16)

    loop(NPAIR, copy)


def gather_rows(ref, off, per, first, count, c0, width):
    n = count // per
    v = ref[pl.ds(first * n, n), off : off + per, pl.ds(c0, width)]
    return v.reshape(count, width)


class Plan:
    def __init__(self, kind, shards, rows, row0=0):
        self.kind = kind
        self.shards = shards
        self.rows = rows
        self.row0 = row0

    @property
    def count(self):
        return {"near": 8, "wide": 4, "part": 8, "half": 2}[self.kind]

    def scratch(self):
        return [pltpu.VMEM((self.shards, self.rows, WIDE), bf16), pltpu.SemaphoreType.DMA]


def place(ids):
    s, m = ids[0], ids[1]
    return s & 1, s >> 1, m & 1, m >> 1


def start_load(plan, refs, dst, sem, ids, spans=None):
    c, y, x, z = place(ids)
    for lo, hi in spans or ((0, plan.rows),):
        for kc in range(2):
            if plan.kind == "half":
                lane = pl.multiple_of((c ^ kc) * HALF, HALF)
                pltpu.make_async_copy(
                    refs[kc].at[:, plan.row0 + lo : plan.row0 + hi, :],
                    dst.at[:, lo:hi, pl.ds(lane, HALF)],
                    sem,
                ).start()
                continue
            if plan.kind in ("wide", "part"):
                lane = pl.multiple_of((c ^ kc) * HALF, HALF)
                for k in range(8):
                    owner = (z ^ (k & 3)) * 2 + (x ^ (k >> 2))
                    row = 0
                    if plan.kind == "wide":
                        src = refs[kc * 2 + (k >> 2)].at[k & 3]
                    elif k & 3 == 3:
                        src = refs[kc * 4 + (k >> 2) * 2 + 1]
                        row = plan.row0
                    else:
                        src = refs[kc * 4 + (k >> 2) * 2].at[k & 3]
                    pltpu.make_async_copy(
                        src.at[row + lo : row + hi],
                        dst.at[owner, lo:hi, pl.ds(lane, HALF)],
                        sem,
                    ).start()
                continue
            for k in range(16):
                kxy, kz = k >> 2, k & 3
                owner = (z ^ kz) * 2 + (x ^ (kxy & 1))
                lane = pl.multiple_of((c ^ kc) * HALF + (y ^ (kxy >> 1)) * QUAD, QUAD)
                src = refs[kc * 4 + kxy].at[kz, lo:hi]
                pltpu.make_async_copy(src, dst.at[owner, lo:hi, pl.ds(lane, QUAD)], sem).start()


def wait_all(ref, sem):
    pltpu.make_async_copy(ref, ref, sem).wait()


def grad_shapes(plan):
    if plan.kind == "near":
        shape = (4, 4, plan.rows, QUAD)
    elif plan.kind == "wide":
        shape = (2, 2, 2, plan.rows, HALF)
    else:
        shape = (2, plan.shards, plan.rows, QUAD)
    return (sds(shape, bf16), sds(shape, bf16))


def start_grads(plan, src, outs, sem, ids):
    c, y, x, z = place(ids)
    for kc in range(2):
        if plan.kind == "near":
            for k in range(16):
                kxy, kz = k >> 2, k & 3
                owner = (z ^ kz) * 2 + (x ^ (kxy & 1))
                lane = pl.multiple_of((c ^ kc) * HALF + (y ^ (kxy >> 1)) * QUAD, QUAD)
                pltpu.make_async_copy(
                    src.at[owner, :, pl.ds(lane, QUAD)], outs[kc].at[kxy, kz], sem
                ).start()
        elif plan.kind == "wide":
            lane = pl.multiple_of((c ^ kc) * HALF, HALF)
            for k in range(8):
                owner = (z ^ (k & 3)) * 2 + (x ^ (k >> 2))
                pltpu.make_async_copy(
                    src.at[owner, :, pl.ds(lane, HALF)],
                    outs[kc].at[k >> 2, k & 1, (k >> 1) & 1],
                    sem,
                ).start()
        else:
            for part in range(2):
                lane = pl.multiple_of((c ^ kc) * HALF + part * QUAD, QUAD)
                pltpu.make_async_copy(
                    src.at[:, :, pl.ds(lane, QUAD)], outs[kc].at[part], sem
                ).start()


def put_dense(dst, pad):
    def group(i):
        for q in range(4):
            tile = pad[i, :WIN, q * QUAD : (q + 1) * QUAD]
            dst[pl.ds(4 * WIN * i + q, WIN, stride=4), :] = tile

    loop(NWIN * WIN, group)


def prep_kernel(ids, valid_ref, x_ref, cot_ref, x_out, c0, c1, c2, c3, pad):
    s = ids[0]
    pad[...] = jnp.zeros_like(pad)
    x_out[ROWS:, :] = jnp.zeros((TOK - ROWS, WIDE), bf16)

    def xrow(i):
        pad[pl.ds(i * WIN, WIN), :WIN, :] = x_ref[pl.ds(i * WIN, WIN)].astype(f32)

    loop(NWIN, xrow)

    def xpair(i):
        v = pad[pl.ds(i * 2 * WIN, 2 * WIN)].reshape(PAIR, WIDE)
        x_out[pl.ds(pl.multiple_of(i * PAIR, 16), PAIR), :] = v.astype(bf16)

    loop(NPAIR, xpair)

    def image(i):
        v = valid_ref[i].astype(f32)

        def row(r):
            g = i * WIN + r
            for q in range(4):
                tile = cot_ref[pl.ds(4 * WIN * g + q, WIN, stride=4), :]
                pad[g, :WIN, q * QUAD : (q + 1) * QUAD] = tile * v

        loop(WIN, row)

    loop(NWIN, image)
    for k, out in enumerate((c0, c1, c2, c3)):
        d = s ^ k
        v = pad[pl.ds(d * GROUP * WIN, GROUP * WIN)].reshape(GROUP * CELLS, WIDE)
        out[: GROUP * CELLS, :] = v.astype(bf16)
        out[GROUP * CELLS :, :] = jnp.zeros((BLOCK - GROUP * CELLS, WIDE), bf16)


def prep(ids, valid, x, cot):
    block = sds((BLOCK, WIDE), bf16)
    return call(
        prep_kernel,
        (sds((TOK, WIDE), bf16), block, block, block, block),
        [SM, SM, VM, VM],
        [pltpu.VMEM((NWIN * WIN, 8, WIDE), f32)],
        10**6,
        10**7,
        limit=16,
    )(ids, valid, x, cot)


def pack_rows(per, pc, q, p, e, k):
    parts = [(q, 0, per, j * WIDE) for j in range(3)]
    parts += [(p, 0, per, 0), (k, 0, pc, 0)]
    parts += [(e, 0, per, j * WIDE) for j in range(4)]
    return parts


def pack_kernel(per, pc, widths, count, ids, q, p, e, k, vec, tab, *refs):
    outs, tmp = refs[:count], refs[count:]
    c = ids[0] & 1
    y = ids[0] >> 1
    row = 0
    for ref, r0, n, col in pack_rows(per, pc, q, p, e, k):
        at = row
        for out, (lo, hi, wide) in zip(outs, widths):
            if lo <= row < hi:
                off = c * HALF + (y * QUAD if wide == QUAD else 0)
                lane = pl.multiple_of(col + off, QUAD)
                at = row - lo
                out[at : at + n, :] = ref[0, r0 : r0 + n, pl.ds(lane, wide)].astype(bf16)
        row += n
    if tmp:
        small = tmp[0]
        small[...] = jnp.zeros_like(small)
        small[0:12, :per] = vec[0]
        small[12:24, :per] = vec[1]
        small[24 : 24 + tab.shape[0], :SPAN] = tab[...]
        n = outs[-1].shape[0]
        outs[-1][n - SMALL :, :] = small[...].astype(bf16)


def pack(layer, per, pc, pieces, small, ids, masters):
    q, p, e, k, vec, tab = masters
    outs = tuple(sds((hi - lo, wide), bf16) for lo, hi, wide in pieces)
    if small == "row":
        outs = outs[:-1] + (sds((outs[-1].shape[0] + SMALL, HALF), bf16),)
    if small == "own":
        outs = outs + (sds((SMALL, HALF), bf16),)

    def spec(a):
        return pl.BlockSpec((1,) + a.shape[1:], lambda i: (layer, 0, 0))

    def whole(shape):
        return pl.BlockSpec(shape, lambda i: (0,) * len(shape))

    return pl.pallas_call(
        functools.partial(pack_kernel, per, pc, pieces, len(outs)),
        grid=(1,),
        scratch_shapes=[pltpu.VMEM((SMALL, HALF), f32)] if small else [],
        out_shape=outs,
        in_specs=[SM, spec(q), spec(p), spec(e), spec(k), whole(vec.shape), whole(tab.shape)],
        out_specs=tuple(whole(o.shape) for o in outs),
        compiler_params=pltpu.CompilerParams(vmem_limit_bytes=58 * MIB),
        cost_estimate=pl.CostEstimate(flops=10**5, bytes_accessed=3 * 10**6, transcendentals=0),
    )(ids, q, p, e, k, vec, tab)


def onehot(rb, shifted):
    lane = lax.broadcasted_iota(jnp.int32, (1, 1024), 1)
    cb = lane >> 7
    a = lane & 63
    ra = a >> 3
    ca = a & 7

    def moved(v):
        return jnp.where(v >= SHIFT, v - SHIFT, v + WIN - SHIFT) if shifted else v

    rbm = (rb - SHIFT if rb >= SHIFT else rb + WIN - SHIFT) if shifted else rb
    idx = (moved(ra) - rbm + WIN - 1) * (2 * WIN - 1) + moved(ca) - moved(cb) + WIN - 1
    good = (ra < WIN) & (ca < WIN) & (cb < WIN)
    idx = jnp.where(good, idx, -1)
    entry = lax.broadcasted_iota(jnp.int32, (256, 1024), 0)
    return jnp.where(entry == idx, 1.0, 0.0).astype(bf16)


def smalls_kernel(per, own, natural, ids, *refs):
    vec_ref, hide_ref, b0_ref, b1_ref, nat, tmp = refs[-6:]
    shards = WIDE // per
    for k in range(shards):
        if natural:
            nat[k] = refs[0][k].astype(f32)
        else:
            i = ids[1] ^ ((k & 3) * 2 + (k >> 2))
            nat[i] = refs[k >> 2][k & 3, 3 * per :, :].astype(f32)
    for l in range(2):
        rows = jnp.concatenate(
            [nat[i, 12 * l : 12 * l + 12, :per] for i in range(shards)], axis=1
        )
        vec_ref[l] = rows[:8]
        for r in range(4):
            for half in range(2):
                hide_ref[l, 2 * r + half] = rows[8 + r : 9 + r, half * HALF : (half + 1) * HALF]
    for layer in range(2):
        first = layer * (HEADS // own)
        table = jnp.concatenate(
            [nat[first + i, 24 : 24 + own, :] for i in range(HEADS // own)], axis=0
        ).astype(bf16)
        for rb in range(WIN):
            r = dot(table, onehot(rb, layer == 1))
            for cb in range(8):
                tmp[:, rb * 8 + cb, :] = r[:, cb * 128 : (cb + 1) * 128]
        b = lax.broadcasted_iota(jnp.int32, (CELLS, 128), 0)
        lane = lax.broadcasted_iota(jnp.int32, (CELLS, 128), 1)
        a = lane & 63
        gone = (b & 7) == 7
        if layer == 0:
            add = jnp.where(gone, pad_fill, 0.0)
            for h in range(HEADS):
                b0_ref[0, h * CELLS : (h + 1) * CELLS, :] = tmp[h] + add
        else:
            rows = ((b >> 3) < SHIFT) != ((a >> 3) < SHIFT)
            cols = (((b & 7) < SHIFT) != ((a & 7) < SHIFT)) & (lane >= 64)
            for r in range(2):
                cut = cols | rows if r else cols
                add = jnp.where(gone, pad_fill, jnp.where(cut, mask_fill, 0.0))
                for h in range(HEADS):
                    b1_ref[r, h * CELLS : (h + 1) * CELLS, :] = tmp[h] + add


def expand_smalls(per, own, natural, ids, small):
    shards = WIDE // per
    return call(
        functools.partial(smalls_kernel, per, own, natural),
        (
            sds((2, 8, WIDE), f32),
            sds((2, 8, 1, HALF), f32),
            sds((1, HEADS * CELLS, 128), f32),
            sds((2, HEADS * CELLS, 128), f32),
        ),
        [SM] + [VM] * len(small),
        [pltpu.VMEM((shards, SMALL, HALF), f32), pltpu.VMEM((HEADS, CELLS, 128), f32)],
        10**8,
        2 * 10**6,
        limit=16,
    )(ids, *small)


def attn_fwd_kernel(layer, per, plan, *refs):
    ids, nw = refs[0], plan.count
    xs, refs = (refs[1:2], refs[2:]) if layer == 0 else (refs[1:5], refs[5:])
    w_in, vec_ref, bias_ref, refs = refs[:nw], refs[nw], refs[nw + 1], refs[nw + 2 :]
    if layer == 0:
        x_out = xs[0]
        n1_ref, qkv_ref, p_ref, o_ref, w_ref, sem = refs
    else:
        x_out, n1_ref, qkv_ref, p_ref, o_ref, w_ref, sem, one, two = refs
    start_load(plan, w_in, w_ref, sem, ids)
    if layer == 1:
        for k, ref in enumerate(xs):
            w = ids[0] ^ k
            v = ref[: GROUP * CELLS, :].astype(f32).reshape(GROUP, CELLS, WIDE)
            for i in range(GROUP):
                one[pl.ds((i * 4 + w) * WIN, WIN)] = v[i].reshape(WIN, 8, WIDE)

        def put(p):
            v = one[pl.ds(p * 2 * WIN, 2 * WIN)].reshape(PAIR, WIDE)
            x_out[pl.ds(pl.multiple_of(p * PAIR, 16), PAIR), :] = v.astype(bf16)

        loop(NPAIR, put)
        x_out[ROWS:, :] = jnp.zeros((TOK - ROWS, WIDE), bf16)

    gain = vec_ref[layer, 0:1, :]
    shift = vec_ref[layer, 1:2, :]
    if layer == 0:

        def norm(c):
            rows = pl.ds(pl.multiple_of(c * STRIP, STRIP), STRIP)
            cen, rstd = centred(x_out[rows, :].astype(f32))
            n1_ref[rows, :] = (cen * rstd * gain + shift).astype(bf16)

        loop(NCH, norm)
    else:

        def norm(p):
            rows = pl.ds(p * QUADS, QUADS)
            cen, rstd = centred(one[rows].reshape(FOUR, WIDE))
            one[rows] = (cen * rstd * gain + shift).reshape(QUADS, 8, WIDE)

        loop(GROUP, norm)
        swap_into(one, n1_ref, two)
        n1_ref[ROWS:, :] = jnp.zeros((TOK - ROWS, WIDE), bf16)

    wait_all(w_ref, sem)
    for j in range(3):
        for half in range(2):
            c0 = half * 256
            r = dot(n1_ref[...], gather_rows(w_ref, j * per, per, 0, WIDE, c0, 256))
            if j != 1:
                row = 2 if j == 0 else 3
                r = r + vec_ref[layer, row : row + 1, c0 : c0 + 256]
            qkv_ref[:, j * WIDE + c0 : j * WIDE + c0 + 256] = r.astype(bf16)

    masks = head_masks()

    def pair(p):
        rows = pl.ds(pl.multiple_of(p * PAIR, 16), PAIR)
        kind = 0 if layer == 0 else p & 1
        lanes = [slice(t * 128, t * 128 + 128) for t in range(4)]

        def tile(t, part):
            c = part * WIDE + t * 128
            v = qkv_ref[rows, c : c + 128].astype(f32)
            return v[:CELLS], v[CELLS:]

        ks = [stacked(*tile(t, 1), masks) for t in range(4)]
        qs = [diagonal(*tile(t, 0)) for t in range(4)]
        vs = [stacked(*tile(t, 2), masks) for t in range(4)]
        sc = [dot_nt(ks[t], qs[t]) for t in range(4)]
        prs = []
        for t in range(4):
            v = scale * sc[t] + bias_ref[kind, t * QT : (t + 1) * QT, :]
            v = v.reshape(4, CELLS, 128)
            e = jnp.exp(v - jnp.max(v, axis=1, keepdims=True))
            pr = e * (1.0 / jnp.sum(e, axis=1, keepdims=True))
            prs.append(pr.reshape(QT, 128).astype(bf16))
        os = [from_diagonal(dot_tn(prs[t], vs[t])) for t in range(4)]
        for t in range(4):
            p_ref[p, t * QT : (t + 1) * QT, :] = prs[t]
            if layer == 0:
                o_ref[rows, lanes[t]] = os[t].astype(bf16)
            else:
                one[pl.ds(p * 2 * WIN, 2 * WIN), :, lanes[t]] = os[t].reshape(2 * WIN, 8, 128)

    loop(NPAIR, pair)
    if layer == 1:
        swap_into(one, o_ref, two)
    o_ref[ROWS:, :] = jnp.zeros((TOK - ROWS, WIDE), bf16)


def attn_fwd(layer, per, plan, ids, xs, w, vec, bias):
    act = sds((TOK, WIDE), bf16)
    saved = (act, sds((TOK, 3 * WIDE), bf16), sds((NPAIR, HEADS * CELLS, 128), bf16), act)
    kernel = functools.partial(attn_fwd_kernel, layer, per, plan)
    scratch = plan.scratch()
    outs = saved
    if layer == 1:
        tile = pltpu.VMEM((NWIN * WIN, 8, WIDE), f32)
        scratch = scratch + [tile, tile]
        outs = (act,) + saved
    return call(
        kernel,
        outs,
        [SM] + [VM] * len(xs) + [HB] * plan.count + [VM, VM],
        scratch,
        2 * TOK * WIDE * 3 * WIDE,
        12 * 10**6,
        limit=30,
    )(ids, *xs, *w, vec, bias)


def mlp_forward(layer, per, pc, load, x_ref, o_ref, w1, vec_ref, f_ref, y_ref, n2_ref, h_ref, g_ref, emit):
    load()
    for half in range(2):
        c0 = half * 256
        r = dot(o_ref[...], gather_rows(w1, 0, per, 0, WIDE, c0, 256))
        x = x_ref[:, c0 : c0 + 256].astype(f32)
        y_ref[:, c0 : c0 + 256] = x + (r + vec_ref[layer, 4:5, c0 : c0 + 256])
    gain = vec_ref[layer, 5:6, :]
    shift = vec_ref[layer, 6:7, :]

    def norm(c):
        rows = pl.ds(pl.multiple_of(c * STRIP, STRIP), STRIP)
        cen, rstd = centred(y_ref[rows, :])
        n2_ref[rows, :] = (cen * rstd * gain + shift).astype(bf16)

    loop(NCH, norm)

    def act(j):
        c0 = pl.multiple_of((j & 1) * 256, 256)
        v = w1[:, pl.ds(pl.multiple_of(per + pc + (j >> 1) * per, 16), per), pl.ds(c0, 256)]
        u = dot(n2_ref[...], v.reshape(WIDE, 256)) + f_ref[layer, j]
        h, g = gelu_pair(u)
        cols = pl.ds(pl.multiple_of(j * 256, 256), 256)
        h_ref[:, cols] = h.astype(bf16)
        g_ref[:, cols] = g.astype(bf16)

    loop(HIDE // 256, act)
    for half in range(2):
        c0 = half * 256
        v = w1[:, per : per + pc, c0 : c0 + 256].reshape(HIDE, 256)
        r = dot(h_ref[...], v)
        emit(c0, y_ref[:, c0 : c0 + 256] + (r + vec_ref[layer, 7:8, c0 : c0 + 256]))


def mlp_load(plan, w_in, w1, s1, ids):
    start_load(plan, w_in, w1, s1, ids)
    return lambda: wait_all(w1, s1)


def mlp_fwd_kernel(per, pc, plan, *refs):
    nw = plan.count
    ids, x_ref, o_ref = refs[:3]
    w_in, refs = refs[3 : 3 + nw], refs[3 + nw :]
    vec_ref, f_ref, y_ref, n2_ref, h_ref, g_ref, xa, xb, xc, xd, nxt, w1, s1 = refs
    load = mlp_load(plan, w_in, w1, s1, ids)

    def emit(c0, v):
        nxt[:, c0 : c0 + 256] = v

    mlp_forward(
        0, per, pc, load, x_ref, o_ref, w1, vec_ref, f_ref, y_ref, n2_ref, h_ref, g_ref, emit
    )
    size = GROUP * CELLS
    for k, out in enumerate((xa, xb, xc, xd)):
        v = nxt[pl.ds(pl.multiple_of((ids[0] ^ k) * size, 8), size), :]
        out[:size, :] = v.astype(bf16)
        out[size:, :] = jnp.zeros((BLOCK - size, WIDE), bf16)


def mlp_fwd(per, pc, plan, ids, x, o, w, vec, f):
    act = sds((TOK, WIDE), bf16)
    wide = sds((TOK, HIDE), bf16)
    return call(
        functools.partial(mlp_fwd_kernel, per, pc, plan),
        (sds((TOK, WIDE), f32), act, wide, wide) + (sds((BLOCK, WIDE), bf16),) * 4,
        [SM, VM, VM] + [HB] * len(w) + [VM, VM],
        [pltpu.VMEM((TOK, WIDE), f32)] + plan.scratch(),
        2 * TOK * WIDE * (WIDE + 2 * HIDE),
        25 * 10**6,
        limit=40,
    )(ids, x, o, *w, vec, f)


def rows_sum(v):
    return jnp.sum(v, axis=0, keepdims=True)


def mlp_back(per, pc, plan, ids, dm_ref, wc, n2_ref, h_ref, g_ref, du, df_ref, dm_sum, outs, scratch):
    turned, g1, t1 = scratch
    shards = WIDE // per
    turned[...] = n2_ref[...].T
    grows = WIDE // pc

    def step(j):
        cols = pl.ds(pl.multiple_of(j * WIDE, WIDE), WIDE)
        w = wc[pl.ds(j * grows, grows)].reshape(WIDE, WIDE)
        dm = dm_ref[...]
        dh = dot_nt(dm, w)
        d = (dh * g_ref[:, cols].astype(f32)).astype(bf16)
        du[:, cols] = d
        total = rows_sum(d.astype(f32))
        for half in range(2):
            df_ref[2 * j + half] = total[:, half * 256 : half * 256 + 256]
        gc = dot_tn(h_ref[:, cols], dm)
        g1[pl.ds(j * grows, grows), 0:pc, :] = gc.astype(bf16).reshape(grows, pc, WIDE)
        ge = dot(turned[...], d)
        g1[:, pl.ds(pl.multiple_of(pc + j * per, 16), per), :] = ge.astype(bf16).reshape(
            shards, per, WIDE
        )

    loop(HIDE // WIDE, step)
    start_grads(plan, g1, outs, t1, ids)
    dm_sum[...] = rows_sum(dm_ref[...].astype(f32))
    return lambda: wait_all(g1, t1)


def mlp_back_scratch(gplan):
    return [pltpu.VMEM((WIDE, TOK), bf16)] + gplan.scratch()


def mlp_back_outs(gplan):
    outs = (
        sds((TOK, WIDE), bf16),
        sds((TOK, HIDE), bf16),
        sds((8, 1, 256), f32),
        sds((1, WIDE), f32),
    )
    return outs + grad_shapes(gplan)


def mlp_both_kernel(per, pc, plan, gplan, *refs):
    nw = plan.count
    ids, x_ref, o_ref = refs[:3]
    w_in, refs = refs[3 : 3 + nw], refs[3 + nw :]
    vec_ref, f_ref = refs[:2]
    cots, blocks, refs = refs[2:6], refs[6:10], refs[10:]
    do_ref, dy_ref, da_ref, gv_ref, df_ref, dm_sum = refs[:6]
    outs, refs = refs[6:8], refs[8:]
    y_ref, dm_ref, du, n2_ref, h_ref, g_ref, nxt, tmp, w1, s1 = refs[:10]
    scratch = refs[10:]
    load = mlp_load(plan, w_in, w1, s1, ids)

    def emit(c0, v):
        nxt[:, c0 : c0 + 256] = v

    mlp_forward(
        1, per, pc, load, x_ref, o_ref, w1, vec_ref, f_ref, y_ref, n2_ref, h_ref, g_ref, emit
    )
    s = ids[0]
    size = GROUP * CELLS
    for k, out in enumerate(blocks):
        for i in range(GROUP):
            row = pl.multiple_of((i * 4 + (s ^ k)) * CELLS, 8)
            tmp[i * CELLS : (i + 1) * CELLS, :] = nxt[pl.ds(row, CELLS), :]
        out[:size, :] = tmp[:size, :].astype(bf16)
        out[size:, :] = jnp.zeros((BLOCK - size, WIDE), bf16)
    for k, ref in enumerate(cots):
        v = ref[:size, :].astype(f32)
        for i in range(GROUP):
            row = pl.multiple_of((i * 4 + (s ^ k)) * CELLS, 8)
            nxt[pl.ds(row, CELLS), :] = v[i * CELLS : (i + 1) * CELLS, :]
    dm_ref[:ROWS, :] = nxt[:ROWS, :].astype(bf16)
    dm_ref[ROWS:, :] = jnp.zeros((TOK - ROWS, WIDE), bf16)
    wc = w1.at[:, per : per + pc, :]
    done = mlp_back(
        per, pc, gplan, ids, dm_ref, wc, n2_ref, h_ref, g_ref, du, df_ref, dm_sum, outs, scratch
    )
    mid_body(1, per, pc, w1, vec_ref, y_ref, dm_ref, du, do_ref, dy_ref, da_ref, gv_ref, nxt)
    done()


def mlp_both(per, pc, plan, gplan, ids, x, o, w, vec, f, cots):
    block = sds((BLOCK, WIDE), bf16)
    outs = (block,) * 4 + mid_outs() + mlp_back_outs(gplan)[2:]
    scratch = [
        pltpu.VMEM((TOK, WIDE), f32),
        pltpu.VMEM((TOK, WIDE), bf16),
        pltpu.VMEM((TOK, HIDE), bf16),
        pltpu.VMEM((TOK, WIDE), bf16),
        pltpu.VMEM((TOK, HIDE), bf16),
        pltpu.VMEM((TOK, HIDE), bf16),
        pltpu.VMEM((TOK, WIDE), f32),
        pltpu.VMEM((BLOCK, WIDE), f32),
    ]
    return call(
        functools.partial(mlp_both_kernel, per, pc, plan, gplan),
        outs,
        [SM, VM, VM] + [HB] * len(w) + [VM] * 6,
        scratch + plan.scratch() + mlp_back_scratch(gplan),
        5 * TOK * WIDE * (WIDE + 2 * HIDE),
        25 * 10**6,
        (VM,) * 10 + (HB,) * 2,
        50,
    )(ids, x, o, *w, vec, f, *cots)


def mlp_bwd_kernel(per, pc, plan, gplan, *refs):
    nw = plan.count
    ids, w_in, refs = refs[0], refs[1 : 1 + nw], refs[1 + nw :]
    n2_ref, h_ref, g_ref = refs[:3]
    grads, refs = refs[3:7], refs[7:]
    dm_ref, du, df_ref, dm_sum = refs[:4]
    outs, refs = refs[4:6], refs[6:]
    tmp, w1, s1 = refs[:3]
    scratch = refs[3:]
    start_load(plan, w_in, w1, s1, ids, ((per, per + pc),))
    s = ids[0]
    size = GROUP * CELLS
    for k, ref in enumerate(grads):
        tmp[pl.ds(pl.multiple_of((s ^ k) * size, 8), size), :] = ref[:size, :].astype(f32)
    dm_ref[:ROWS, :] = tmp[:ROWS, :].astype(bf16)
    dm_ref[ROWS:, :] = jnp.zeros((TOK - ROWS, WIDE), bf16)
    wc = w1.at[:, per : per + pc, :]
    wait_all(wc, s1)
    mlp_back(
        per, pc, gplan, ids, dm_ref, wc, n2_ref, h_ref, g_ref, du, df_ref, dm_sum, outs, scratch
    )()


def mlp_bwd(per, pc, plan, gplan, ids, w, n2, h, g, grads):
    return call(
        functools.partial(mlp_bwd_kernel, per, pc, plan, gplan),
        mlp_back_outs(gplan),
        [SM] + [HB] * len(w) + [VM] * 7,
        [pltpu.VMEM((TOK, WIDE), f32)] + plan.scratch() + mlp_back_scratch(gplan),
        3 * TOK * WIDE * 2 * HIDE,
        25 * 10**6,
        (VM,) * 4 + (HB,) * 2,
        limit=48,
    )(ids, *w, n2, h, g, *grads)


def mid_kernel(layer, per, pc, plan, *refs):
    nw = plan.count
    ids, w_in, refs = refs[0], refs[1 : 1 + nw], refs[1 + nw :]
    vec_ref, y_ref, dm_ref, du, do_ref, dy_ref, da_ref, gv_ref, dn2, w1, s1, s2 = refs
    spans = ((0, per), (per + pc, 5 * per + pc))
    start_load(plan, w_in, w1, s1, ids, spans[:1])
    start_load(plan, w_in, w1, s2, ids, spans[1:])
    for (lo, hi), sem in zip(spans, (s1, s2)):
        wait_all(w1.at[:, lo:hi, :], sem)
    mid_body(layer, per, pc, w1, vec_ref, y_ref, dm_ref, du, do_ref, dy_ref, da_ref, gv_ref, dn2)


def mid_outs():
    act = sds((TOK, WIDE), bf16)
    return (act, sds((TOK, WIDE), f32), act, sds((8, WIDE), f32))


def mid_body(layer, per, pc, w1, vec_ref, y_ref, dm_ref, du, do_ref, dy_ref, da_ref, gv_ref, dn2):
    gv_ref[...] = jnp.zeros_like(gv_ref)
    for half in range(2):
        total = None
        for c in range(4):
            w = gather_rows(w1, per + pc + c * per, per, half, 256, 0, WIDE)
            part = dot_nt(du[:, c * WIDE : (c + 1) * WIDE], w)
            total = part if total is None else total + part
        dn2[:, half * 256 : half * 256 + 256] = total
    gain = vec_ref[layer, 5:6, :]

    def norm(c):
        rows = pl.ds(pl.multiple_of(c * STRIP, STRIP), STRIP)
        cen, rstd = centred(y_ref[rows, :])
        xhat = cen * rstd
        dn = dn2[rows, :]
        gv_ref[5:6, :] += rows_sum(dn * xhat)
        gv_ref[6:7, :] += rows_sum(dn)
        dx = dn * gain
        m1 = jnp.mean(dx, axis=-1, keepdims=True)
        m2 = jnp.mean(dx * xhat, axis=-1, keepdims=True)
        dy = dm_ref[rows, :].astype(f32) + rstd * (dx - m1 - xhat * m2)
        dy_ref[rows, :] = dy
        da = dy.astype(bf16)
        gv_ref[4:5, :] += rows_sum(da.astype(f32))
        da_ref[rows, :] = da

    loop(NCH, norm)
    for half in range(2):
        c0 = half * 256
        w = gather_rows(w1, 0, per, half, 256, 0, WIDE)
        do_ref[:, c0 : c0 + 256] = dot_nt(da_ref[...], w).astype(bf16)


def mid_bwd(layer, per, pc, plan, ids, w, vec, y, dm, du):
    return call(
        functools.partial(mid_kernel, layer, per, pc, plan),
        mid_outs(),
        [SM] + [HB] * len(w) + [VM] * 4,
        [pltpu.VMEM((TOK, WIDE), f32)] + plan.scratch() + [pltpu.SemaphoreType.DMA],
        2 * TOK * WIDE * (WIDE + HIDE),
        16 * 10**6,
        limit=34,
    )(ids, *w, vec, y, dm, du)


def attn_bwd_kernel(layer, do_ref, qkv_ref, p_ref, dqkv, gv_ref, gt_ref, *rest):
    dsum = rest[0]
    if layer == 1:
        one, two = rest[1:]

        def widen(p):
            v = do_ref[pl.ds(pl.multiple_of(p * PAIR, 16), PAIR), :].astype(f32)
            one[pl.ds(p * 2 * WIN, 2 * WIN)] = v.reshape(2 * WIN, 8, WIDE)

        loop(NPAIR, widen)

        def emit(w, tile):
            two[pl.ds(w * WIN, WIN)] = tile

        swap_windows(one, emit)
    gv_ref[...] = jnp.zeros_like(gv_ref)
    dsum[...] = jnp.zeros_like(dsum)
    dqkv[ROWS:, :] = jnp.zeros((TOK - ROWS, 3 * WIDE), bf16)
    masks = head_masks()

    def pair(p):
        rows = pl.ds(pl.multiple_of(p * PAIR, 16), PAIR)
        def tile(t, part):
            c = part * WIDE + t * 128
            v = qkv_ref[rows, c : c + 128].astype(f32)
            return v[:CELLS], v[CELLS:]

        def grad(t):
            c = t * 128
            if layer == 0:
                d = do_ref[rows, c : c + 128].astype(f32)
            else:
                d = two[pl.ds(p * 2 * WIN, 2 * WIN), :, c : c + 128].reshape(PAIR, 128)
            return d[:CELLS], d[CELLS:]

        four = range(4)
        vs = [stacked(*tile(t, 2), masks) for t in four]
        dd = [diagonal(*grad(t)) for t in four]
        ks = [stacked(*tile(t, 1), masks) for t in four]
        qs = [diagonal(*tile(t, 0)) for t in four]
        pb = [p_ref[p, t * QT : (t + 1) * QT, :] for t in four]
        dp = [dot_nt(vs[t], dd[t]) for t in four]
        dv = [from_stacked(dot(pb[t], dd[t]), masks).astype(bf16) for t in four]
        ds = []
        for t in four:
            pf = pb[t].astype(f32).reshape(4, CELLS, 128)
            g = dp[t].reshape(4, CELLS, 128)
            tot = jnp.sum(g * pf, axis=1, keepdims=True)
            ds.append((pf * (g - tot)).reshape(QT, 128).astype(bf16))
        dq = [(scale * from_diagonal(dot_tn(ds[t], ks[t]))).astype(bf16) for t in four]
        dk = [(scale * from_stacked(dot(ds[t], qs[t]), masks)).astype(bf16) for t in four]
        for t in four:
            c = t * 128
            dsum[4 * t : 4 * t + 4] += ds[t].astype(f32).reshape(4, CELLS, 128)
            dqkv[rows, c : c + 128] = dq[t]
            dqkv[rows, WIDE + c : WIDE + c + 128] = dk[t]
            dqkv[rows, 2 * WIDE + c : 2 * WIDE + c + 128] = dv[t]
            gv_ref[2:3, c : c + 128] += rows_sum(dq[t].astype(f32))
            gv_ref[3:4, c : c + 128] += rows_sum(dv[t].astype(f32))

    loop(NPAIR, pair)
    total = jnp.zeros((HEADS, 256), f32)
    for rb in range(WIN):
        x = jnp.concatenate([dsum[:, rb * 8 + cb, :] for cb in range(8)], axis=1)
        hi = x.astype(bf16)
        lo = (x - hi.astype(f32)).astype(bf16)
        oh = onehot(rb, layer == 1)
        total = total + (dot_nt(hi, oh) + dot_nt(lo, oh))
    gt_ref[...] = total


def attn_bwd(layer, do, qkv, probs):
    tile = pltpu.VMEM((NWIN * WIN, 8, WIDE), f32)
    return call(
        functools.partial(attn_bwd_kernel, layer),
        (sds((TOK, 3 * WIDE), bf16), sds((8, WIDE), f32), sds((HEADS, 256), f32)),
        [VM] * 3,
        [pltpu.VMEM((HEADS, CELLS, 128), f32)] + [tile, tile] * layer,
        2 * TOK * WIDE * 3 * WIDE,
        12 * 10**6,
        limit=28,
    )(do, qkv, probs)


def qkv_grad_kernel(per, plan, ids, n1_ref, dqkv, o_ref, da_ref, keep, send, turned, gq, sem):
    shards = WIDE // per
    turned[...] = o_ref[...].T
    for half in range(2):
        c0 = half * 256
        g = dot(turned[...], da_ref[:, c0 : c0 + 256])
        gq[:, 3 * per : 4 * per, c0 : c0 + 256] = g.astype(bf16).reshape(shards, per, 256)
    turned[...] = n1_ref[...].T
    for j in range(3):
        for half in range(2):
            c0 = half * 256
            g = dot(turned[...], dqkv[:, j * WIDE + c0 : j * WIDE + c0 + 256])
            gq[:, j * per : (j + 1) * per, c0 : c0 + 256] = g.astype(bf16).reshape(
                shards, per, 256
            )
    start_grads(plan, gq, (keep, send), sem, ids)
    wait_all(gq, sem)


def qkv_grad(per, plan, ids, n1, dqkv, o, da):
    return call(
        functools.partial(qkv_grad_kernel, per, plan),
        grad_shapes(plan),
        [SM, VM, VM, VM, VM],
        [pltpu.VMEM((WIDE, TOK), bf16)] + plan.scratch(),
        2 * TOK * WIDE * 4 * WIDE,
        9 * 10**6,
        (HB, HB),
        limit=24,
    )(ids, n1, dqkv, o, da)


def dx_kernel(layer, per, plan, *refs):
    nw = plan.count
    ids, dqkv, dy_ref, x_ref = refs[:4]
    w_in, vec_ref, refs = refs[4 : 4 + nw], refs[4 + nw], refs[5 + nw :]
    nout = 1 if layer == 0 else 4
    dx_refs, gv_ref, refs = refs[:nout], refs[nout], refs[nout + 1 :]
    dn, one, w_ref, sem = refs
    start_load(plan, w_in, w_ref, sem, ids)
    gv_ref[...] = jnp.zeros_like(gv_ref)
    wait_all(w_ref, sem)
    for half in range(2):
        total = None
        for c in range(3):
            w = gather_rows(w_ref, c * per, per, half, 256, 0, WIDE)
            part = dot_nt(dqkv[:, c * WIDE : (c + 1) * WIDE], w)
            total = part if total is None else total + part
        dn[:, half * 256 : half * 256 + 256] = total
    gain = vec_ref[layer, 0:1, :]
    if layer == 1:

        def widen_dn(p):
            v = dn[pl.ds(pl.multiple_of(p * PAIR, 8), PAIR), :].astype(bf16).astype(f32)
            one[pl.ds(p * 2 * WIN, 2 * WIN)] = v.reshape(2 * WIN, 8, WIDE)

        loop(NPAIR, widen_dn)

        def emit_dn(w, tile):
            dn[pl.ds(pl.multiple_of(w * CELLS, 8), CELLS), :] = tile.reshape(CELLS, WIDE)

        swap_windows(one, emit_dn)

    def norm(p):
        rows = pl.ds(pl.multiple_of(p * FOUR, 16), FOUR)
        cen, rstd = centred(x_ref[rows, :].astype(f32))
        xhat = cen * rstd
        d = dn[rows, :]
        gv_ref[0:1, :] += rows_sum(d * xhat)
        gv_ref[1:2, :] += rows_sum(d)
        dx = d * gain
        m1 = jnp.mean(dx, axis=-1, keepdims=True)
        m2 = jnp.mean(dx * xhat, axis=-1, keepdims=True)
        out = dy_ref[rows, :] + rstd * (dx - m1 - xhat * m2)
        one[pl.ds(p * QUADS, QUADS)] = out.reshape(QUADS, 8, WIDE)

    loop(GROUP, norm)
    if layer == 0:
        put_dense(dx_refs[0], one)
    else:
        s = ids[0]
        size = GROUP * CELLS
        for k, out in enumerate(dx_refs):
            for i in range(GROUP):
                tile = one[pl.ds((i * 4 + (s ^ k)) * WIN, WIN)]
                dn[i * CELLS : (i + 1) * CELLS, :] = tile.reshape(CELLS, WIDE)
            out[:size, :] = dn[:size, :].astype(bf16)
            out[size:, :] = jnp.zeros((BLOCK - size, WIDE), bf16)


def dx_step(layer, per, plan, ids, dqkv, dy, x, w, vec):
    if layer == 0:
        outs = (sds((NWIN * WIN * WIN * 4, QUAD), f32),)
    else:
        outs = (sds((BLOCK, WIDE), bf16),) * 4
    tile = pltpu.VMEM((NWIN * WIN, 8, WIDE), f32)
    return call(
        functools.partial(dx_kernel, layer, per, plan),
        outs + (sds((8, WIDE), f32),),
        [SM, VM, VM, VM] + [HB] * plan.count + [VM],
        [pltpu.VMEM((TOK, WIDE), f32), tile] + plan.scratch(),
        2 * TOK * WIDE * 3 * WIDE,
        12 * 10**6,
        limit=28,
    )(ids, dqkv, dy, x, *w, vec)


def join_kernel(ids, xa, xb, xc, xd, out_ref, pad):
    s = ids[0]
    size = GROUP * CELLS
    for k, ref in enumerate((xa, xb, xc, xd)):
        v = ref[:size, :].astype(f32).reshape(GROUP * WIN, 8, WIDE)
        pad[pl.ds((s ^ k) * GROUP * WIN, GROUP * WIN)] = v
    put_dense(out_ref, pad)


def join_blocks(ids, blocks):
    return call(
        join_kernel,
        (sds((NWIN * WIN * WIN * 4, QUAD), f32),),
        [SM] + [VM] * 4,
        [pltpu.VMEM((NWIN * WIN, 8, WIDE), f32)],
        10**6,
        5 * 10**6,
        limit=58,
    )(ids, *blocks)[0]


def hop(value, way):
    axes = {"c": ("core",), "cy": ("y", "core"), "xy": ("y", "x")}.get(way, (way[0],))
    mask = {"z2": 2, "z3": 3, "cy": 3, "xy": 3}.get(way, 1)
    size = math.prod(lax.axis_size(a) for a in axes)
    return lax.ppermute(value, axes, [(i, i ^ mask) for i in range(size)])


def tie(*values):
    return lax.optimization_barrier(values)


def exchange(blocks):
    return [blocks[0]] + [hop(b, way) for b, way in zip(blocks[1:], ("c", "y", "cy"))]


def swap_all(value, axes):
    return lax.all_to_all(value, axes, 0, 0)


def share(value, axes):
    n = math.prod(lax.axis_size(a) for a in axes)
    return swap_all(jnp.stack([value] * n), axes)


def gather_c(gs):
    return gs + [hop(g, "c") for g in gs]


def add16(*terms):
    total = terms[0].astype(f32)
    for t in terms[1:]:
        total = total + t.astype(f32)
    return total.astype(bf16)


def near_xy(keep, r):
    own, *others = [add16(keep[k], r[k]) for k in range(4)]
    return own, [hop(t, way) for t, way in zip(others, ("x", "y", "xy"))]


def near_z(own, got):
    own, *others = [add16(own[k], *[g[k] for g in got]) for k in range(4)]
    return own, [hop(t, way) for t, way in zip(others, ("z1", "z2", "z3"))]


def near_spread(own, got):
    f = add16(own, *got)
    return [f, hop(f, "y"), hop(f, "c"), hop(f, "cy")]


def step_core(grads, r):
    keep = grads[0]
    return add16(keep[0], r[0]), hop(add16(keep[1], r[1]), "x")


def step_next(own, r, way):
    return add16(own[0], r[0]), hop(add16(own[1], r[1]), way)


def step_last(own, r):
    f = add16(own, r)
    return f, hop(f, "y")


def step_spread(f, r):
    f = add16(f, r)
    return [f, hop(f, "c")]


def half_reduce(grads, shard):
    total = add16(grads[0], hop(grads[1], "c"))
    total = total.reshape((-1,) + total.shape[2:])
    f = lax.psum_scatter(total, ("y",) + shard, scatter_dimension=0, tiled=False)
    return [f, hop(f, "y"), hop(f, "c"), hop(f, "cy")]


def adam_math(weight, moment_one, moment_two, gradient, step_rate, decay_rate):
    first_new = beta_one * moment_one + (1.0 - beta_one) * gradient
    second_new = beta_two * moment_two + (1.0 - beta_two) * gradient * gradient
    correct_one = 1.0 - beta_one**ADAM_STEP
    correct_two = 1.0 - beta_two**ADAM_STEP
    update = first_new / correct_one / (jnp.sqrt(second_new / correct_two) + adam_eps)
    weight_new = weight * (1.0 - step_rate * decay_rate) - step_rate * update
    return (first_new, second_new, weight_new)


def adam_kernel(segments, members, old, count, ids, *refs):
    n = len(members)
    blocks, refs = refs[:count], refs[count:]
    ins, outs, tot = refs[: 3 * n], refs[3 * n + old : 6 * n + old], refs[-1]
    c, y, x, z = place(ids)
    for k, ref in enumerate(blocks):
        if count == 2:
            lane = pl.multiple_of((c ^ k) * HALF, HALF)
        else:
            lane = pl.multiple_of((c ^ (k >> 1)) * HALF + (y ^ (k & 1)) * QUAD, QUAD)
        tot[:, pl.ds(lane, WIDE // count)] = ref[...].astype(f32)
    for row, m, count, col in segments:
        at = (0, slice(0, count), slice(col, col + WIDE))
        pos = members[m]
        new = adam_math(
            ins[3 * m][at],
            ins[3 * m + 1][at],
            ins[3 * m + 2][at],
            tot[row : row + count, :],
            step_rates[pos],
            decay_rates[pos],
        )
        for k in range(3):
            outs[3 * m + k][at] = new[k]


def adam_step(layer, segments, members, ids, blocks, params, old):
    ins = [a for pos in members for a in (params[0][pos], params[1][pos], params[2][pos])]
    rows = blocks[0].shape[0]

    def spec(a):
        return pl.BlockSpec((1,) + a.shape[1:], lambda i: (layer, 0, 0))

    outs = tuple(sds(a.shape, f32) for a in ins)
    held = list(old or [])
    base = 1 + len(blocks) + len(ins)
    return pl.pallas_call(
        functools.partial(adam_kernel, segments, members, len(held), len(blocks)),
        grid=(1,),
        out_shape=outs,
        in_specs=[SM]
        + [pl.BlockSpec(b.shape, lambda i: (0, 0)) for b in blocks]
        + [spec(a) for a in ins]
        + [HB] * len(held),
        out_specs=tuple(spec(a) for a in ins),
        scratch_shapes=[pltpu.VMEM((rows, WIDE), f32)],
        input_output_aliases={base + k: k for k in range(len(held))},
        compiler_params=pltpu.CompilerParams(vmem_limit_bytes=58 * MIB),
        cost_estimate=pl.CostEstimate(
            flops=20 * rows * WIDE, bytes_accessed=24 * rows * WIDE, transcendentals=0
        ),
    )(ids, *blocks, *ins, *held)


def body(shard, *args):
    inputs, cotangent, image_valid = args[:3]
    masters, firsts, seconds = args[3:9], args[9:15], args[15:21]
    params = (masters, firsts, seconds)
    per = masters[0].shape[1]
    pc = masters[3].shape[1]
    own = masters[5].shape[0]
    shards = WIDE // per
    fast = len(shard) == 2
    seq = lax.axis_index(("y", "core")).astype(jnp.int32)
    me = lax.axis_index(shard).astype(jnp.int32)
    ids = jnp.stack([seq, me])

    nq, nm = 3 * per, 5 * per + pc
    whole = ((0, nq + nm, HALF),)
    wide = "wide" if fast else "half"
    pq0 = Plan(wide, shards, nq)
    pm0 = Plan("near" if fast else "half", shards, nm, 0 if fast else nq)
    part = "part" if fast else "half"
    pq1, pm1 = Plan(part, shards, nq), Plan(part, shards, nm, nq)
    gqp, gmp = Plan(wide, shards, 4 * per), Plan(wide, shards, 4 * per + pc)
    gmp0 = Plan("near" if fast else "half", shards, 4 * per + pc)
    x_in = inputs.reshape(NWIN * WIN, WIN, WIDE)
    cot = cotangent.reshape(NWIN * WIN * WIN * 4, QUAD)
    seg_q = [(j * per, 0, per, j * WIDE) for j in range(3)] + [(3 * per, 1, per, 0)]
    seg_m = [(0, 1, pc, 0)] + [(pc + j * per, 0, per, j * WIDE) for j in range(4)]

    def adam_q(layer, blocks, old=None):
        return adam_step(layer, seg_q, (0, 1), ids, blocks, params, old)

    def adam_m(layer, blocks, old=None):
        return adam_step(layer, seg_m, (2, 3), ids, blocks, params, old)

    def all_smalls(parts):
        rows = []
        for gvm, dms, df, gva, gvx, gt in parts:
            total = gvm + gva + gvx
            rows += [total[:7], dms, df.reshape(4, WIDE), gt.reshape(8, WIDE)]
        return jnp.concatenate(rows, axis=0).astype(bf16)

    if fast:
        em0, eq0 = pack(0, per, pc, ((nq, nq + nm, QUAD), (0, nq, HALF)), "row", ids, masters)
        zq = [hop(eq0, "z1"), hop(eq0, "z2")]
        zm = [hop(em0, "z1"), hop(em0, "z2")]
        x0, *cots = prep(ids, image_valid, x_in, cot)
        zq, zm, x0 = tie(zq, zm, x0)
        zq.append(hop(zq[1], "z1"))
        zm.append(hop(zm[1], "z1"))
        (e1,) = pack(1, per, pc, whole, "", ids, masters)
        zq, zm, e1 = tie(zq, zm, e1)
        g = jnp.stack([eq0] + zq)
        gx = hop(g, "x")
        gm = jnp.stack([em0] + zm)
        wm0 = [gm] + [hop(gm, way) for way in ("x", "y", "xy")]
        z1, z2 = hop(e1, "z1"), hop(e1, "z2")
        vec, hide, bias0, bias1 = expand_smalls(per, own, False, ids, [g, gx])
        wq0 = gather_c([g, gx])
        n1a, qkva, pa, oa = attn_fwd(0, per, pq0, ids, [x0], wq0, vec, bias0)
        oa, z1, z2, wm0 = tie(oa, z1, z2, wm0)
        z3 = hop(z2, "z1")
        gaq = jnp.stack([v[:nq] for v in (e1, z1, z2)])
        gam = jnp.stack([v[nq:] for v in (e1, z1, z2)])
        gaqx = hop(gaq, "x")
        wm0 = gather_c(wm0)
        wm0, gaq, gam = tie(wm0, gaq, gam)
        gamx = hop(gam, "x")
        gaqc, gamc = hop(gaq, "c"), hop(gam, "c")
        ya, n2a, ha, ga, *x1s = mlp_fwd(per, pc, pm0, ids, x0, oa, wm0, vec, hide)
        x1s, z3, gaqx, gaqc, gamc = tie(x1s, z3, gaqx, gaqc, gamc)
        x1s = exchange(x1s)
        z3x = hop(z3, "x")
        z3c, gaqxc = hop(z3, "c"), hop(gaqx, "c")
        x1s, z3x, z3c, gaqxc = tie(x1s, z3x, z3c, gaqxc)
        z3xc = hop(z3x, "c")
        w1q = [gaq, z3, gaqx, z3x, gaqc, z3c, gaqxc, z3xc]
        cots = exchange(cots)
        x1, n1b, qkvb, pb, ob = attn_fwd(1, per, pq1, ids, x1s, w1q, vec, bias1)
        ob, cots, gamx = tie(ob, cots, gamx)
        w1 = [gam, z3, gamx, z3x, gamc, z3c, hop(gamx, "c"), z3xc]
        res = mlp_both(per, pc, pm1, gmp, ids, x1, ob, w1, vec, hide, cots)
        outs, (dob, dyb, dab, gvm1, df1, dms1), gm1 = res[:4], res[4:10], res[10:12]
        rm1 = hop(gm1[1], "c")
        outs = exchange(outs)
        dqkvb, gva1, gt1 = attn_bwd(1, dob, qkvb, pb)
        dqkvb, rm1, outs = tie(dqkvb, rm1, outs)
        sm1 = step_core(gm1, rm1)
        *dx1s, gvx1 = dx_step(1, per, pq1, ids, dqkvb, dyb, x1, w1q, vec)
        dx1s, dqkvb = tie(dx1s, dqkvb)
        dx1s = exchange(dx1s)
        gq1 = qkv_grad(per, gqp, ids, n1b, dqkvb, ob, dab)
        gq1, dx1s, sm1 = tie(gq1, dx1s, sm1)
        rq1 = hop(gq1[1], "c")
        sm1 = step_next(*sm1, "z1")
        dma, dua, df0, dms0, *gm0 = mlp_bwd(per, pc, pm0, gmp0, ids, wm0, n2a, ha, ga, dx1s)
        dua, rq1, sm1, gm0 = tie(dua, rq1, sm1, gm0)
        rm0 = hop(gm0[1], "c")
        sq1 = step_core(gq1, rq1)
        sm1 = step_next(*sm1, "z2")
        doa, dya, daa, gvm0 = mid_bwd(0, per, pc, pm0, ids, wm0, vec, ya, dma, dua)
        doa, rm0, sq1, sm1 = tie(doa, rm0, sq1, sm1)
        sm0 = near_xy(gm0[0], rm0)
        sq1 = step_next(*sq1, "z1")
        sm1 = step_last(*sm1)
        dqkva, gva0, gt0 = attn_bwd(0, doa, qkva, pa)
        dqkva, sq1, sm1 = tie(dqkva, sq1, sm1)
        sq1 = step_next(*sq1, "z2")
        fm1 = step_spread(*sm1)
        gq0 = qkv_grad(per, gqp, ids, n1a, dqkva, oa, daa)
        gq0, sm0, sq1, fm1, outs = tie(gq0, sm0, sq1, fm1, outs)
        rq0 = hop(gq0[1], "c")
        sm0 = near_z(*sm0)
        output = join_blocks(ids, outs)
        output, rq0 = tie(output, rq0)
        sq0 = step_core(gq0, rq0)
        sq1 = step_last(*sq1)
        dx0, gvx0 = dx_step(0, per, pq0, ids, dqkva, dya, x0, wq0, vec)
        dx0, gvx0, sq0, sm0, sq1 = tie(dx0, gvx0, sq0, sm0, sq1)
        sq0 = step_next(*sq0, "z1")
        fm0 = near_spread(*sm0)
        smalls = all_smalls(
            ((gvm0, dms0, df0, gva0, gvx0, gt0), (gvm1, dms1, df1, gva1, gvx1, gt1))
        )
        fq1 = step_spread(*sq1)
        sc = hop(smalls, "c")
        new_m = adam_m(1, fm1)
        new_m, sq0, sc, fq1 = tie(new_m, sq0, sc, fq1)
        sq0 = step_next(*sq0, "z2")
        smalls = add16(smalls, sc)
        sc = hop(smalls, "x")
        new_q = adam_q(1, fq1)
        new_q, sq0, fm0, sc = tie(new_q, sq0, fm0, sc)
        sq0 = step_last(*sq0)
        smalls = add16(smalls, sc)
        sc = hop(smalls, "z1")
        new_m = adam_m(0, fm0, new_m)
        new_m, sq0, sc = tie(new_m, sq0, sc)
        fq0 = step_spread(*sq0)
        smalls = add16(smalls, sc)
        sc = hop(smalls, "z2")
        fq0, sc = tie(fq0, sc)
        smalls = add16(smalls, sc)
        sc = hop(smalls, "y")
        new_q = adam_q(0, fq0, new_q)
        new_q, sc = tie(new_q, sc)
        smalls = add16(smalls, sc)
    else:
        half0, small = pack(0, per, pc, whole, "own", ids, masters)
        (e1,) = pack(1, per, pc, whole, "", ids, masters)
        x0, *cots = prep(ids, image_valid, x_in, cot)
        cots = exchange(cots)
        small = lax.all_gather(small, shard, axis=0, tiled=False)
        vec, hide, bias0, bias1 = expand_smalls(per, own, True, ids, [small])
        own0 = lax.all_gather(half0, shard, axis=0, tiled=False)
        own1 = lax.all_gather(e1, shard, axis=0, tiled=False)
        w0 = [own0, hop(own0, "c")]
        w1 = [own1, hop(own1, "c")]
        n1a, qkva, pa, oa = attn_fwd(0, per, pq0, ids, [x0], w0, vec, bias0)
        ya, n2a, ha, ga, *x1s = mlp_fwd(per, pc, pm0, ids, x0, oa, w0, vec, hide)
        x1s = exchange(x1s)
        x1, n1b, qkvb, pb, ob = attn_fwd(1, per, pq1, ids, x1s, w1, vec, bias1)
        res = mlp_both(per, pc, pm1, gmp, ids, x1, ob, w1, vec, hide, cots)
        outs, (dob, dyb, dab, gvm1, df1, dms1), gm1 = res[:4], res[4:10], res[10:12]
        output = join_blocks(ids, exchange(outs))
        dqkvb, gva1, gt1 = attn_bwd(1, dob, qkvb, pb)
        *dx1s, gvx1 = dx_step(1, per, pq1, ids, dqkvb, dyb, x1, w1, vec)
        dx1s = exchange(dx1s)
        gq1 = qkv_grad(per, gqp, ids, n1b, dqkvb, ob, dab)
        dma, dua, df0, dms0, *gm0 = mlp_bwd(per, pc, pm0, gmp0, ids, w0, n2a, ha, ga, dx1s)
        doa, dya, daa, gvm0 = mid_bwd(0, per, pc, pm0, ids, w0, vec, ya, dma, dua)
        dqkva, gva0, gt0 = attn_bwd(0, doa, qkva, pa)
        gq0 = qkv_grad(per, gqp, ids, n1a, dqkva, oa, daa)
        dx0, gvx0 = dx_step(0, per, pq0, ids, dqkva, dya, x0, w0, vec)
        smalls = all_smalls(
            ((gvm0, dms0, df0, gva0, gvx0, gt0), (gvm1, dms1, df1, gva1, gvx1, gt1))
        )
        smalls = lax.psum(smalls, ("y", "core") + shard)
        fq1, fm1, fq0, fm0 = [half_reduce(g, shard) for g in (gq1, gm1, gq0, gm0)]
        new_m = adam_m(0, fm0, adam_m(1, fm1))
        new_q = adam_q(0, fq0, adam_q(1, fq1))

    smalls = smalls.astype(f32).reshape(2, 20, WIDE)
    g_vec = lax.dynamic_slice_in_dim(smalls[:, :12], me * per, per, axis=2)
    g_tab = smalls[:, 12:20].reshape(2 * HEADS, 256)
    g_tab = lax.dynamic_slice_in_dim(g_tab, me * own, own, axis=0)[:, :SPAN]
    flat = [*new_q, *new_m]
    for pos, g in ((4, g_vec), (5, g_tab)):
        flat += adam_math(
            masters[pos], firsts[pos], seconds[pos], g, step_rates[pos], decay_rates[pos]
        )
    return (output.reshape(inputs.shape), dx0.reshape(inputs.shape), *flat, g_vec[:, 7])


def solution(mesh):
    count = mesh.shape["shard"]
    if count == 8:
        mesh = Mesh(mesh.devices.reshape(2, 2, 4, 2), ("y", "core", "z", "x"))
        shard = ("z", "x")
    else:
        mesh = Mesh(mesh.devices.reshape(2, 2, count), ("y", "core", "s"))
        shard = ("s",)
    tokens = P(shard, ("y", "core"), None, None, None)
    params = (P(None, shard, None),) * 4 + (P(None, None, shard), P(shard, None))
    in_specs = (tokens, tokens, P(shard)) + params * 3
    out_specs = (tokens, tokens)
    for spec in params:
        out_specs = out_specs + (spec,) * 3
    out_specs = out_specs + (P(None, shard),)
    return jax.shard_map(
        functools.partial(body, shard),
        mesh=mesh,
        in_specs=in_specs,
        out_specs=out_specs,
        check_vma=False,
    )
```
